32 devices in a mesh: seq: 4 (over z), fsdp: 8 (over y, x, core).
Axes of the slice: x: 2, y: 2, z: 4, core: 2. Of those that a mesh axis runs over, the one named last changes fastest.
Arguments:
- tokens: bfloat16 [8, 1024, 1536], P('fsdp', 'seq'), may hold values from -6 to 6
- gain_attn: bfloat16 [1536], P(('seq', 'fsdp')), may hold values from 0.5 to 1.5
- w_query: bfloat16 [1536, 1536], P(('seq', 'fsdp')), may hold values from -0.15625 to 0.15625
- key_weight: bfloat16 [1536, 768], P(('seq', 'fsdp')), may hold values from -0.15625 to 0.15625
- value_weight: bfloat16 [1536, 768], P(('seq', 'fsdp')), may hold values from -0.15625 to 0.15625
- w_out: bfloat16 [1536, 1536], P(('seq', 'fsdp')), may hold values from -0.625 to 0.625
- gain_mlp: bfloat16 [1536], P(('seq', 'fsdp')), may hold values from 0.5 to 1.5
- w_gate: bfloat16 [1536, 4096], P(('seq', 'fsdp')), may hold values from -0.15625 to 0.15625
- w_up: bfloat16 [1536, 4096], P(('seq', 'fsdp')), may hold values from -0.15625 to 0.15625
- w_down: bfloat16 [4096, 1536], P(('seq', 'fsdp')), may hold values from -0.09375 to 0.09375
- out_grad: bfloat16 [8, 1024, 1536], P('fsdp', 'seq'), may hold values from -6 to 6
- lengths: int32 [8, 4], P('fsdp'), may hold values from 1 to 640, 1024 in all within a row
- stretch_map: int32 [8, 8], P('fsdp'), may hold values from 0 to 7, as said below
Outputs:
- result: bfloat16 [8, 1024, 1536], P('fsdp', 'seq')
- input_grad: bfloat16 [8, 1024, 1536], P('fsdp', 'seq')
- grad_gain_attn: float32 [1536], P(('seq', 'fsdp'))
- grad_query: float32 [1536, 1536], P(('seq', 'fsdp'))
- grad_key: float32 [1536, 768], P(('seq', 'fsdp'))
- grad_value: float32 [1536, 768], P(('seq', 'fsdp'))
- grad_out: float32 [1536, 1536], P(('seq', 'fsdp'))
- grad_gain_mlp: float32 [1536], P(('seq', 'fsdp'))
- grad_gate: float32 [1536, 4096], P(('seq', 'fsdp'))
- grad_up: float32 [1536, 4096], P(('seq', 'fsdp'))
- grad_down: float32 [4096, 1536], P(('seq', 'fsdp'))
The draws below stay inside these ranges and needn't reach their ends.
Inputs may be any that keep to these rules, and one draw needn't show every extreme that they name: stretch_map of a group holds every slot once; slot s is stored rows s * 128 to (s + 1) * 128 - 1 of the group; logical stretches whose difference is not a multiple of 4 lie in different blocks of 256 stored rows. Each group's lengths sum to 1024; the longest has exactly 640 tokens.
All inputs are finite; a program needn't handle non-finite values.
Results may differ from the reference program's by a relative error of at most 0.015.
Values may be sent and summed in bfloat16 or wider, within the bound.
No kernel may reach another device: no remote copies, remote signals or barrier semaphores. Data moves between devices by JAX's collectives and lax.ppermute only.
A program may use at most 320 MiB of HBM per device.

```python
import math
import jax
import jax.numpy as jnp
import numpy as np
from jax import lax

MODEL_WIDTH = 1536
QUERY_HEADS = 16
KEY_VALUE_HEADS = 8
HEAD_SIZE = 96
FF = 4096
STRETCH = 128
DOCS = 4
TOK_DEV = 256
BATCH = 8
GROUP_TOK = 1024
STRETCHES = 8
LONGEST = 640


def draw_stretch_map(key, part):
    key = jax.random.fold_in(key, 11)
    devices = STRETCHES * STRETCH // TOK_DEV
    per_device = TOK_DEV // STRETCH
    key_rows = jax.random.split(key, BATCH)
    orders = jax.vmap(lambda single: jax.random.permutation(single, devices))(key_rows).astype(jnp.int32)
    logical = jnp.arange(STRETCHES, dtype=jnp.int32)
    holder = orders[:, logical % devices]
    return (holder * per_device + (logical // devices)[None, :]).astype(jnp.int32)


def levels(stream_key, dims, cuts, low, largest):
    factor_of = 1.0
    for position, parts in cuts:
        heights = jax.random.uniform(jax.random.fold_in(jax.random.fold_in(stream_key, 6), position), (parts,), jnp.float32, low / len(cuts), largest / len(cuts))
        factor_of = factor_of * jnp.repeat(jnp.exp(heights), dims[position] // parts).reshape((-1,) + (1,) * (len(dims) - 1 - position))
    return factor_of


def length_profile(amount, total, bound, lean):
    loads = [(1 << 20) // math.isqrt(rank ** lean) + 1 for rank in range(2, amount + 1)]
    rest, counts = total - bound - (amount - 1), [1] * (amount - 1)
    while rest > 0:
        free = [i for i in range(amount - 1) if counts[i] < bound]
        pool, remaining = sum([loads[i] for i in free]), rest
        for i in free:
            extra = min(bound - counts[i], max(1, remaining * loads[i] // pool), rest)
            counts[i] = counts[i] + extra
            rest = rest - extra
    return np.array([bound] + counts)


def uneven(stream_key, count, total, bound, skew):
    if count == 2:
        one = jax.random.randint(stream_key, (), max(1, total - bound), min(bound, total - 1) + 1)
        return jnp.stack([one, total - one])
    sizes = jnp.asarray(length_profile(count, total, bound, skew), jnp.int32)
    twos = (count - 1) // 2
    donor, receiver = sizes[1:1 + 2 * twos:2], sizes[2:2 + 2 * twos:2]
    room = jnp.minimum(donor - 1, bound - receiver)
    shifted = jax.random.randint(jax.random.fold_in(stream_key, 1), (twos,), 0, 1 << 20) % (room + 1)
    sizes = sizes.at[1:1 + 2 * twos:2].set(donor - shifted).at[2:2 + 2 * twos:2].set(receiver + shifted)
    return sizes[jax.random.permutation(jax.random.fold_in(stream_key, 2), count)]


def gaussian(stream_key, dims, spread, reach, pieces=(), held_as=jnp.bfloat16):
    array = jax.random.normal(stream_key, dims, jnp.float32) * spread
    if len(pieces) > 0:
        array = levels(stream_key, dims, pieces, -0.22, 0.18) * array
    return jnp.clip(array, min=-reach, max=reach).astype(held_as)


def setup_inputs(seed: int = 0) -> dict:
    seeds = jax.random.split(jax.random.key(seed), 14)
    tokens = gaussian(seeds[0], (BATCH, GROUP_TOK, MODEL_WIDTH), 1.0, 6.0, ((0, 8), (1, 4)))
    gain_attn = jnp.clip(1.0 + 0.1 * jax.random.normal(seeds[1], (MODEL_WIDTH,), jnp.float32), 0.5, 1.5).astype(jnp.bfloat16)
    w_query = gaussian(seeds[2], (MODEL_WIDTH, QUERY_HEADS * HEAD_SIZE), MODEL_WIDTH ** -0.5, 0.15625, ((0, 32),))
    key_weight = gaussian(seeds[3], (MODEL_WIDTH, KEY_VALUE_HEADS * HEAD_SIZE), MODEL_WIDTH ** -0.5, 0.15625, ((0, 32),))
    value_weight = gaussian(seeds[4], (MODEL_WIDTH, KEY_VALUE_HEADS * HEAD_SIZE), MODEL_WIDTH ** -0.5, 0.15625, ((0, 32),))
    w_out = gaussian(seeds[5], (QUERY_HEADS * HEAD_SIZE, MODEL_WIDTH), (QUERY_HEADS * HEAD_SIZE // 16) ** -0.5, 0.625, ((0, 32),))
    gain_mlp = jnp.clip(1.0 + 0.1 * jax.random.normal(seeds[6], (MODEL_WIDTH,), jnp.float32), 0.5, 1.5).astype(jnp.bfloat16)
    w_gate = gaussian(seeds[7], (MODEL_WIDTH, FF), MODEL_WIDTH ** -0.5, 0.15625, ((0, 32),))
    w_up = gaussian(seeds[8], (MODEL_WIDTH, FF), MODEL_WIDTH ** -0.5, 0.15625, ((0, 32),))
    w_down = gaussian(seeds[9], (FF, MODEL_WIDTH), FF ** -0.5, 0.09375, ((0, 32),))
    out_grad = gaussian(seeds[10], (BATCH, GROUP_TOK, MODEL_WIDTH), 1.0, 6.0, ((0, 8), (1, 4)))
    lengths = jax.vmap(lambda own: uneven(own, DOCS, GROUP_TOK, LONGEST, 2))(jax.random.split(seeds[11], BATCH)).reshape((BATCH, DOCS)).astype(jnp.int32)
    stretch_map = draw_stretch_map(jax.random.fold_in(seeds[13], 71), 0)
    return {"tokens": tokens, "gain_attn": gain_attn, "w_query": w_query, "key_weight": key_weight, "value_weight": value_weight, "w_out": w_out, "gain_mlp": gain_mlp, "w_gate": w_gate, "w_up": w_up, "w_down": w_down, "out_grad": out_grad, "lengths": lengths, "stretch_map": stretch_map}


EPSILON = 1e-05
THETA = 100000.0
FULL_PRECISION = lax.Precision.HIGHEST

@jax.custom_vjp
def low(v):
    return lax.optimization_barrier(v.astype(jnp.bfloat16)).astype(jnp.float32)

@jax.custom_vjp
def low_back(v):
    return v

def low_keep(v):
    return (low(v), None)

def low_pass(kept, grad):
    return (grad,)

def back_keep(v):
    return (v, None)

def back_low(kept, grad):
    return (low(grad),)
low.defvjp(low_keep, low_pass)
low_back.defvjp(back_keep, back_low)

def layout(doc_lengths, slot_map):
    token_count = slot_map.shape[0]
    slots = jnp.arange(token_count, dtype=jnp.int32)
    logical = lax.optimization_barrier(jnp.sum(jnp.where(slot_map[None, :] == slots[:, None], slots[None, :], 0), axis=1)).astype(jnp.int32)
    position_list = (logical[:, None] * STRETCH + jnp.arange(STRETCH, dtype=jnp.int32)[None, :]).reshape(-1)
    endings = jnp.cumsum(doc_lengths).astype(jnp.int32)
    passed = endings[None, :] <= position_list[:, None]
    document_index = lax.optimization_barrier(jnp.sum(passed.astype(jnp.int32), axis=1)).astype(jnp.int32)
    starts = lax.optimization_barrier(jnp.sum(jnp.where(passed, doc_lengths[None, :], 0), axis=1)).astype(jnp.int32)
    return (document_index, position_list - starts)

def apply_rotary(value_rows, position_list, direction):
    half = value_rows.shape[-1] // 2
    freqs = THETA ** (-2.0 * jnp.arange(half, dtype=jnp.float32) / value_rows.shape[-1])
    angles = position_list.astype(jnp.float32)[:, None] * freqs[None, :]
    cosine = jnp.cos(angles)[:, None, :]
    sine = direction * jnp.sin(angles)[:, None, :]
    first = value_rows[..., :half]
    second = value_rows[..., half:]
    return jnp.concatenate([first * cosine - second * sine, second * cosine + first * sine], axis=-1)

def rms_norm(value_rows, gain):
    return value_rows * lax.rsqrt(lax.optimization_barrier(jnp.mean(value_rows * value_rows, axis=-1, keepdims=True)) + EPSILON) * gain

def grouped_query_attention(item):
    query_rows, key_rows, value_rows, document_index, position_list = item
    token_total = query_rows.shape[0]
    layer_width = min(512, token_total)
    group_ratio = QUERY_HEADS // KEY_VALUE_HEADS
    scale = 1.0 / math.sqrt(HEAD_SIZE)
    block_list = (query_rows.reshape(token_total // layer_width, layer_width, KEY_VALUE_HEADS, group_ratio, HEAD_SIZE), document_index.reshape(-1, layer_width), position_list.reshape(-1, layer_width))

    def attend(block):
        block_queries, block_docs, block_places = block
        scores = low_back(jnp.einsum('qhrd,khd->hrqk', block_queries, key_rows, precision=FULL_PRECISION) * scale)
        allowed = (block_docs[:, None] == document_index[None, :]) & (position_list[None, :] <= block_places[:, None])
        scores = jnp.where(allowed[None, None], scores, -1e+30)
        peak = lax.optimization_barrier(jnp.max(scores, axis=-1, keepdims=True))
        weights = jnp.exp(scores - peak)
        probs = weights / lax.optimization_barrier(jnp.sum(weights, axis=-1, keepdims=True))
        mixed = jnp.einsum('hrqk,khd->qhrd', low(probs), value_rows, precision=FULL_PRECISION)
        return mixed.reshape(layer_width, QUERY_HEADS * HEAD_SIZE)
    return lax.map(jax.checkpoint(attend), block_list).reshape(token_total, QUERY_HEADS * HEAD_SIZE)

def forward(inputs, gain_one, query_w, key_matrix, value_matrix, out_w, gain_two, gate_w, up_w, down_w, document_index, position_list):
    group_count, token_total = (inputs.shape[0], inputs.shape[1])
    flat = inputs.reshape(-1, MODEL_WIDTH)
    flattened_positions = position_list.reshape(-1)
    normalized_input = low(rms_norm(flat, gain_one))
    query_rows = low(apply_rotary(low_back(jnp.dot(normalized_input, query_w, precision=FULL_PRECISION)).reshape(-1, QUERY_HEADS, HEAD_SIZE), flattened_positions, 1.0))
    key_rows = low(apply_rotary(low_back(jnp.dot(normalized_input, key_matrix, precision=FULL_PRECISION)).reshape(-1, KEY_VALUE_HEADS, HEAD_SIZE), flattened_positions, 1.0))
    value_rows = low(low_back(jnp.dot(normalized_input, value_matrix, precision=FULL_PRECISION))).reshape(-1, KEY_VALUE_HEADS, HEAD_SIZE)
    attention_output = lax.map(grouped_query_attention, (query_rows.reshape(group_count, token_total, QUERY_HEADS, HEAD_SIZE), key_rows.reshape(group_count, token_total, KEY_VALUE_HEADS, HEAD_SIZE), value_rows.reshape(group_count, token_total, KEY_VALUE_HEADS, HEAD_SIZE), document_index, position_list))
    attention_output = low(low_back(attention_output.reshape(-1, QUERY_HEADS * HEAD_SIZE)))
    resid = flat + low_back(jnp.dot(attention_output, out_w, precision=FULL_PRECISION))
    second = low(rms_norm(resid, gain_two))
    gate = low_back(jnp.dot(second, gate_w, precision=FULL_PRECISION))
    upper = low_back(jnp.dot(second, up_w, precision=FULL_PRECISION))
    hidden = low(jax.nn.silu(gate) * upper)
    output = resid + low_back(jnp.dot(hidden, down_w, precision=FULL_PRECISION))
    return output.reshape(group_count, token_total, MODEL_WIDTH)

def reference(tokens, gain_attn, w_query, key_weight, value_weight, w_out, gain_mlp, w_gate, w_up, w_down, out_grad, lengths, stretch_map):
    document_index, position_list = jax.vmap(layout)(lengths, stretch_map)
    params = tuple((item.astype(jnp.float32) for item in (tokens, gain_attn, w_query, key_weight, value_weight, w_out, gain_mlp, w_gate, w_up, w_down)))
    output, pullback = jax.vjp(lambda *given: forward(*given, document_index, position_list), *params)
    grads = pullback(out_grad.astype(jnp.float32))
    return (output.astype(jnp.bfloat16), grads[0].astype(jnp.bfloat16), grads[1], grads[2], grads[3], grads[4], grads[5], grads[6], grads[7], grads[8], grads[9])
```

```python
import math

import jax
import jax.numpy as jnp
from jax import lax
from jax.sharding import Mesh
from jax.sharding import PartitionSpec as P

QUERY_HEADS = 16
KEY_VALUE_HEADS = 8
HEAD_SIZE = 96
FF = 4096
STRETCH = 128

EPSILON = 1e-05
THETA = 100000.0

BF = jnp.bfloat16
F32 = jnp.float32


def layout(doc_lengths, slot_map, slots):
    count = slot_map.shape[0]
    stretches = jnp.arange(count, dtype=jnp.int32)
    logical = jnp.sum(
        jnp.where(slot_map[None, :] == slots[:, None], stretches[None, :], 0), axis=1
    )
    places = (
        logical[:, None] * STRETCH + jnp.arange(STRETCH, dtype=jnp.int32)[None, :]
    ).reshape(-1)
    endings = jnp.cumsum(doc_lengths)
    passed = endings[None, :] <= places[:, None]
    document = jnp.sum(passed.astype(jnp.int32), axis=1)
    starts = jnp.sum(jnp.where(passed, doc_lengths[None, :], 0), axis=1)
    return document, places - starts


def rotary_tables(positions):
    half = HEAD_SIZE // 2
    freqs = THETA ** (-2.0 * jnp.arange(half, dtype=F32) / HEAD_SIZE)
    angles = positions.astype(F32)[:, None] * freqs[None, :]
    return jnp.cos(angles)[:, None, :], jnp.sin(angles)[:, None, :]


def apply_rotary(rows, cosine, sine):
    half = rows.shape[-1] // 2
    first, second = rows[..., :half], rows[..., half:]
    return jnp.concatenate(
        [first * cosine - second * sine, second * cosine + first * sine], axis=-1
    )


def product(left, right):
    return jnp.dot(left, right, preferred_element_type=F32)


def over_rows(left, right):
    return lax.dot_general(left, right, (((0,), (0,)), ((), ())), preferred_element_type=F32)


def times_transposed(left, right):
    return lax.dot_general(left, right, (((1,), (1,)), ((), ())), preferred_element_type=F32)


def on_device(n, m, *operands):
    (
        tokens,
        gain_attn,
        w_query,
        key_weight,
        value_weight,
        w_out,
        gain_mlp,
        w_gate,
        w_up,
        w_down,
        out_grad,
        lengths,
        stretch_map,
    ) = operands
    at_z, at_y = lax.axis_index("z"), lax.axis_index("y")
    at_x, at_c = lax.axis_index("x"), lax.axis_index("c")
    rank = at_x * 2 + at_c
    tp = 4

    def shift(a, axis, size, by):
        return lax.ppermute(a, axis, [(i, (i + by) % size) for i in range(size)])

    def across(a, delta):
        if delta == 1:
            return lax.ppermute(a, "c", [(0, 1), (1, 0)])
        if delta == 2:
            return lax.ppermute(a, "x", [(0, 1), (1, 0)])
        return lax.ppermute(a, ("x", "c"), [(i, i ^ delta) for i in range(tp)])

    def ring(a, axis, size):
        blocks = [a]
        for _ in range(size - 1):
            blocks.append(shift(blocks[-1], axis, size, 1))
        return blocks

    def ring_sum(block, axis, size):
        total = block(1)
        for step in range(1, size):
            arrived = shift(total, axis, size, 1)
            mine = block((step + 1) % size)
            total = arrived.astype(F32) + mine.astype(F32)
            if step < size - 1:
                total = total.astype(BF)
        return total

    def pick(a, index, axis):
        return lax.dynamic_index_in_dim(a, index, axis, keepdims=False)

    def put(a, piece, *index):
        index = index + (0,) * (a.ndim - len(index))
        return lax.dynamic_update_slice(a, piece, index)

    def stack_z(blocks):
        out = jnp.zeros((n,) + blocks[0].shape, blocks[0].dtype)
        for k, block in enumerate(blocks):
            out = put(out, block[None], (at_z - k) % n)
        return out

    def gather_all(shard):
        pieces = [(0, 0, 0, stack_z(ring(shard, "z", n)))]
        pieces = [(k, 0, 0, p) for k, p in enumerate(ring(pieces[0][3], "y", m))]
        pieces += [(k, 1, 0, across(p, 2)) for k, _, _, p in pieces]
        pieces += [(k, j, 1, across(p, 1)) for k, j, _, p in pieces]
        rows, cols = shard.shape
        out = jnp.zeros((n, m, 2, 2, rows, cols), shard.dtype)
        for k, j, i, p in pieces:
            out = put(out, p[:, None, None, None], 0, (at_y - k) % m, at_x ^ j, at_c ^ i)
        return out.reshape(n * m * tp * rows, cols)

    def gather_zy(shard):
        out = jnp.zeros((n, m) + shard.shape, shard.dtype)
        for k, block in enumerate(ring(shard, "z", n)):
            for j, piece in enumerate(ring(block, "y", m)):
                out = put(out, piece[None, None], (at_z - k) % n, (at_y - j) % m)
        return out.reshape((n * m * shard.shape[0],) + shard.shape[1:])

    def sum_zy(terms):
        terms = ring_sum(lambda k: pick(terms, (at_y - k) % m, 1), "y", m).astype(BF)
        return ring_sum(lambda k: pick(terms, (at_z - k) % n, 0), "z", n)

    def sum_all(terms):
        cols = terms.shape[1]
        terms = terms.reshape(n, m, 2, 2, -1, cols)
        terms = ring_sum(lambda k: pick(terms, at_c ^ k, 3), "c", 2).astype(BF)
        terms = ring_sum(lambda k: pick(terms, at_x ^ k, 2), "x", 2).astype(BF)
        return sum_zy(terms)

    def spread(rows):
        by_c, by_x = across(rows, 1), across(rows, 2)
        return jnp.concatenate([rows, by_c, by_x, across(by_x, 1)], axis=0)

    def collect(terms):
        near, far = jnp.split(terms.reshape(tp, -1, terms.shape[-1]), 2)
        by_c = across(jnp.stack([near[1], far[1]]).astype(BF), 1).astype(F32)
        by_x = across((far[0] + by_c[1]).astype(BF), 2).astype(F32)
        return near[0] + by_c[0] + by_x

    token_count, width = tokens.shape[1:]
    group_ratio = QUERY_HEADS // KEY_VALUE_HEADS
    scale = 1.0 / math.sqrt(HEAD_SIZE)
    shard_rows = w_query.shape[0]
    unit = w_down.shape[0]
    pair_cols = KEY_VALUE_HEADS * HEAD_SIZE
    gain_one = gain_attn.astype(F32)[:, None]
    gain_two = gain_mlp.astype(F32)[:, None]

    own = tokens[0]
    group_rows = jnp.concatenate(ring(own, "z", n), axis=0)
    span = group_rows.shape[0]

    def scaled(weight, gain):
        return (weight.astype(F32) * gain).astype(BF)

    kv_weight = gather_all(
        scaled(jnp.concatenate([key_weight, value_weight], axis=1), gain_one)
    )
    query_out = gather_all(jnp.concatenate([scaled(w_query, gain_one), w_out], axis=1))
    q_weight, out_weight = query_out[:, :width], query_out[:, width:]

    gate_up = jnp.stack([w_gate, w_up], axis=1).reshape(shard_rows, 2, n * m, tp, unit)
    gate_up = (gate_up.astype(F32) * gain_two[:, :, None, None, None]).astype(BF)
    ff_cols = 2 * n * m * unit
    mine = jnp.zeros((2, 2, shard_rows, ff_cols), BF)
    for delta in range(tp):
        part = pick(gate_up, rank ^ delta, 3).reshape(shard_rows, ff_cols)
        if delta:
            part = across(part, delta)
        mine = put(mine, part[None, None], at_x ^ (delta >> 1), at_c ^ (delta & 1))
    gu_weight = gather_zy(mine.reshape(tp * shard_rows, ff_cols))
    down_weight = gather_zy(w_down)
    grad_rows = spread(out_grad[0])

    slots_each = stretch_map.shape[1] // n
    slots = (
        ((at_z - jnp.arange(n, dtype=jnp.int32)) % n)[:, None] * slots_each
        + jnp.arange(slots_each, dtype=jnp.int32)[None, :]
    ).reshape(-1)
    doc_all, place_all = layout(lengths[0], stretch_map[0], slots)
    allowed = (doc_all[:token_count, None] == doc_all[None, :]) & (
        place_all[None, :] <= place_all[:token_count, None]
    )
    cosine, sine = rotary_tables(place_all)
    own_cosine, own_sine = cosine[:token_count], sine[:token_count]

    inputs = group_rows.astype(F32)
    inverse_all = lax.rsqrt(jnp.mean(inputs * inputs, axis=-1, keepdims=True) + EPSILON)
    normed_group = (inputs * inverse_all).astype(BF)
    inputs = own.astype(F32)
    first_inverse = inverse_all[:token_count]
    first_normed = inputs * first_inverse
    normed_one = normed_group[:token_count]

    keys_values = product(normed_group, kv_weight)
    keys = apply_rotary(
        keys_values[:, :pair_cols].reshape(span, KEY_VALUE_HEADS, HEAD_SIZE), cosine, sine
    ).astype(BF)
    values = keys_values[:, pair_cols:].reshape(span, KEY_VALUE_HEADS, HEAD_SIZE).astype(BF)
    queries = apply_rotary(
        product(normed_one, q_weight).reshape(token_count, QUERY_HEADS, HEAD_SIZE),
        own_cosine,
        own_sine,
    ).astype(BF)

    def by_head(rows):
        return rows.reshape(token_count, KEY_VALUE_HEADS, group_ratio, HEAD_SIZE).transpose(
            1, 2, 0, 3
        )

    query_heads = by_head(queries)
    key_heads = keys.transpose(1, 0, 2)
    value_heads = values.transpose(1, 0, 2)

    def head_scores(head_queries, head_keys):
        scores = (
            jnp.einsum("rqd,kd->rqk", head_queries, head_keys, preferred_element_type=F32) * scale
        )
        return jnp.where(allowed[None], scores, -1e30)

    def head_forward(item):
        head_queries, head_keys, head_values = item
        scores = head_scores(head_queries, head_keys)
        peak = jnp.max(scores, axis=-1, keepdims=True)
        weights = jnp.exp(scores - peak)
        totals = jnp.sum(weights, axis=-1, keepdims=True)
        probs = weights / totals
        mixed = jnp.einsum(
            "rqk,kd->rqd", probs.astype(BF), head_values, preferred_element_type=F32
        )
        return mixed.astype(BF), peak[..., 0] + jnp.log(totals[..., 0])

    mixed_heads, log_totals = lax.map(head_forward, (query_heads, key_heads, value_heads))
    attention_output = mixed_heads.transpose(2, 0, 1, 3).reshape(token_count, width)
    resid = inputs + product(attention_output, out_weight)

    second_inverse = lax.rsqrt(jnp.mean(resid * resid, axis=-1, keepdims=True) + EPSILON)
    second_normed = resid * second_inverse
    normed_two = spread(second_normed.astype(BF))
    gate_up_rows = product(normed_two, gu_weight)
    gate, upper = jnp.split(gate_up_rows, 2, axis=1)
    sigmoid_gate = jax.nn.sigmoid(gate)
    silu_gate = gate * sigmoid_gate
    hidden = (silu_gate * upper).astype(BF)
    down_terms = over_rows(hidden, grad_rows).astype(BF).reshape(n, m, unit, width)
    result = (resid + collect(product(hidden, down_weight))).astype(BF)

    grad_hidden = times_transposed(grad_rows, down_weight)
    grad_gate_in = (
        grad_hidden * upper * sigmoid_gate * (1.0 + gate * (1.0 - sigmoid_gate))
    ).astype(BF)
    grad_up_in = (grad_hidden * silu_gate).astype(BF)
    grad_gate_up = jnp.concatenate([grad_gate_in, grad_up_in], axis=1)
    scaled_two = collect(times_transposed(grad_gate_up, gu_weight))
    gate_up_terms = (
        over_rows(normed_two, grad_gate_up).astype(BF).reshape(n, m, tp * shard_rows, ff_cols)
    )

    def norm_back(scaled_grad, normed, inverse):
        return inverse * (
            scaled_grad - normed * jnp.mean(scaled_grad * normed, axis=-1, keepdims=True)
        )

    grad_resid = out_grad[0].astype(F32) + norm_back(scaled_two, second_normed, second_inverse)
    grad_attn_out = grad_resid.astype(BF)

    out_terms = over_rows(attention_output, grad_attn_out).astype(BF)
    head_gradient = by_head(times_transposed(grad_attn_out, out_weight).astype(BF))

    def head_backward(item):
        head_queries, head_keys, head_values, head_grads, head_totals = item
        probs = jnp.exp(head_scores(head_queries, head_keys) - head_totals[..., None])
        grad_probs = jnp.einsum(
            "rqd,kd->rqk", head_grads, head_values, preferred_element_type=F32
        )
        centre = jnp.sum(probs * grad_probs, axis=-1, keepdims=True)
        grad_scores = (probs * (grad_probs - centre)).astype(BF)
        grad_queries = (
            jnp.einsum("rqk,kd->rqd", grad_scores, head_keys, preferred_element_type=F32) * scale
        )
        grad_keys = (
            jnp.einsum("rqk,rqd->kd", grad_scores, head_queries, preferred_element_type=F32)
            * scale
        )
        grad_values = jnp.einsum(
            "rqk,rqd->kd", probs.astype(BF), head_grads, preferred_element_type=F32
        )
        return grad_queries, grad_keys, grad_values

    grad_query_heads, grad_key_heads, grad_value_heads = lax.map(
        head_backward, (query_heads, key_heads, value_heads, head_gradient, log_totals)
    )
    grad_key_rows = apply_rotary(grad_key_heads.transpose(1, 0, 2), cosine, -sine)
    grad_kv = jnp.concatenate(
        [
            grad_key_rows.reshape(span, pair_cols).astype(BF),
            grad_value_heads.transpose(1, 0, 2).reshape(span, pair_cols).astype(BF),
        ],
        axis=1,
    )
    grad_query_rows = (
        apply_rotary(
            grad_query_heads.transpose(2, 0, 1, 3).reshape(token_count, QUERY_HEADS, HEAD_SIZE),
            own_cosine,
            -own_sine,
        )
        .reshape(token_count, width)
        .astype(BF)
    )
    kv_terms = over_rows(normed_group, grad_kv).astype(BF)
    query_terms = over_rows(normed_one, grad_query_rows).astype(BF)
    by_block = grad_kv.reshape(n, token_count, 2 * pair_cols)
    own_kv = ring_sum(lambda k: by_block[k], "z", n).astype(BF)
    scaled_one = times_transposed(grad_query_rows, q_weight) + times_transposed(own_kv, kv_weight)
    input_grad = (grad_resid + norm_back(scaled_one, first_normed, first_inverse)).astype(BF)

    down_owned = sum_zy(down_terms)
    parts = sum_zy(gate_up_terms).astype(BF).reshape(tp, shard_rows, ff_cols)
    arrived = []
    for delta in range(tp):
        part = pick(parts, rank ^ delta, 0)
        arrived.append(across(part, delta) if delta else part)
    arrived = jnp.stack(arrived)
    gate_up_owned = jnp.stack([pick(arrived, rank ^ r, 0) for r in range(tp)], axis=1)
    gate_up_owned = (
        gate_up_owned.astype(F32)
        .reshape(shard_rows, tp, 2, n * m, unit)
        .transpose(2, 0, 3, 1, 4)
        .reshape(2, shard_rows, n * m * tp * unit)
    )
    out_owned = sum_all(out_terms)
    query_owned = sum_all(query_terms)
    kv_owned = sum_all(kv_terms)
    key_owned, value_owned = kv_owned[:, :pair_cols], kv_owned[:, pair_cols:]
    gate_owned, up_owned = gate_up_owned[0], gate_up_owned[1]

    def along(weight, grad):
        return jnp.sum(weight.astype(F32) * grad, axis=1)

    gain_one_owned = (
        along(w_query, query_owned)
        + along(key_weight, key_owned)
        + along(value_weight, value_owned)
    )
    gain_two_owned = along(w_gate, gate_owned) + along(w_up, up_owned)
    return (
        result[None],
        input_grad[None],
        gain_one_owned,
        query_owned * gain_one,
        key_owned * gain_one,
        value_owned * gain_one,
        out_owned,
        gain_two_owned,
        gate_owned * gain_two,
        up_owned * gain_two,
        down_owned,
    )


def solution(mesh):
    n, groups = mesh.shape["seq"], mesh.shape["fsdp"]
    m = groups // 4
    fine = Mesh(mesh.devices.reshape(n, m, 2, 2), ("z", "y", "x", "c"))
    fsdp = ("y", "x", "c")
    every = ("z", "y", "x", "c")
    rows, vector, matrix = P(fsdp, "z", None), P(every), P(every, None)
    in_specs = (
        rows,
        vector,
        matrix,
        matrix,
        matrix,
        matrix,
        vector,
        matrix,
        matrix,
        matrix,
        rows,
        P(fsdp, None),
        P(fsdp, None),
    )
    out_specs = (rows, rows, vector) + (matrix,) * 4 + (vector,) + (matrix,) * 3

    def step(*operands):
        return on_device(n, m, *operands)

    return jax.shard_map(
        step, mesh=fine, in_specs=in_specs, out_specs=out_specs, check_vma=False
    )
```

```python
import math

import jax
import jax.numpy as jnp
from jax import lax
from jax.experimental import pallas as pl
from jax.experimental.pallas import tpu as pltpu
from jax.sharding import Mesh
from jax.sharding import PartitionSpec as P

QUERY_HEADS = 16
KEY_VALUE_HEADS = 8
HEAD_SIZE = 96
FF = 4096
STRETCH = 128

EPSILON = 1e-05
THETA = 100000.0

BF = jnp.bfloat16
F32 = jnp.float32


def layout(doc_lengths, slot_map, slots):
    count = slot_map.shape[0]
    stretches = jnp.arange(count, dtype=jnp.int32)
    logical = jnp.sum(
        jnp.where(slot_map[None, :] == slots[:, None], stretches[None, :], 0), axis=1
    )
    places = (
        logical[:, None] * STRETCH + jnp.arange(STRETCH, dtype=jnp.int32)[None, :]
    ).reshape(-1)
    endings = jnp.cumsum(doc_lengths)
    passed = endings[None, :] <= places[:, None]
    document = jnp.sum(passed.astype(jnp.int32), axis=1)
    starts = jnp.sum(jnp.where(passed, doc_lengths[None, :], 0), axis=1)
    return document, places - starts


def rotary_tables(positions):
    half = HEAD_SIZE // 2
    freqs = THETA ** (-2.0 * jnp.arange(half, dtype=F32) / HEAD_SIZE)
    angles = positions.astype(F32)[:, None] * freqs[None, :]
    return jnp.cos(angles).T, jnp.sin(angles).T


def rotate(rows, cosine, sine):
    half = rows.shape[0] // 2
    first, second = rows[:half], rows[half:]
    return jnp.concatenate(
        [first * cosine - second * sine, second * cosine + first * sine], axis=0
    )


def contract(left, right, at_left, at_right):
    return lax.dot_general(
        left, right, (((at_left,), (at_right,)), ((), ())), preferred_element_type=F32
    )


RATIO = QUERY_HEADS // KEY_VALUE_HEADS
SCALE = 1.0 / math.sqrt(HEAD_SIZE)
VMEM_BYTES = 40 * 1024 * 1024
MOST_VMEM_BYTES = 60 * 1024 * 1024


def lasting(microseconds):
    return pl.CostEstimate(
        flops=int(microseconds * 1e9), bytes_accessed=int(microseconds * 3e6), transcendentals=0
    )


def forward_kernel(q_ref, k_ref, v_ref, bias_ref, out_ref, lse_ref):
    keys, values = k_ref[...], v_ref[...]
    for head in range(RATIO):
        rows = slice(head * HEAD_SIZE, (head + 1) * HEAD_SIZE)
        scores = contract(keys, q_ref[rows, :], 0, 0) * SCALE + bias_ref[...]
        peak = jnp.max(scores, axis=0, keepdims=True)
        weights = jnp.exp(scores - peak)
        totals = jnp.sum(weights, axis=0, keepdims=True)
        mixed = contract(values, weights.astype(BF), 1, 0)
        out_ref[rows, :] = (mixed / totals).astype(BF)
        lse_ref[0, head : head + 1, :] = peak + jnp.log(totals)


def backward_kernel(
    q_ref,
    k_ref,
    v_ref,
    grad_ref,
    lse_ref,
    cos_ref,
    sin_ref,
    bias_ref,
    token_ref,
    dq_ref,
    dkv_ref,
    *ring_refs,
):
    count = q_ref.shape[1]
    keys, values = k_ref[...], v_ref[...]
    cosine, sine = cos_ref[:, :count], sin_ref[:, :count]
    grad_keys = jnp.zeros(keys.shape, F32)
    grad_values = jnp.zeros(keys.shape, F32)
    for head in range(RATIO):
        rows = slice(head * HEAD_SIZE, (head + 1) * HEAD_SIZE)
        queries, grads = q_ref[rows, :], grad_ref[rows, :]
        scores = contract(keys, queries, 0, 0) * SCALE + bias_ref[...]
        probs = jnp.exp(scores - lse_ref[0, head : head + 1, :])
        grad_probs = contract(values, grads, 0, 0)
        centre = jnp.sum(probs * grad_probs, axis=0, keepdims=True)
        grad_scores = (probs * (grad_probs - centre)).astype(BF)
        grad_queries = contract(keys, grad_scores, 1, 0) * SCALE
        dq_ref[rows, :] = rotate(grad_queries, cosine, -sine).astype(BF)
        grad_keys += contract(queries, grad_scores, 1, 1)
        grad_values += contract(grads, probs.astype(BF), 1, 1)
    grad_keys = rotate(grad_keys * SCALE, cos_ref[...], -sin_ref[...]).astype(BF)
    grad_values = grad_values.astype(BF)
    dkv_ref[0] = grad_keys
    dkv_ref[1] = grad_values
    for block, ring_ref in enumerate(ring_refs):
        at = slice(block * count, (block + 1) * count)
        ring_ref[0] = grad_keys[:, at]
        ring_ref[1] = grad_values[:, at]


def attention_forward(queries, keys, values, bias):
    count, span = queries.shape[1], keys.shape[1]
    pair = RATIO * HEAD_SIZE
    mine = lambda rows, cols: pl.BlockSpec((rows, cols), lambda g: (g, 0))
    return pl.pallas_call(
        forward_kernel,
        grid=(KEY_VALUE_HEADS,),
        in_specs=[
            mine(pair, count),
            mine(HEAD_SIZE, span),
            mine(HEAD_SIZE, span),
            pl.BlockSpec(bias.shape, lambda g: (0, 0)),
        ],
        out_specs=[
            mine(pair, count),
            pl.BlockSpec((1, RATIO, count), lambda g: (g, 0, 0)),
        ],
        out_shape=[
            jax.ShapeDtypeStruct(queries.shape, BF),
            jax.ShapeDtypeStruct((KEY_VALUE_HEADS, RATIO, count), F32),
        ],
        compiler_params=pltpu.CompilerParams(vmem_limit_bytes=VMEM_BYTES),
        cost_estimate=lasting(0.1),
        name="attention_forward",
    )(queries, keys, values, bias)


def attention_backward(heads, queries, keys, values, grads, totals, cosine, sine, bias, token, blocks):
    count, span = queries.shape[1], keys.shape[1]
    pair = RATIO * HEAD_SIZE
    first, amount = heads.start, len(heads)
    whole = lambda a: pl.BlockSpec(a.shape, lambda g: (0,) * a.ndim)
    mine = lambda rows, cols: pl.BlockSpec((rows, cols), lambda g: (g + first, 0))
    rows = amount * HEAD_SIZE
    return pl.pallas_call(
        backward_kernel,
        grid=(amount,),
        in_specs=[
            mine(pair, count),
            mine(HEAD_SIZE, span),
            mine(HEAD_SIZE, span),
            mine(pair, count),
            pl.BlockSpec((1, RATIO, count), lambda g: (g + first, 0, 0)),
            whole(cosine),
            whole(sine),
            whole(bias),
            whole(token),
        ],
        out_specs=[
            pl.BlockSpec((pair, count), lambda g: (g, 0)),
            pl.BlockSpec((2, HEAD_SIZE, span), lambda g: (0, g, 0)),
        ]
        + [pl.BlockSpec((2, HEAD_SIZE, count), lambda g: (0, g, 0))] * blocks,
        out_shape=[
            jax.ShapeDtypeStruct((amount * pair, count), BF),
            jax.ShapeDtypeStruct((2, rows, span), BF),
        ]
        + [jax.ShapeDtypeStruct((2, rows, count), BF)] * blocks,
        compiler_params=pltpu.CompilerParams(vmem_limit_bytes=VMEM_BYTES),
        cost_estimate=lasting(0.1),
        name="attention_backward",
    )(queries, keys, values, grads, totals, cosine, sine, bias, token)


def product(left, right):
    return jnp.dot(left, right, preferred_element_type=F32)


def over_rows(left, right):
    return lax.dot_general(left, right, (((0,), (0,)), ((), ())), preferred_element_type=F32)


def times_transposed(left, right):
    return lax.dot_general(left, right, (((1,), (1,)), ((), ())), preferred_element_type=F32)


def blank(shape, dtype):
    return pl.pallas_call(
        lambda out_ref: None,
        out_shape=jax.ShapeDtypeStruct(shape, dtype),
        out_specs=pl.BlockSpec(memory_space=pl.ANY),
        name="blank",
    )()


def terms_kernel(steps, by_rows, owners_ref, left_ref, *refs):
    rights, (away_ref, mine_ref, total_ref) = refs[:-3], refs[-3:]
    step = pl.program_id(0)
    slots, n, rows, cols = away_ref.shape
    for right_ref, (first, last) in zip(rights, steps):

        @pl.when((step >= first) & (step < last))
        def _(right_ref=right_ref):
            if by_rows:
                right = right_ref[...]
                product = contract(left_ref[:, : right.shape[1]], right, 1, 1)
            else:
                product = contract(left_ref[...], right_ref[...], 1, 0)
            total_ref[...] = product.astype(BF)

    for slot in range(slots):
        for z in range(n):
            base = z * 2 * slots * rows
            for out_ref, at in ((mine_ref, slot), (away_ref, slots + slot)):
                start = pl.multiple_of(base + owners_ref[at] * rows, 16)
                out_ref[slot, z] = total_ref[pl.ds(start, rows), :]


def owned_terms(owners, n, left, rights, by_rows):
    tile = 256
    depth = left.shape[0] // (8 * n)
    steps, first = [], 0
    for right in rights:
        last = first + right.shape[0 if by_rows else 1] // tile
        steps.append((first, last))
        first = last
    specs = []
    for right, (start, stop) in zip(rights, steps):
        if by_rows:
            specs.append(
                pl.BlockSpec(
                    (tile, right.shape[1]),
                    lambda j, o, start=start, stop=stop: (jnp.clip(j, start, stop - 1) - start, 0),
                )
            )
        else:
            specs.append(pl.BlockSpec((right.shape[0], tile), lambda j, o: (0, j)))
    out = jax.ShapeDtypeStruct((4, n, depth, first * tile), BF)
    out_spec = pl.BlockSpec((4, n, depth, tile), lambda j, o: (0, 0, 0, j))
    return pl.pallas_call(
        lambda *refs: terms_kernel(steps, by_rows, *refs),
        grid_spec=pltpu.PrefetchScalarGridSpec(
            num_scalar_prefetch=1,
            grid=(first,),
            in_specs=[pl.BlockSpec(left.shape, lambda j, o: (0, 0))] + specs,
            out_specs=[out_spec, out_spec],
            scratch_shapes=[pltpu.VMEM((left.shape[0], tile), BF)],
        ),
        out_shape=[out, out],
        compiler_params=pltpu.CompilerParams(vmem_limit_bytes=VMEM_BYTES),
        cost_estimate=lasting(0.1),
        name="owned_terms",
    )(owners, left, *rights)


def project_kernel(n, count, starts_ref, *refs):
    parts, blocks, (cos_ref, sin_ref) = refs[:count], refs[count : count + n], refs[count + n : count + n + 2]
    refs = refs[count + n + 2 :]
    q_ref, k_ref, v_ref, normed_ref, weight_out, weight_ref, token_ref, part_sem, token_sem, out_sem = refs
    rows, (count, width) = parts[0].shape[1], blocks[0].shape
    token_copies = [
        pltpu.make_async_copy(block, token_ref.at[pl.ds(k * count, count)], token_sem.at[k])
        for k, block in enumerate(blocks)
    ]
    part_copies = []
    for part in parts:
        for j in range(part.shape[0]):
            k = len(part_copies)
            at = pl.multiple_of(starts_ref[k], 16)
            part_copies.append(
                pltpu.make_async_copy(part.at[j], weight_ref.at[pl.ds(at, rows)], part_sem.at[k])
            )
    for copy in token_copies + part_copies:
        copy.start()
    for k, copy in enumerate(token_copies):
        copy.wait()
        x = token_ref[k * count : (k + 1) * count, :].astype(F32)
        inverse = lax.rsqrt(jnp.mean(x * x, axis=-1, keepdims=True) + EPSILON)
        normed_ref[:, k * count : (k + 1) * count] = (x * inverse).astype(BF).T
    for copy in part_copies:
        copy.wait()
    out_copy = pltpu.make_async_copy(weight_ref, weight_out, out_sem)
    out_copy.start()
    pair_cols = k_ref.shape[0]
    tile = 4 * HEAD_SIZE
    for out_ref, base, rotated in ((q_ref, 0, True), (k_ref, width, True), (v_ref, width + pair_cols, False)):
        tokens = out_ref.shape[1]

        def step(j, carry, out_ref=out_ref, base=base, rotated=rotated, tokens=tokens):
            at = pl.multiple_of(j * tile, tile)
            columns = weight_ref[:, pl.ds(pl.multiple_of(base + at, 128), tile)]
            product = contract(columns, normed_ref[:, :tokens], 0, 0)
            for head in range(4):
                part = product[head * HEAD_SIZE : (head + 1) * HEAD_SIZE]
                if rotated:
                    part = rotate(part, cos_ref[:, :tokens], sin_ref[:, :tokens])
                start = pl.multiple_of(at + head * HEAD_SIZE, 16)
                out_ref[pl.ds(start, HEAD_SIZE), :] = part.astype(BF)
            return carry

        lax.fori_loop(0, out_ref.shape[0] // tile, step, 0)
    out_copy.wait()


def project(starts, parts, blocks, cosine, sine):
    rows, cols = parts[0].shape[1:]
    n, (count, width) = len(blocks), blocks[0].shape
    span, pair_cols = n * count, KEY_VALUE_HEADS * HEAD_SIZE
    every = pl.BlockSpec(memory_space=pl.ANY)
    vmem = pl.BlockSpec(memory_space=pltpu.VMEM)
    shape = (starts.shape[0] * rows, cols)
    return pl.pallas_call(
        lambda *refs: project_kernel(n, len(parts), *refs),
        in_specs=[pl.BlockSpec(memory_space=pltpu.SMEM)] + [every] * (len(parts) + n) + [vmem, vmem],
        out_specs=[vmem, vmem, vmem, vmem, every],
        out_shape=[
            jax.ShapeDtypeStruct((width, count), BF),
            jax.ShapeDtypeStruct((pair_cols, span), BF),
            jax.ShapeDtypeStruct((pair_cols, span), BF),
            jax.ShapeDtypeStruct((width, span), BF),
            jax.ShapeDtypeStruct(shape, BF),
        ],
        scratch_shapes=[
            pltpu.VMEM(shape, BF),
            pltpu.VMEM((span, width), BF),
            pltpu.SemaphoreType.DMA(starts.shape),
            pltpu.SemaphoreType.DMA((n,)),
            pltpu.SemaphoreType.DMA,
        ],
        compiler_params=pltpu.CompilerParams(vmem_limit_bytes=MOST_VMEM_BYTES),
        cost_estimate=lasting(0.1),
        name="project",
    )(starts, *parts, *blocks, cosine, sine)


def feed_kernel(count, first, *refs):
    parts, grads, blocks_ref = refs[:count], refs[count : 2 * count], refs[2 * count]
    refs = refs[2 * count + 1 :]
    if not first:
        earlier_ref, refs = refs[0], refs[1:]
    scaled_ref, hidden_ref, both_ref, sum_ref, down_ref = refs[:5]
    total_ref, part_ref, grad_ref, block_ref, weight_ref, part_sem, grad_sem, block_sem = refs[5:]
    step = pl.program_id(0)
    units = hidden_ref.shape[1]
    (n, rows, _), width = block_ref.shape, down_ref.shape[1]
    unit = units // n
    pieces = rows // unit
    piece = width // pieces

    def copies(k):
        return (
            pltpu.make_async_copy(parts[k], part_ref.at[k], part_sem.at[k]),
            pltpu.make_async_copy(grads[k], grad_ref.at[k], grad_sem.at[k]),
        )

    @pl.when(step == 0)
    def _():
        block_copies = [
            pltpu.make_async_copy(blocks_ref.at[k], block_ref.at[k], block_sem.at[k])
            for k in range(n)
        ]
        for copy in block_copies:
            copy.start()
        for k in range(count):
            for copy in copies(k):
                copy.start()
        for k, copy in enumerate(block_copies):
            copy.wait()
            weight_ref[k * rows : (k + 1) * rows, :] = block_ref[k, :, : 2 * units]
            for j in range(pieces):
                down_ref[k * unit : (k + 1) * unit, j * piece : (j + 1) * piece] = block_ref[
                    k, j * unit : (j + 1) * unit, 2 * units :
                ]
        total_ref[...] = jnp.zeros_like(total_ref) if first else earlier_ref[...]

    for k in range(count):

        @pl.when(step == k)
        def _(k=k):
            for copy in copies(k):
                copy.wait()

    part, grad = part_ref[step], grad_ref[step]
    gate = product(part, weight_ref[:, :units])
    upper = product(part, weight_ref[:, units:])
    sigmoid = jax.nn.sigmoid(gate)
    silu = gate * sigmoid
    hidden = (silu * upper).astype(BF)
    hidden_ref[...] = hidden
    grad_hidden = contract(grad, down_ref[...], 1, 1)
    grad_gate = (grad_hidden * upper * sigmoid * (1.0 + gate * (1.0 - sigmoid))).astype(BF)
    grad_up = (grad_hidden * silu).astype(BF)
    both_ref[:, :units] = grad_gate
    both_ref[:, units:] = grad_up
    scaled = contract(grad_gate, weight_ref[:, :units], 1, 1)
    scaled += contract(grad_up, weight_ref[:, units:], 1, 1)
    scaled_ref[...] = scaled.astype(BF)
    total_ref[...] += contract(hidden, grad, 0, 0)

    @pl.when(step == count - 1)
    def _():
        sum_ref[...] = total_ref[...].astype(sum_ref.dtype)


def feed_forward(parts, grads, blocks, units, earlier=None):
    count, n = len(parts), blocks.shape[0]
    rows, width = parts[0].shape
    every = pl.BlockSpec(memory_space=pl.ANY)
    part = lambda cols: pl.BlockSpec((rows, cols), lambda k: (k, 0))
    whole = pl.BlockSpec((units, width), lambda k: (0, 0))
    first = earlier is None
    return pl.pallas_call(
        lambda *refs: feed_kernel(count, first, *refs),
        grid=(count,),
        in_specs=[every] * (2 * count + 1) + ([] if first else [whole]),
        out_specs=[part(width), part(units), part(2 * units), whole, whole],
        out_shape=[
            jax.ShapeDtypeStruct((count * rows, width), BF),
            jax.ShapeDtypeStruct((count * rows, units), BF),
            jax.ShapeDtypeStruct((count * rows, 2 * units), BF),
            jax.ShapeDtypeStruct((units, width), F32 if first else BF),
            jax.ShapeDtypeStruct((units, width), BF),
        ],
        scratch_shapes=[
            pltpu.VMEM((units, width), F32),
            pltpu.VMEM((count, rows, width), BF),
            pltpu.VMEM((count, rows, width), BF),
            pltpu.VMEM(blocks.shape, BF),
            pltpu.VMEM((n * blocks.shape[1], 2 * units), BF),
            pltpu.SemaphoreType.DMA((count,)),
            pltpu.SemaphoreType.DMA((count,)),
            pltpu.SemaphoreType.DMA((n,)),
        ],
        compiler_params=pltpu.CompilerParams(vmem_limit_bytes=VMEM_BYTES),
        cost_estimate=lasting(30),
        name="feed_forward",
    )(*parts, *grads, blocks, *(() if first else (earlier,)))


def gate_up_kernel(count, *refs):
    parts, boths, out_ref, token_ref = refs[:count], refs[count:-2], refs[-2], refs[-1]
    token_ref[...] = jnp.zeros_like(token_ref)
    rows = parts[0].shape[0]
    each = boths[0].shape[0] // rows
    total = jnp.zeros(out_ref.shape, F32)
    for k, part in enumerate(parts):
        at = k % each * rows
        total += contract(part[...], boths[k // each][at : at + rows, :], 0, 0)
    out_ref[...] = total.astype(BF)


def gate_up_terms_of(parts, boths):
    rows, width = parts[0].shape
    cols = boths[0].shape[1]
    tile = 256
    return pl.pallas_call(
        lambda *refs: gate_up_kernel(len(parts), *refs),
        grid=(width // tile,),
        in_specs=[pl.BlockSpec((rows, tile), lambda j: (0, j))] * len(parts)
        + [pl.BlockSpec(both.shape, lambda j: (0, 0)) for both in boths],
        out_specs=[
            pl.BlockSpec((tile, cols), lambda j: (j, 0)),
            pl.BlockSpec((8, 128), lambda j: (0, 0)),
        ],
        out_shape=[
            jax.ShapeDtypeStruct((width, cols), BF),
            jax.ShapeDtypeStruct((8, 128), F32),
        ],
        compiler_params=pltpu.CompilerParams(vmem_limit_bytes=VMEM_BYTES),
        cost_estimate=lasting(15),
        name="gate_up_terms",
    )(*parts, *boths)


def on_device(n, ranks, *operands):
    (
        tokens,
        gain_attn,
        w_query,
        key_weight,
        value_weight,
        w_out,
        gain_mlp,
        w_gate,
        w_up,
        w_down,
        out_grad,
        lengths,
        stretch_map,
    ) = operands
    at_z, rank = lax.axis_index("z"), lax.axis_index("f")
    grid = ranks == 8
    turn = rank % 2
    first, second = 4 >> turn, 2 << turn
    scope = jax.named_scope

    def stage(*arrays):
        return lax.optimization_barrier(arrays)

    def shift(a, by):
        return lax.ppermute(a, "z", [(i, (i + by) % n) for i in range(n)])

    def swap_first(a):
        return lax.ppermute(a, "f", [(i, i ^ (4 >> i % 2)) for i in range(ranks)])

    def swap_second(a):
        return lax.ppermute(a, "f", [(i, i ^ (2 << i % 2)) for i in range(ranks)])

    def swap_core(a):
        return lax.ppermute(a, "f", [(i, i ^ 1) for i in range(ranks)])

    def pick(a, index, axis):
        return lax.dynamic_index_in_dim(a, index, axis, keepdims=False)

    def put(a, piece, *index):
        index = index + (0,) * (a.ndim - len(index))
        return lax.dynamic_update_slice(a, piece, index)

    def direct(a):
        return [a] + [shift(a, by) for by in range(1, n)]

    def stack_z(blocks):
        out = blank((n,) + blocks[0].shape, BF)
        for k, block in enumerate(blocks):
            out = put(out, block[None], (at_z - k) % n)
        return out

    def send_z(terms):
        sent = [shift(pick(terms, (at_z - by) % n, 0), -by) for by in range(1, n)]
        return [pick(terms, at_z, 0)] + sent

    def total(terms):
        return sum(term.astype(F32) for term in terms)

    def add(a, b):
        return (a.astype(F32) + b.astype(F32)).astype(BF)

    def spread_second(pair):
        return swap_second(pair) if grid else pair

    def spread_all(pair, other):
        if grid:
            return [pair, other, swap_core(pair), swap_core(other)]
        rows = lax.all_gather(pair, "f", tiled=True)
        return jnp.split(rows, rows.shape[0] // (2 * pair.shape[0]))

    def send_core(terms):
        return swap_core(terms) if grid else terms

    def add_halves(terms, arrived):
        half = terms.shape[0] // 2
        far = add(terms[half:], arrived[half:])
        return add(terms[:half], arrived[:half]), far

    if grid:
        owners = [rank, rank ^ first, rank ^ second, rank ^ 6]
        owners += [rank ^ 1, rank ^ 1 ^ second, rank ^ 1 ^ first, rank ^ 7]
        owners = jnp.stack(owners).astype(jnp.int32)

    def weight_terms(left, rights, by_rows):
        if grid:
            return owned_terms(owners, n, left, rights, by_rows)
        columns = [
            contract(left[:, : r.shape[1]], r, 1, 1) if by_rows else product(left, r)
            for r in rights
        ]
        terms = jnp.concatenate(columns, axis=1).astype(BF)
        return terms, terms

    def sum_f(mine):
        terms = mine.reshape(n, ranks, -1, mine.shape[1]).transpose(1, 0, 2, 3)
        return lax.psum_scatter(terms, "f", scatter_dimension=0, tiled=False)

    token_count, width = tokens.shape[1:]
    shard_rows = w_query.shape[0]
    unit = w_down.shape[0]
    hidden_units = n * unit
    pair_cols = KEY_VALUE_HEADS * HEAD_SIZE
    gain_one = gain_attn.astype(F32)[:, None]
    gain_two = gain_mlp.astype(F32)[:, None]

    def along(weight, grad):
        return jnp.sum(weight.astype(F32) * grad, axis=1)

    def scaled(weight, gain):
        return (weight.astype(F32) * gain).astype(BF)

    shard = jnp.concatenate([w_query, key_weight, value_weight], axis=1)
    shard = jnp.concatenate([scaled(shard, gain_one), w_out], axis=1)
    own = tokens[0]
    blocks = [own]
    grad_own = grad_first = out_grad[0]
    if grid:
        with scope("attention_weights_z"):
            behind = [shift(shard, by) for by in range(1, n)]
        with scope("attention_weights_own"):
            near = [shard, swap_first(shard), swap_second(shard)]
    with scope("gate_up_f"):
        gate_up = scaled(jnp.concatenate([w_gate, w_up], axis=1), gain_two)
        gate_up = gate_up.reshape(shard_rows, 2, n, ranks, unit).transpose(3, 0, 1, 2, 4)
        gate_up = gate_up.reshape(ranks, shard_rows, 2 * hidden_units)
        gate_up = lax.all_to_all(gate_up, "f", 0, 0, tiled=True)
        gate_up_rows = ranks * shard_rows
        gate_up = gate_up.reshape(gate_up_rows, 2 * hidden_units)
        pieces = gate_up_rows // unit
        down = w_down.reshape(unit, pieces, width // pieces).transpose(1, 0, 2)
        gate_up_down = jnp.concatenate(
            [gate_up, down.reshape(gate_up_rows, width // pieces)], axis=1
        )

    if grid:
        with scope("attention_weights_own"):
            near.append(swap_second(near[1]))
        *behind, near[2], near[3], gate_up_down = stage(*behind, near[2], near[3], gate_up_down)
        with scope("attention_weights_core"):
            near_core = [swap_core(part) for part in near]
        rest = [jnp.stack(behind)]
        with scope("attention_weights_first"):
            rest.append(swap_first(rest[0]))
        with scope("tokens_z"):
            blocks.append(shift(own, 1))
        rest[0], rest[1], blocks[1], *near_core = stage(rest[0], rest[1], blocks[1], *near_core)
        with scope("attention_weights_core"):
            rest_core = [swap_core(rest[0])]
        with scope("attention_weights_second"):
            rest.append(swap_second(rest[0]))
        with scope("tokens_z"):
            blocks.append(shift(blocks[1], 1))
        rest[1], rest[2], blocks[2], rest_core[0] = stage(
            rest[1], rest[2], blocks[2], rest_core[0]
        )
        with scope("attention_weights_core"):
            rest_core += [swap_core(rest[1]), swap_core(rest[2])]
        with scope("attention_weights_second"):
            rest.append(swap_second(rest[1]))
        with scope("out_grad_first"):
            grad_first = swap_first(grad_own)
        with scope("tokens_z"):
            while len(blocks) < n:
                blocks.append(shift(blocks[-1], 1))
        rest[3], blocks[-1], grad_first, *rest_core = stage(
            rest[3], blocks[-1], grad_first, *rest_core
        )
        with scope("attention_weights_core"):
            rest_core.append(swap_core(rest[3]))
    else:
        while len(blocks) < n:
            blocks.append(shift(blocks[-1], 1))
    with scope("gate_up_down_z"):
        gate_up_down, blocks[-1] = stage(gate_up_down, blocks[-1])
        gate_up_down = lax.all_gather(gate_up_down, "z")
    cuts = [width, width + pair_cols, width + 2 * pair_cols]

    slots_each = stretch_map.shape[1] // n
    slots = (
        ((at_z - jnp.arange(n, dtype=jnp.int32)) % n)[:, None] * slots_each
        + jnp.arange(slots_each, dtype=jnp.int32)[None, :]
    ).reshape(-1)
    doc_all, place_all = layout(lengths[0], stretch_map[0], slots)
    allowed = (doc_all[:, None] == doc_all[None, :token_count]) & (
        place_all[:, None] <= place_all[None, :token_count]
    )
    bias = jnp.where(allowed, 0.0, -1e30).astype(F32)
    cosine, sine = rotary_tables(place_all)

    inputs = own.astype(F32)
    first_inverse = lax.rsqrt(jnp.mean(inputs * inputs, axis=-1, keepdims=True) + EPSILON)
    first_normed = inputs * first_inverse
    if grid:
        parts, starts = [], []
        for near_parts, rest_parts, moves in (
            (near, rest, (0, first, second, 6)),
            (near_core, rest_core, (1, 1 ^ second, 1 ^ first, 7)),
        ):
            for near_part, rest_part, move in zip(near_parts, rest_parts, moves):
                parts += [near_part[None], rest_part]
                starts += [(at_z - k) % n * ranks + (rank ^ move) for k in range(n)]
        starts = jnp.stack(starts).astype(jnp.int32) * shard_rows
        queries, keys, values, normed_group, gathered = project(
            starts, parts, blocks, cosine, sine
        )
        q_weight, key_matrix, value_matrix, out_weight = jnp.split(gathered, cuts, axis=1)
    else:
        gathered = lax.all_gather(shard, ("z", "f"), tiled=True)
        q_weight, key_matrix, value_matrix, out_weight = jnp.split(gathered, cuts, axis=1)
        normed_group = jnp.concatenate(blocks, axis=0).astype(F32)
        inverse = lax.rsqrt(jnp.mean(normed_group * normed_group, axis=-1, keepdims=True) + EPSILON)
        normed_group = (normed_group * inverse).astype(BF).T

        def rotated(weight, tokens):
            rows = contract(weight, normed_group[:, :tokens], 0, 0)
            rows = rows.reshape(-1, HEAD_SIZE, tokens)
            turned = [rotate(r, cosine[:, :tokens], sine[:, :tokens]) for r in rows]
            return jnp.concatenate(turned, axis=0).astype(BF)

        queries, keys = rotated(q_weight, token_count), rotated(key_matrix, n * token_count)
        values = contract(value_matrix, normed_group, 0, 0).astype(BF)
    span = n * token_count

    with scope("out_grad_second"):
        grad_pair = jnp.concatenate([grad_own, grad_first], axis=0) if grid else grad_own
        grad_other = spread_second(grad_pair)

    attention_output, log_totals = attention_forward(queries, keys, values, bias)
    resid = inputs + contract(attention_output, out_weight, 0, 0)
    second_inverse = lax.rsqrt(jnp.mean(resid * resid, axis=-1, keepdims=True) + EPSILON)
    second_normed = resid * second_inverse
    normed_two = second_normed.astype(BF)
    normed_two, grad_other = stage(normed_two, grad_other)

    with scope("normed_first"):
        normed_first = swap_first(normed_two) if grid else normed_two
    with scope("out_grad_all"):
        grad_parts = spread_all(grad_pair, grad_other)
    with scope("normed_second"):
        (normed_first,) = stage(normed_first)
        normed_pair = normed_first
        if grid:
            normed_pair = jnp.concatenate([normed_two, normed_first], axis=0)
        normed_other = spread_second(normed_pair)
        normed_parts = spread_all(normed_pair, normed_other)
    half = len(normed_parts) // 2

    scaled_far, hidden_far, both_far, down_terms, down_weight = feed_forward(
        normed_parts[half:], grad_parts[half:], gate_up_down, hidden_units
    )
    with scope("scaled_core"):
        scaled_far = send_core(scaled_far)
    scaled_near, hidden_near, both_near, down_terms, _ = feed_forward(
        normed_parts[:half], grad_parts[:half], gate_up_down, hidden_units, down_terms
    )
    with scope("down_sum_z"):
        down_owned = lax.psum_scatter(down_terms, "z", scatter_dimension=0, tiled=True)

    def norm_back(scaled_grad, normed, inverse):
        return inverse * (
            scaled_grad - normed * jnp.mean(scaled_grad * normed, axis=-1, keepdims=True)
        )

    with scope("scaled_second"):
        if grid:
            scaled_near, far = add_halves(scaled_near, scaled_far)
            far, both_near = stage(far, both_near)
            far = swap_second(far)
        else:
            scaled_two = jnp.concatenate([scaled_near, scaled_far], axis=0)
            scaled_two = lax.psum_scatter(scaled_two, "f", scatter_dimension=0, tiled=True)
            scaled_two = far = scaled_two.astype(F32)
    with scope("gate_up_sum_z"):
        gate_up_terms, token = gate_up_terms_of(normed_parts, [both_near, both_far])
        gate_up_owned = lax.psum_scatter(gate_up_terms, "z", scatter_dimension=0, tiled=True)
    with scope("result_core"):
        hidden_far, token = stage(hidden_far, token)
        result_far = send_core(product(hidden_far, down_weight).astype(BF))
        result_near = product(hidden_near, down_weight).astype(BF)
        if grid:
            result_near, result_far = add_halves(result_near, result_far)
        else:
            result = jnp.concatenate([result_near, result_far], axis=0)
            result = lax.psum_scatter(result, "f", scatter_dimension=0, tiled=True)
            result_near = result_far = result
    far, result_far = stage(far, result_far)
    if grid:
        with scope("scaled_first"):
            scaled_near, far = add_halves(scaled_near, far)
            far, result_far = stage(swap_first(far), result_far)
            scaled_two = scaled_near.astype(F32) + far.astype(F32)
        with scope("result_second"):
            result_far = swap_second(result_far)
    grad_resid = out_grad[0].astype(F32) + norm_back(scaled_two, second_normed, second_inverse)
    grad_attn_out = grad_resid.astype(BF)

    with scope("out_core"):
        out_away, out_mine = weight_terms(attention_output, [grad_attn_out], False)
        out_away = send_core(out_away)
    grad_mixed = contract(out_weight, grad_attn_out, 1, 1).astype(BF)
    grad_mixed, out_away = stage(grad_mixed, out_away)
    with scope("out_second"):
        if grid:
            out_near, out_far = add_halves(out_mine, out_away)
            out_far = swap_second(out_far)
        else:
            out_near = out_far = sum_f(out_mine)
    grad_queries, grad_kv, *by_block = attention_backward(
        range(KEY_VALUE_HEADS),
        queries,
        keys,
        values,
        grad_mixed,
        log_totals,
        cosine,
        sine,
        bias,
        token,
        n,
    )
    grad_queries, result_far, down_owned = stage(grad_queries, result_far, down_owned)

    def pass_on(total):
        with scope("kv_grad_z"):
            return shift(total, 1)

    arrived = pass_on(by_block[1])
    if grid:
        with scope("result_first"):
            result_near, result_far = add_halves(result_near, result_far)
            result_far = swap_first(result_far)
    with scope("projected_core"):
        away, mine = weight_terms(
            normed_group, [grad_queries, grad_kv.reshape(2 * pair_cols, span)], True
        )
    away, arrived, out_far, result_far, gate_up_owned = stage(
        away, arrived, out_far, result_far, gate_up_owned
    )
    with scope("projected_core"):
        away = send_core(away)
    arrived = pass_on(add(arrived, by_block[2 % n]))
    if grid:
        result = result_near.astype(F32) + result_far.astype(F32)
        with scope("out_first"):
            out_near, out_far = add_halves(out_near, out_far)
            out_far = swap_first(out_far)
        with scope("projected_second"):
            near, far = add_halves(mine, away)
            far, out_far = stage(far, out_far)
            far = swap_second(far)
        out_near = add(out_near[0], out_far[0])
    else:
        result = result.astype(F32)
        near = far = sum_f(mine)
    result = (resid + result).astype(BF)
    with scope("out_z"):
        out_owned = total(send_z(out_near))
    arrived, far, out_owned = stage(arrived, far, out_owned)
    for step in range(3, n):
        arrived = pass_on(add(arrived, by_block[step]))
    if grid:
        with scope("projected_first"):
            near, far = add_halves(near, far)
            far = swap_first(far)
    far, gate_up_owned = stage(far, gate_up_owned)
    with scope("projected_z"):
        projected = send_z(add(near[0], far[0]) if grid else near)
    with scope("gate_up_sum_f"):
        gate_up_owned = lax.all_to_all(
            gate_up_owned.reshape(ranks, shard_rows, 2 * hidden_units), "f", 0, 0, tiled=True
        )
    kv_total = add(arrived, by_block[0])
    scaled_one = (
        contract(grad_queries, q_weight, 0, 1)
        + contract(kv_total[0], key_matrix, 0, 1)
        + contract(kv_total[1], value_matrix, 0, 1)
    )

    gate_up_owned = (
        gate_up_owned.astype(F32)
        .reshape(ranks, shard_rows, 2, n, unit)
        .transpose(2, 1, 3, 0, 4)
        .reshape(2, shard_rows, n * ranks * unit)
    )
    gate_owned, up_owned = gate_up_owned[0], gate_up_owned[1]
    gain_two_owned = along(w_gate, gate_owned) + along(w_up, up_owned)
    scaled_one, gain_two_owned, *projected = stage(scaled_one, gain_two_owned, *projected)
    input_grad = (grad_resid + norm_back(scaled_one, first_normed, first_inverse)).astype(BF)
    projected_owned = total(projected)
    query_owned, key_owned, value_owned = jnp.split(projected_owned, cuts[:2], axis=1)

    gain_one_owned = (
        along(w_query, query_owned)
        + along(key_weight, key_owned)
        + along(value_weight, value_owned)
    )
    return (
        result[None],
        input_grad[None],
        gain_one_owned,
        query_owned * gain_one,
        key_owned * gain_one,
        value_owned * gain_one,
        out_owned,
        gain_two_owned,
        gate_owned * gain_two,
        up_owned * gain_two,
        down_owned.astype(F32),
    )


def solution(mesh):
    n, ranks = mesh.shape["seq"], mesh.shape["fsdp"]
    named = Mesh(mesh.devices, ("z", "f"))
    every = ("z", "f")
    rows, vector, matrix = P("f", "z", None), P(every), P(every, None)
    in_specs = (
        rows,
        vector,
        matrix,
        matrix,
        matrix,
        matrix,
        vector,
        matrix,
        matrix,
        matrix,
        rows,
        P("f", None),
        P("f", None),
    )
    out_specs = (rows, rows, vector) + (matrix,) * 4 + (vector,) + (matrix,) * 3

    def step(*operands):
        return on_device(n, ranks, *operands)

    return jax.shard_map(
        step, mesh=named, in_specs=in_specs, out_specs=out_specs, check_vma=False
    )
```

```python
import math

import jax
import jax.numpy as jnp
from jax import lax
from jax.experimental import pallas as pl
from jax.experimental.pallas import tpu as pltpu
from jax.sharding import Mesh
from jax.sharding import PartitionSpec as P

QUERY_HEADS = 16
KEY_VALUE_HEADS = 8
HEAD_SIZE = 96
FF = 4096
STRETCH = 128

EPSILON = 1e-05
THETA = 100000.0

BF = jnp.bfloat16
F32 = jnp.float32


def layout(doc_lengths, slot_map, slots):
    count = slot_map.shape[0]
    stretches = jnp.arange(count, dtype=jnp.int32)
    logical = jnp.sum(
        jnp.where(slot_map[None, :] == slots[:, None], stretches[None, :], 0), axis=1
    )
    places = (
        logical[:, None] * STRETCH + jnp.arange(STRETCH, dtype=jnp.int32)[None, :]
    ).reshape(-1)
    endings = jnp.cumsum(doc_lengths)
    passed = endings[None, :] <= places[:, None]
    document = jnp.sum(passed.astype(jnp.int32), axis=1)
    starts = jnp.sum(jnp.where(passed, doc_lengths[None, :], 0), axis=1)
    return document, places - starts


def rotary_tables(positions):
    half = HEAD_SIZE // 2
    freqs = THETA ** (-2.0 * jnp.arange(half, dtype=F32) / HEAD_SIZE)
    angles = positions.astype(F32)[:, None] * freqs[None, :]
    return jnp.cos(angles).T, jnp.sin(angles).T


def rotate(rows, cosine, sine):
    half = rows.shape[0] // 2
    first, second = rows[:half], rows[half:]
    return jnp.concatenate(
        [first * cosine - second * sine, second * cosine + first * sine], axis=0
    )


def contract(left, right, at_left, at_right):
    return lax.dot_general(
        left, right, (((at_left,), (at_right,)), ((), ())), preferred_element_type=F32
    )


RATIO = QUERY_HEADS // KEY_VALUE_HEADS
SCALE = 1.0 / math.sqrt(HEAD_SIZE)
VMEM_BYTES = 40 * 1024 * 1024
MOST_VMEM_BYTES = 60 * 1024 * 1024


def lasting(microseconds):
    return pl.CostEstimate(
        flops=int(microseconds * 1e9), bytes_accessed=int(microseconds * 3e6), transcendentals=0
    )


def forward_kernel(q_ref, k_ref, v_ref, bias_ref, out_ref, lse_ref):
    keys, values = k_ref[...], v_ref[...]
    for head in range(RATIO):
        rows = slice(head * HEAD_SIZE, (head + 1) * HEAD_SIZE)
        scores = contract(keys, q_ref[rows, :], 0, 0) * SCALE + bias_ref[...]
        peak = jnp.max(scores, axis=0, keepdims=True)
        weights = jnp.exp(scores - peak)
        totals = jnp.sum(weights, axis=0, keepdims=True)
        mixed = contract(values, weights.astype(BF), 1, 0)
        out_ref[rows, :] = (mixed / totals).astype(BF)
        lse_ref[0, head : head + 1, :] = peak + jnp.log(totals)


def backward_kernel(
    place_ref,
    q_ref,
    k_ref,
    v_ref,
    grad_ref,
    lse_ref,
    cos_ref,
    sin_ref,
    bias_ref,
    token_ref,
    dq_ref,
    dkv_ref,
    block_ref,
):
    count = q_ref.shape[1]
    keys, values = k_ref[...], v_ref[...]
    cosine, sine = cos_ref[:, :count], sin_ref[:, :count]
    grad_keys = jnp.zeros(keys.shape, F32)
    grad_values = jnp.zeros(keys.shape, F32)
    for head in range(RATIO):
        rows = slice(head * HEAD_SIZE, (head + 1) * HEAD_SIZE)
        queries, grads = q_ref[rows, :], grad_ref[rows, :]
        scores = contract(keys, queries, 0, 0) * SCALE + bias_ref[...]
        probs = jnp.exp(scores - lse_ref[0, head : head + 1, :])
        grad_probs = contract(values, grads, 0, 0)
        centre = jnp.sum(probs * grad_probs, axis=0, keepdims=True)
        grad_scores = (probs * (grad_probs - centre)).astype(BF)
        grad_queries = contract(keys, grad_scores, 1, 0) * SCALE
        dq_ref[rows, :] = rotate(grad_queries, cosine, -sine).astype(BF)
        grad_keys += contract(queries, grad_scores, 1, 1)
        grad_values += contract(grads, probs.astype(BF), 1, 1)
    grad_keys = rotate(grad_keys * SCALE, cos_ref[...], -sin_ref[...]).astype(BF)
    grad_values = grad_values.astype(BF)
    dkv_ref[0] = grad_keys
    dkv_ref[1] = grad_values
    blocks = block_ref.shape[0]
    for block in range(blocks):
        at = slice(block * count, (block + 1) * count)
        place = lax.rem(place_ref[0] - block + blocks, blocks)
        block_ref[place, 0] = grad_keys[:, at]
        block_ref[place, 1] = grad_values[:, at]


def attention_forward(queries, keys, values, bias):
    count, span = queries.shape[1], keys.shape[1]
    pair = RATIO * HEAD_SIZE
    mine = lambda rows, cols: pl.BlockSpec((rows, cols), lambda g: (g, 0))
    return pl.pallas_call(
        forward_kernel,
        grid=(KEY_VALUE_HEADS,),
        in_specs=[
            mine(pair, count),
            mine(HEAD_SIZE, span),
            mine(HEAD_SIZE, span),
            pl.BlockSpec(bias.shape, lambda g: (0, 0)),
        ],
        out_specs=[
            mine(pair, count),
            pl.BlockSpec((1, RATIO, count), lambda g: (g, 0, 0)),
        ],
        out_shape=[
            jax.ShapeDtypeStruct(queries.shape, BF),
            jax.ShapeDtypeStruct((KEY_VALUE_HEADS, RATIO, count), F32),
        ],
        compiler_params=pltpu.CompilerParams(vmem_limit_bytes=MOST_VMEM_BYTES),
        cost_estimate=lasting(0.1),
        name="attention_forward",
    )(queries, keys, values, bias)


def attention_backward(place, heads, queries, keys, values, grads, totals, cosine, sine, bias, token, blocks):
    count, span = queries.shape[1], keys.shape[1]
    pair = RATIO * HEAD_SIZE
    first, amount = heads.start, len(heads)
    whole = lambda a: pl.BlockSpec(a.shape, lambda g: (0,) * a.ndim)
    mine = lambda rows, cols: pl.BlockSpec((rows, cols), lambda g: (g + first, 0))
    rows = amount * HEAD_SIZE
    return pl.pallas_call(
        backward_kernel,
        grid=(amount,),
        in_specs=[
            pl.BlockSpec(memory_space=pltpu.SMEM),
            mine(pair, count),
            mine(HEAD_SIZE, span),
            mine(HEAD_SIZE, span),
            mine(pair, count),
            pl.BlockSpec((1, RATIO, count), lambda g: (g + first, 0, 0)),
            whole(cosine),
            whole(sine),
            whole(bias),
            whole(token),
        ],
        out_specs=[
            pl.BlockSpec((pair, count), lambda g: (g, 0)),
            pl.BlockSpec((2, HEAD_SIZE, span), lambda g: (0, g, 0)),
            pl.BlockSpec((blocks, 2, HEAD_SIZE, count), lambda g: (0, 0, g, 0)),
        ],
        out_shape=[
            jax.ShapeDtypeStruct((amount * pair, count), BF),
            jax.ShapeDtypeStruct((2, rows, span), BF),
            jax.ShapeDtypeStruct((blocks, 2, rows, count), BF),
        ],
        compiler_params=pltpu.CompilerParams(vmem_limit_bytes=VMEM_BYTES),
        cost_estimate=lasting(0.1),
        name="attention_backward",
    )(place, queries, keys, values, grads, totals, cosine, sine, bias, token)


def product(left, right):
    return jnp.dot(left, right, preferred_element_type=F32)


def over_rows(left, right):
    return lax.dot_general(left, right, (((0,), (0,)), ((), ())), preferred_element_type=F32)


def times_transposed(left, right):
    return lax.dot_general(left, right, (((1,), (1,)), ((), ())), preferred_element_type=F32)


def blank(shape, dtype):
    return pl.pallas_call(
        lambda out_ref: None,
        out_shape=jax.ShapeDtypeStruct(shape, dtype),
        out_specs=pl.BlockSpec(memory_space=pl.ANY),
        name="blank",
    )()


def terms_kernel(steps, by_rows, owners_ref, left_ref, *refs):
    rights, (away_ref, mine_ref, total_ref) = refs[:-3], refs[-3:]
    step = pl.program_id(0)
    slots, n, rows, cols = away_ref.shape
    for right_ref, (first, last) in zip(rights, steps):

        @pl.when((step >= first) & (step < last))
        def _(right_ref=right_ref):
            if by_rows:
                right = right_ref[...]
                product = contract(left_ref[:, : right.shape[1]], right, 1, 1)
            else:
                product = contract(left_ref[...], right_ref[...], 1, 0)
            total_ref[...] = product.astype(BF)

    for slot in range(slots):
        for z in range(n):
            base = z * 2 * slots * rows
            for out_ref, at in ((mine_ref, slot), (away_ref, slots + slot)):
                start = pl.multiple_of(base + owners_ref[at] * rows, 16)
                out_ref[slot, z] = total_ref[pl.ds(start, rows), :]


def owned_terms(owners, n, left, rights, by_rows):
    tile = 256
    depth = left.shape[0] // (8 * n)
    steps, first = [], 0
    for right in rights:
        last = first + right.shape[0 if by_rows else 1] // tile
        steps.append((first, last))
        first = last
    specs = []
    for right, (start, stop) in zip(rights, steps):
        if by_rows:
            specs.append(
                pl.BlockSpec(
                    (tile, right.shape[1]),
                    lambda j, o, start=start, stop=stop: (jnp.clip(j, start, stop - 1) - start, 0),
                )
            )
        else:
            specs.append(pl.BlockSpec((right.shape[0], tile), lambda j, o: (0, j)))
    out = jax.ShapeDtypeStruct((4, n, depth, first * tile), BF)
    out_spec = pl.BlockSpec((4, n, depth, tile), lambda j, o: (0, 0, 0, j))
    return pl.pallas_call(
        lambda *refs: terms_kernel(steps, by_rows, *refs),
        grid_spec=pltpu.PrefetchScalarGridSpec(
            num_scalar_prefetch=1,
            grid=(first,),
            in_specs=[pl.BlockSpec(left.shape, lambda j, o: (0, 0))] + specs,
            out_specs=[out_spec, out_spec],
            scratch_shapes=[pltpu.VMEM((left.shape[0], tile), BF)],
        ),
        out_shape=[out, out],
        compiler_params=pltpu.CompilerParams(vmem_limit_bytes=VMEM_BYTES),
        cost_estimate=lasting(0.1),
        name="owned_terms",
    )(owners, left, *rights)


def project_kernel(n, count, starts_ref, *refs):
    parts, blocks, (cos_ref, sin_ref) = refs[:count], refs[count : count + n], refs[count + n : count + n + 2]
    refs = refs[count + n + 2 :]
    q_ref, k_ref, v_ref, normed_ref, weight_out, weight_ref, token_ref, part_sem, token_sem, out_sem = refs
    rows, (count, width) = parts[0].shape[1], blocks[0].shape
    token_copies = [
        pltpu.make_async_copy(block, token_ref.at[pl.ds(k * count, count)], token_sem.at[k])
        for k, block in enumerate(blocks)
    ]
    part_copies = []
    for part in parts:
        for j in range(part.shape[0]):
            k = len(part_copies)
            at = pl.multiple_of(starts_ref[k], 16)
            part_copies.append(
                pltpu.make_async_copy(part.at[j], weight_ref.at[pl.ds(at, rows)], part_sem.at[k])
            )
    for copy in token_copies + part_copies:
        copy.start()
    for k, copy in enumerate(token_copies):
        copy.wait()
        x = token_ref[k * count : (k + 1) * count, :].astype(F32)
        inverse = lax.rsqrt(jnp.mean(x * x, axis=-1, keepdims=True) + EPSILON)
        normed_ref[:, k * count : (k + 1) * count] = (x * inverse).astype(BF).T
    for copy in part_copies:
        copy.wait()
    out_copy = pltpu.make_async_copy(weight_ref, weight_out, out_sem)
    out_copy.start()
    pair_cols = k_ref.shape[0]
    tile = 4 * HEAD_SIZE
    for out_ref, base, rotated in ((q_ref, 0, True), (k_ref, width, True), (v_ref, width + pair_cols, False)):
        tokens = out_ref.shape[1]

        def step(j, carry, out_ref=out_ref, base=base, rotated=rotated, tokens=tokens):
            at = pl.multiple_of(j * tile, tile)
            columns = weight_ref[:, pl.ds(pl.multiple_of(base + at, 128), tile)]
            product = contract(columns, normed_ref[:, :tokens], 0, 0)
            for head in range(4):
                part = product[head * HEAD_SIZE : (head + 1) * HEAD_SIZE]
                if rotated:
                    part = rotate(part, cos_ref[:, :tokens], sin_ref[:, :tokens])
                start = pl.multiple_of(at + head * HEAD_SIZE, 16)
                out_ref[pl.ds(start, HEAD_SIZE), :] = part.astype(BF)
            return carry

        lax.fori_loop(0, out_ref.shape[0] // tile, step, 0)
    out_copy.wait()


def project(starts, parts, blocks, cosine, sine):
    rows, cols = parts[0].shape[1:]
    n, (count, width) = len(blocks), blocks[0].shape
    span, pair_cols = n * count, KEY_VALUE_HEADS * HEAD_SIZE
    every = pl.BlockSpec(memory_space=pl.ANY)
    vmem = pl.BlockSpec(memory_space=pltpu.VMEM)
    shape = (starts.shape[0] * rows, cols)
    return pl.pallas_call(
        lambda *refs: project_kernel(n, len(parts), *refs),
        in_specs=[pl.BlockSpec(memory_space=pltpu.SMEM)] + [every] * (len(parts) + n) + [vmem, vmem],
        out_specs=[vmem, vmem, vmem, vmem, every],
        out_shape=[
            jax.ShapeDtypeStruct((width, count), BF),
            jax.ShapeDtypeStruct((pair_cols, span), BF),
            jax.ShapeDtypeStruct((pair_cols, span), BF),
            jax.ShapeDtypeStruct((width, span), BF),
            jax.ShapeDtypeStruct(shape, BF),
        ],
        scratch_shapes=[
            pltpu.VMEM(shape, BF),
            pltpu.VMEM((span, width), BF),
            pltpu.SemaphoreType.DMA(starts.shape),
            pltpu.SemaphoreType.DMA((n,)),
            pltpu.SemaphoreType.DMA,
        ],
        compiler_params=pltpu.CompilerParams(vmem_limit_bytes=MOST_VMEM_BYTES),
        cost_estimate=lasting(0.1),
        name="project",
    )(starts, *parts, *blocks, cosine, sine)


def feed_kernel(count, first, *refs):
    parts, grads, blocks_ref = refs[:count], refs[count : 2 * count], refs[2 * count]
    refs = refs[2 * count + 1 :]
    if not first:
        earlier_ref, refs = refs[0], refs[1:]
    scaled_ref, hidden_ref, both_ref, sum_ref, down_ref = refs[:5]
    total_ref, part_ref, grad_ref, weight_ref, part_sem, grad_sem, block_sem = refs[5:]
    step = pl.program_id(0)
    units = hidden_ref.shape[1]
    (n, rows, _), width = blocks_ref.shape, down_ref.shape[1]
    unit = units // n
    pieces = rows // unit
    piece = width // pieces

    def copies(k):
        return (
            pltpu.make_async_copy(parts[k], part_ref.at[k], part_sem.at[k]),
            pltpu.make_async_copy(grads[k], grad_ref.at[k], grad_sem.at[k]),
        )

    @pl.when(step == 0)
    def _():
        block_copies = [
            pltpu.make_async_copy(
                blocks_ref.at[k, :, : 2 * units],
                weight_ref.at[pl.ds(k * rows, rows)],
                block_sem.at[k * (1 + pieces)],
            )
            for k in range(n)
        ]
        block_copies += [
            pltpu.make_async_copy(
                blocks_ref.at[k, pl.ds(j * unit, unit), 2 * units :],
                down_ref.at[pl.ds(k * unit, unit), j * piece : (j + 1) * piece],
                block_sem.at[k * (1 + pieces) + 1 + j],
            )
            for k in range(n)
            for j in range(pieces)
        ]
        for copy in block_copies:
            copy.start()
        for k in range(count):
            for copy in copies(k):
                copy.start()
        for copy in block_copies:
            copy.wait()
        total_ref[...] = jnp.zeros_like(total_ref) if first else earlier_ref[...]

    for k in range(count):

        @pl.when(step == k)
        def _(k=k):
            for copy in copies(k):
                copy.wait()

    part, grad = part_ref[step], grad_ref[step]
    gate = product(part, weight_ref[:, :units])
    upper = product(part, weight_ref[:, units:])
    sigmoid = jax.nn.sigmoid(gate)
    silu = gate * sigmoid
    hidden = (silu * upper).astype(BF)
    hidden_ref[...] = hidden
    grad_hidden = contract(grad, down_ref[...], 1, 1)
    grad_gate = (grad_hidden * upper * sigmoid * (1.0 + gate * (1.0 - sigmoid))).astype(BF)
    grad_up = (grad_hidden * silu).astype(BF)
    both_ref[:, :units] = grad_gate
    both_ref[:, units:] = grad_up
    scaled = contract(grad_gate, weight_ref[:, :units], 1, 1)
    scaled += contract(grad_up, weight_ref[:, units:], 1, 1)
    scaled_ref[...] = scaled.astype(BF)
    total_ref[...] += contract(hidden, grad, 0, 0)

    @pl.when(step == count - 1)
    def _():
        sum_ref[...] = total_ref[...].astype(sum_ref.dtype)


def feed_forward(parts, grads, blocks, units, earlier=None):
    count, n = len(parts), blocks.shape[0]
    rows, width = parts[0].shape
    every = pl.BlockSpec(memory_space=pl.ANY)
    part = lambda cols: pl.BlockSpec((rows, cols), lambda k: (k, 0))
    whole = pl.BlockSpec((units, width), lambda k: (0, 0))
    first = earlier is None
    return pl.pallas_call(
        lambda *refs: feed_kernel(count, first, *refs),
        grid=(count,),
        in_specs=[every] * (2 * count + 1) + ([] if first else [whole]),
        out_specs=[part(width), part(units), part(2 * units), whole, whole],
        out_shape=[
            jax.ShapeDtypeStruct((count * rows, width), BF),
            jax.ShapeDtypeStruct((count * rows, units), BF),
            jax.ShapeDtypeStruct((count * rows, 2 * units), BF),
            jax.ShapeDtypeStruct((units, width), F32 if first else BF),
            jax.ShapeDtypeStruct((units, width), BF),
        ],
        scratch_shapes=[
            pltpu.VMEM((units, width), F32),
            pltpu.VMEM((count, rows, width), BF),
            pltpu.VMEM((count, rows, width), BF),
            pltpu.VMEM((n * blocks.shape[1], 2 * units), BF),
            pltpu.SemaphoreType.DMA((count,)),
            pltpu.SemaphoreType.DMA((count,)),
            pltpu.SemaphoreType.DMA((n * (1 + blocks.shape[1] * n // units),)),
        ],
        compiler_params=pltpu.CompilerParams(vmem_limit_bytes=MOST_VMEM_BYTES),
        cost_estimate=lasting(30),
        name="feed_forward",
    )(*parts, *grads, blocks, *(() if first else (earlier,)))


def add_kernel(a_ref, b_ref, out_ref):
    out_ref[...] = (a_ref[0].astype(F32) + b_ref[0].astype(F32)).astype(BF)


def add_half(a, b, which):
    cols = a.shape[-1]
    both = [x.reshape(2, -1, cols) for x in (a, b)]
    rows = both[0].shape[1]
    tile = rows // 2 if rows % 32 == 0 else rows
    out = pl.pallas_call(
        add_kernel,
        grid=(rows // tile,),
        in_specs=[pl.BlockSpec((1, tile, cols), lambda j: (which, j, 0))] * 2,
        out_specs=pl.BlockSpec((tile, cols), lambda j: (j, 0)),
        out_shape=jax.ShapeDtypeStruct((rows, cols), BF),
        compiler_params=pltpu.CompilerParams(vmem_limit_bytes=VMEM_BYTES),
        cost_estimate=lasting(0.1),
        name="add_half",
    )(*both)
    return out.reshape((a.shape[0] // 2,) + a.shape[1:])


def feed_terms_kernel(count, *refs):
    parts, (down_ref, *boths, out_ref, token_ref) = refs[:count], refs[count:]
    token_ref[...] = jnp.zeros_like(token_ref)
    rows, cols = parts[0].shape[0], boths[0].shape[1]
    unit, width = down_ref.shape
    pieces = out_ref.shape[0] // unit
    piece = width // pieces
    each = boths[0].shape[0] // rows
    total = jnp.zeros((out_ref.shape[0], cols), F32)
    for k, part in enumerate(parts):
        at = k % each * rows
        total += contract(part[...], boths[k // each][at : at + rows, :], 0, 0)
    out_ref[:, :cols] = total.astype(BF)
    for j in range(pieces):
        out_ref[j * unit : (j + 1) * unit, cols:] = down_ref[:, j * piece : (j + 1) * piece]


def feed_terms(parts, down, boths, n):
    rows, width = parts[0].shape
    tile, cols = width // n, boths[0].shape[1]
    unit = down.shape[0] // n
    more = width * unit // tile
    return pl.pallas_call(
        lambda *refs: feed_terms_kernel(len(parts), *refs),
        grid=(n,),
        in_specs=[pl.BlockSpec((rows, tile), lambda j: (0, j))] * len(parts)
        + [pl.BlockSpec((unit, width), lambda j: (j, 0))]
        + [pl.BlockSpec(both.shape, lambda j: (0, 0)) for both in boths],
        out_specs=[
            pl.BlockSpec((tile, cols + more), lambda j: (j, 0)),
            pl.BlockSpec((8, 128), lambda j: (0, 0)),
        ],
        out_shape=[
            jax.ShapeDtypeStruct((width, cols + more), BF),
            jax.ShapeDtypeStruct((8, 128), F32),
        ],
        compiler_params=pltpu.CompilerParams(vmem_limit_bytes=VMEM_BYTES),
        cost_estimate=lasting(15),
        name="feed_terms",
    )(*parts, down, *boths)


def feed_finish_kernel(
    arrived_ref, gate_ref, up_ref, gain_ref, gate_out, up_out, gain_out
):
    ranks, rows, cols = arrived_ref.shape
    units = cols // 2
    n = gate_ref.shape[1] // (ranks * 128)
    unit = units // n
    gain = gain_ref[...]
    total = jnp.zeros((rows, unit), F32)
    for r in range(ranks):
        for z in range(n):
            at = slice((z * ranks + r) * unit, (z * ranks + r + 1) * unit)
            for half, weight_ref, out_ref in ((0, gate_ref, gate_out), (units, up_ref, up_out)):
                start = half + z * unit
                grad = arrived_ref[r, :, start : start + unit].astype(F32)
                out_ref[:, at] = grad * gain
                total += grad * weight_ref[:, at].astype(F32)
    gain_out[...] = jnp.sum(total, axis=1, keepdims=True)


def feed_finish(arrived, gate, up, gain):
    return pl.pallas_call(
        feed_finish_kernel,
        out_shape=[
            jax.ShapeDtypeStruct(gate.shape, F32),
            jax.ShapeDtypeStruct(up.shape, F32),
            jax.ShapeDtypeStruct(gain.shape, F32),
        ],
        compiler_params=pltpu.CompilerParams(vmem_limit_bytes=VMEM_BYTES),
        cost_estimate=lasting(0.1),
        name="feed_finish",
    )(arrived, gate, up, gain)


def attention_finish_kernel(n, *refs):
    projected, outs, weights = refs[:n], refs[n : 2 * n], refs[2 * n : 2 * n + 3]
    gain_ref, *grad_refs, out_ref, gain_out = refs[2 * n + 3 :]
    gain = gain_ref[...]
    out_ref[...] = sum(ref[...].astype(F32) for ref in outs)
    first = 0
    total = jnp.zeros(gain.shape, F32)
    for weight_ref, grad_ref in zip(weights, grad_refs):
        at = slice(first, first + weight_ref.shape[1])
        first = at.stop
        grad = sum(ref[:, at].astype(F32) for ref in projected)
        grad_ref[...] = grad * gain
        total += jnp.sum(grad * weight_ref[...].astype(F32), axis=1, keepdims=True)
    gain_out[...] = total


def attention_finish(projected, outs, weights, gain):
    shapes = [weight.shape for weight in weights] + [outs[0].shape, gain.shape]
    return pl.pallas_call(
        lambda *refs: attention_finish_kernel(len(outs), *refs),
        out_shape=[jax.ShapeDtypeStruct(shape, F32) for shape in shapes],
        compiler_params=pltpu.CompilerParams(vmem_limit_bytes=VMEM_BYTES),
        cost_estimate=lasting(0.1),
        name="attention_finish",
    )(*projected, *outs, *weights, gain)


def input_kernel(query_ref, pair_ref, weight_ref, own_ref, resid_ref, out_ref, left_ref, total_ref):
    step = pl.program_id(0)
    queries, tile = query_ref.shape[0], weight_ref.shape[0]

    @pl.when(step == 0)
    def _():
        left_ref[:, :queries] = query_ref[...].T
        left_ref[:, queries:] = pair_ref[...].T

    at = pl.multiple_of(step * tile, tile)
    total_ref[:, pl.ds(at, tile)] = contract(
        left_ref[...], weight_ref[:, : left_ref.shape[1]], 1, 1
    )

    @pl.when(step == pl.num_programs(0) - 1)
    def _():
        x, scaled = own_ref[...].astype(F32), total_ref[...]
        inverse = lax.rsqrt(jnp.mean(x * x, axis=-1, keepdims=True) + EPSILON)
        normed = x * inverse
        mean = jnp.mean(scaled * normed, axis=-1, keepdims=True)
        out_ref[...] = (resid_ref[...] + inverse * (scaled - normed * mean)).astype(BF)


def input_gradient(queries, pairs, weight, own, resid):
    count, width = own.shape
    tile = 256
    whole = lambda a: pl.BlockSpec(a.shape, lambda j: (0, 0))
    features = queries.shape[0] + pairs.shape[0]
    return pl.pallas_call(
        input_kernel,
        grid=(width // tile,),
        in_specs=[
            whole(queries),
            whole(pairs),
            pl.BlockSpec((tile, weight.shape[1]), lambda j: (j, 0)),
            whole(own),
            whole(resid),
        ],
        out_specs=pl.BlockSpec((count, width), lambda j: (0, 0)),
        out_shape=jax.ShapeDtypeStruct((count, width), BF),
        scratch_shapes=[pltpu.VMEM((count, features), BF), pltpu.VMEM((count, width), F32)],
        compiler_params=pltpu.CompilerParams(vmem_limit_bytes=VMEM_BYTES),
        cost_estimate=lasting(0.1),
        name="input_gradient",
    )(queries, pairs, weight, own, resid)


def on_device(n, ranks, *operands):
    (
        tokens,
        gain_attn,
        w_query,
        key_weight,
        value_weight,
        w_out,
        gain_mlp,
        w_gate,
        w_up,
        w_down,
        out_grad,
        lengths,
        stretch_map,
    ) = operands
    at_z, rank = lax.axis_index("z"), lax.axis_index("f")
    grid = ranks == 8 and w_down.shape[0] % 128 == 0
    turn = rank % 2
    first, second = 4 >> turn, 2 << turn
    scope = jax.named_scope

    def stage(*arrays):
        return lax.optimization_barrier(arrays)

    def shift(a, by):
        return lax.ppermute(a, "z", [(i, (i + by) % n) for i in range(n)])

    def swap_first(a):
        return lax.ppermute(a, "f", [(i, i ^ (4 >> i % 2)) for i in range(ranks)])

    def swap_second(a):
        return lax.ppermute(a, "f", [(i, i ^ (2 << i % 2)) for i in range(ranks)])

    def swap_core(a):
        return lax.ppermute(a, "f", [(i, i ^ 1) for i in range(ranks)])

    def pick(a, index, axis):
        return lax.dynamic_index_in_dim(a, index, axis, keepdims=False)

    def put(a, piece, *index):
        index = index + (0,) * (a.ndim - len(index))
        return lax.dynamic_update_slice(a, piece, index)

    def direct(a):
        return [a] + [shift(a, by) for by in range(1, n)]

    def stack_z(blocks):
        out = blank((n,) + blocks[0].shape, BF)
        for k, block in enumerate(blocks):
            out = put(out, block[None], (at_z - k) % n)
        return out

    def send_z(terms):
        sent = [shift(pick(terms, (at_z - by) % n, 0), -by) for by in range(1, n)]
        return [pick(terms, at_z, 0)] + sent

    def total(terms):
        return sum(term.astype(F32) for term in terms)

    def add(a, b):
        return (a.astype(F32) + b.astype(F32)).astype(BF)

    def spread_second(pair):
        return swap_second(pair) if grid else pair

    def spread_all(pair, other):
        if grid:
            return [pair, other, swap_core(pair), swap_core(other)]
        rows = lax.all_gather(pair, "f", tiled=True)
        return jnp.split(rows, rows.shape[0] // (2 * pair.shape[0]))

    def send_core(terms):
        return swap_core(terms) if grid else terms

    def add_halves(terms, arrived):
        return add_half(terms, arrived, 0), add_half(terms, arrived, 1)

    if grid:
        owners = [rank, rank ^ first, rank ^ second, rank ^ 6]
        owners += [rank ^ 1, rank ^ 1 ^ second, rank ^ 1 ^ first, rank ^ 7]
        owners = jnp.stack(owners).astype(jnp.int32)

    def weight_terms(left, rights, by_rows):
        if grid:
            return owned_terms(owners, n, left, rights, by_rows)
        columns = [
            contract(left[:, : r.shape[1]], r, 1, 1) if by_rows else product(left, r)
            for r in rights
        ]
        terms = jnp.concatenate(columns, axis=1).astype(BF)
        return terms, terms

    def sum_f(mine):
        terms = mine.reshape(n, ranks, -1, mine.shape[1]).transpose(1, 0, 2, 3)
        return lax.psum_scatter(terms, "f", scatter_dimension=0, tiled=False)

    token_count, width = tokens.shape[1:]
    shard_rows = w_query.shape[0]
    unit = w_down.shape[0]
    hidden_units = n * unit
    pair_cols = KEY_VALUE_HEADS * HEAD_SIZE
    gain_one = gain_attn.astype(F32)[:, None]
    gain_two = gain_mlp.astype(F32)[:, None]

    def along(weight, grad):
        return jnp.sum(weight.astype(F32) * grad, axis=1)

    slots_each = stretch_map.shape[1] // n
    slots = (
        ((at_z - jnp.arange(n, dtype=jnp.int32)) % n)[:, None] * slots_each
        + jnp.arange(slots_each, dtype=jnp.int32)[None, :]
    ).reshape(-1)
    doc_all, place_all = layout(lengths[0], stretch_map[0], slots)
    allowed = (doc_all[:, None] == doc_all[None, :token_count]) & (
        place_all[:, None] <= place_all[None, :token_count]
    )
    bias = jnp.where(allowed, 0.0, -1e30).astype(F32)
    cosine, sine = rotary_tables(place_all)

    def scaled(weight, gain):
        return (weight.astype(F32) * gain).astype(BF)

    shard = jnp.concatenate([w_query, key_weight, value_weight], axis=1)
    shard = jnp.concatenate([scaled(shard, gain_one), w_out], axis=1)
    own = tokens[0]
    blocks = [own]
    gate_up = scaled(jnp.concatenate([w_gate, w_up], axis=1), gain_two)
    gate_up = gate_up.reshape(shard_rows, 2, n, ranks, unit).transpose(3, 0, 1, 2, 4)
    gate_up = gate_up.reshape(ranks, shard_rows, 2 * hidden_units)
    grad_own = grad_first = out_grad[0]
    if grid:
        with scope("attention_weights_z"):
            behind = [shift(shard, 1)]
            while len(behind) < n - 1:
                behind.append(shift(behind[-1], 1))
        with scope("attention_weights_own"):
            near = [shard, swap_first(shard), swap_second(shard)]
    if grid:
        with scope("attention_weights_own"):
            near.append(swap_second(near[1]))
        with scope("tokens_z"):
            blocks.append(shift(own, 1))
        with scope("out_grad_first"):
            grad_first = swap_first(grad_own)
        *behind, near[2], near[3], gate_up, blocks[1], grad_first = stage(
            *behind, near[2], near[3], gate_up, blocks[1], grad_first
        )
        with scope("attention_weights_core"):
            near_core = [swap_core(part) for part in near]
        rest = [jnp.stack(behind)]
        with scope("gate_up_f"):
            gate_up = lax.all_to_all(gate_up, "f", 0, 0, tiled=True)
            gate_up_rows = ranks * shard_rows
            gate_up = gate_up.reshape(gate_up_rows, 2 * hidden_units)
            pieces = gate_up_rows // unit
            down = w_down.reshape(unit, pieces, width // pieces).transpose(1, 0, 2)
            gate_up_down = jnp.concatenate(
                [gate_up, down.reshape(gate_up_rows, width // pieces)], axis=1
            )
        with scope("attention_weights_first"):
            rest.append(swap_first(rest[0]))
        with scope("tokens_z"):
            blocks.append(shift(blocks[1], 1))
        rest[0], rest[1], blocks[2], cosine, sine, bias, gate_up_down, *near_core = stage(
            rest[0], rest[1], blocks[2], cosine, sine, bias, gate_up_down, *near_core
        )
        with scope("attention_weights_core"):
            rest_core = [swap_core(rest[0]), swap_core(rest[1])]
        with scope("attention_weights_second"):
            rest += [swap_second(rest[0]), swap_second(rest[1])]
        with scope("tokens_z"):
            while len(blocks) < n:
                blocks.append(shift(blocks[-1], 1))
        rest[2], rest[3], blocks[-1], *rest_core = stage(rest[2], rest[3], blocks[-1], *rest_core)
        with scope("attention_weights_core"):
            rest_core += [swap_core(rest[2]), swap_core(rest[3])]
    else:
        with scope("gate_up_f"):
            gate_up = lax.all_to_all(gate_up, "f", 0, 0, tiled=True)
            gate_up_rows = ranks * shard_rows
            gate_up = gate_up.reshape(gate_up_rows, 2 * hidden_units)
            pieces = gate_up_rows // unit
            down = w_down.reshape(unit, pieces, width // pieces).transpose(1, 0, 2)
            gate_up_down = jnp.concatenate(
                [gate_up, down.reshape(gate_up_rows, width // pieces)], axis=1
            )
        while len(blocks) < n:
            blocks.append(shift(blocks[-1], 1))
    with scope("gate_up_down_z"):
        gate_up_down, blocks[-1] = stage(gate_up_down, blocks[-1])
        gate_up_down = lax.all_gather(gate_up_down, "z")
    cuts = [width, width + pair_cols, width + 2 * pair_cols]

    inputs = own.astype(F32)
    if grid:
        parts, starts = [], []
        for near_parts, rest_parts, moves in (
            (near, rest, (0, first, second, 6)),
            (near_core, rest_core, (1, 1 ^ second, 1 ^ first, 7)),
        ):
            for near_part, rest_part, move in zip(near_parts, rest_parts, moves):
                parts += [near_part[None], rest_part]
                starts += [(at_z - k) % n * ranks + (rank ^ move) for k in range(n)]
        starts = jnp.stack(starts).astype(jnp.int32) * shard_rows
        queries, keys, values, normed_group, gathered = project(
            starts, parts, blocks, cosine, sine
        )
        q_weight, key_matrix, value_matrix, out_weight = jnp.split(gathered, cuts, axis=1)
    else:
        gathered = lax.all_gather(shard, ("z", "f"), tiled=True)
        q_weight, key_matrix, value_matrix, out_weight = jnp.split(gathered, cuts, axis=1)
        normed_group = jnp.concatenate(blocks, axis=0).astype(F32)
        inverse = lax.rsqrt(jnp.mean(normed_group * normed_group, axis=-1, keepdims=True) + EPSILON)
        normed_group = (normed_group * inverse).astype(BF).T

        def rotated(weight, tokens):
            rows = contract(weight, normed_group[:, :tokens], 0, 0)
            rows = rows.reshape(-1, HEAD_SIZE, tokens)
            turned = [rotate(r, cosine[:, :tokens], sine[:, :tokens]) for r in rows]
            return jnp.concatenate(turned, axis=0).astype(BF)

        queries, keys = rotated(q_weight, token_count), rotated(key_matrix, n * token_count)
        values = contract(value_matrix, normed_group, 0, 0).astype(BF)
    span = n * token_count

    with scope("out_grad_second"):
        grad_pair = jnp.concatenate([grad_own, grad_first], axis=0) if grid else grad_own
        grad_other = spread_second(grad_pair)

    attention_output, log_totals = attention_forward(queries, keys, values, bias)
    resid = inputs + contract(attention_output, out_weight, 0, 0)
    second_inverse = lax.rsqrt(jnp.mean(resid * resid, axis=-1, keepdims=True) + EPSILON)
    second_normed = resid * second_inverse
    normed_two = second_normed.astype(BF)
    normed_two, grad_other = stage(normed_two, grad_other)

    with scope("normed_first"):
        normed_first = swap_first(normed_two) if grid else normed_two
    with scope("out_grad_all"):
        grad_parts = spread_all(grad_pair, grad_other)
    with scope("normed_second"):
        (normed_first,) = stage(normed_first)
        normed_pair = normed_first
        if grid:
            normed_pair = jnp.concatenate([normed_two, normed_first], axis=0)
        normed_other = spread_second(normed_pair)
        normed_parts = spread_all(normed_pair, normed_other)
    half = len(normed_parts) // 2

    scaled_far, hidden_far, both_far, down_terms, down_weight = feed_forward(
        normed_parts[half:], grad_parts[half:], gate_up_down, hidden_units
    )
    with scope("scaled_core"):
        scaled_far = send_core(scaled_far)
    scaled_near, hidden_near, both_near, down_terms, _ = feed_forward(
        normed_parts[:half], grad_parts[:half], gate_up_down, hidden_units, down_terms
    )
    def norm_back(scaled_grad, normed, inverse):
        return inverse * (
            scaled_grad - normed * jnp.mean(scaled_grad * normed, axis=-1, keepdims=True)
        )

    with scope("scaled_second"):
        if grid:
            scaled_near, far = add_halves(scaled_near, scaled_far)
            far, both_near = stage(far, both_near)
            far = swap_second(far)
        else:
            scaled_two = jnp.concatenate([scaled_near, scaled_far], axis=0)
            scaled_two = lax.psum_scatter(scaled_two, "f", scatter_dimension=0, tiled=True)
            scaled_two = far = scaled_two.astype(F32)
    with scope("feed_sum_z"):
        if grid:
            terms, token = feed_terms(normed_parts, down_terms, [both_near, both_far], n)
        else:
            terms = over_rows(
                jnp.concatenate(normed_parts, axis=0),
                jnp.concatenate([both_near, both_far], axis=0),
            ).astype(BF)
            down_terms = down_terms.reshape(n, unit, pieces, width // pieces)
            down_terms = down_terms.transpose(0, 2, 1, 3).reshape(width, width // pieces)
            terms = jnp.concatenate([terms, down_terms], axis=1)
            token = jnp.zeros((8, 128), F32)
        feed_owned = lax.psum_scatter(terms, "z", scatter_dimension=0, tiled=True)
    far, token = stage(far, token)
    if grid:
        with scope("scaled_first"):
            scaled_near, far = add_halves(scaled_near, far)
            far = swap_first(far)
    if grid:
        (far,) = stage(far)
        scaled_two = scaled_near.astype(F32) + far.astype(F32)
    grad_resid = out_grad[0].astype(F32) + norm_back(scaled_two, second_normed, second_inverse)
    grad_attn_out = grad_resid.astype(BF)

    with scope("out_core"):
        out_away, out_mine = weight_terms(attention_output, [grad_attn_out], False)
        out_away = send_core(out_away)
    grad_mixed = contract(out_weight, grad_attn_out, 1, 1).astype(BF)
    grad_mixed, out_away = stage(grad_mixed, out_away)
    with scope("out_second"):
        if grid:
            out_near, out_far = add_halves(out_mine, out_away)
            out_far = swap_second(out_far)
        else:
            out_near = out_far = sum_f(out_mine)
    grad_queries, grad_kv, by_block = attention_backward(
        at_z.astype(jnp.int32)[None],
        range(KEY_VALUE_HEADS),
        queries,
        keys,
        values,
        grad_mixed,
        log_totals,
        cosine,
        sine,
        bias,
        token,
        n,
    )
    grad_queries, out_far = stage(grad_queries, out_far)

    with scope("kv_grad_z"):
        kv_total = lax.psum_scatter(by_block, "z", scatter_dimension=0, tiled=False)
    with scope("projected_core"):
        away, mine = weight_terms(
            normed_group, [grad_queries, grad_kv.reshape(2 * pair_cols, span)], True
        )
    if grid:
        with scope("out_first"):
            out_near, out_far = add_halves(out_near, out_far)
            out_far = swap_first(out_far)
        away, out_far = stage(away, out_far)
        with scope("projected_core"):
            away = send_core(away)
        away, hidden_far, hidden_near = stage(away, hidden_far, hidden_near)
        with scope("projected_second"):
            near, far = add_halves(mine, away)
            far = swap_second(far)
        out_near = add(out_near[0], out_far[0])
    with scope("result_core"):
        result_far = send_core(product(hidden_far, down_weight).astype(BF))
        result_near = product(hidden_near, down_weight).astype(BF)
    def exchange(owned):
        with scope("gate_up_sum_f"):
            owned = owned[:, : 2 * hidden_units].reshape(ranks, shard_rows, -1)
            return lax.all_to_all(owned, "f", 0, 0, tiled=True)

    if grid:
        result_near, result_far = add_halves(result_near, result_far)
        far, result_far = stage(far, result_far)
        with scope("projected_first"):
            near, far = add_halves(near, far)
            far = swap_first(far)
        with scope("out_z"):
            out_owned = send_z(out_near)
        with scope("result_f"):
            own_part, first_part = jnp.split(result_near, 2)
            second_part, both_part = jnp.split(result_far, 2)
            both_part = lax.ppermute(both_part, "f", [(i, i ^ 6) for i in range(ranks)])
            first_part, second_part = swap_first(first_part), swap_second(second_part)
        gate_up_owned = exchange(feed_owned)
        far, kv_total, gate_up_owned, first_part, second_part, both_part, *out_owned = stage(
            far, kv_total, gate_up_owned, first_part, second_part, both_part, *out_owned
        )
        result = own_part.astype(F32) + first_part.astype(F32)
        result = result + second_part.astype(F32) + both_part.astype(F32)
        near = add(near[0], far[0])
    else:
        near = sum_f(mine)
        gate_up_owned = exchange(feed_owned)
        result = jnp.concatenate([result_near, result_far], axis=0)
        result = lax.psum_scatter(result, "f", scatter_dimension=0, tiled=True)
        with scope("out_z"):
            out_owned = send_z(out_near)
    with scope("projected_z"):
        projected = send_z(near)
    result = (resid + result.astype(F32)).astype(BF)

    down_owned = feed_owned[:, 2 * hidden_units :].reshape(pieces, unit, width // pieces)
    down_owned = down_owned.transpose(1, 0, 2).reshape(unit, width).astype(F32)
    input_grad = input_gradient(
        grad_queries, kv_total.reshape(2 * pair_cols, token_count), gathered, own, grad_resid
    )
    if grid:
        gate_owned, up_owned, gain_two_owned = feed_finish(gate_up_owned, w_gate, w_up, gain_two)
        input_grad, gain_two_owned, *projected = stage(input_grad, gain_two_owned, *projected)
        query_owned, key_owned, value_owned, out_owned, gain_one_owned = attention_finish(
            projected, out_owned, [w_query, key_weight, value_weight], gain_one
        )
    else:
        gate_up_owned = (
            gate_up_owned.astype(F32)
            .reshape(ranks, shard_rows, 2, n, unit)
            .transpose(2, 1, 3, 0, 4)
            .reshape(2, shard_rows, n * ranks * unit)
        )
        gate_owned, up_owned = gate_up_owned[0], gate_up_owned[1]
        gain_two_owned = along(w_gate, gate_owned) + along(w_up, up_owned)
        gate_owned, up_owned = gate_owned * gain_two, up_owned * gain_two
        out_owned, grads = total(out_owned), jnp.split(total(projected), cuts[:2], axis=1)
        weights = (w_query, key_weight, value_weight)
        gain_one_owned = sum(along(weight, grad) for weight, grad in zip(weights, grads))
        query_owned, key_owned, value_owned = (grad * gain_one for grad in grads)
    return (
        result[None],
        input_grad[None],
        gain_one_owned.reshape(-1),
        query_owned,
        key_owned,
        value_owned,
        out_owned,
        gain_two_owned.reshape(-1),
        gate_owned,
        up_owned,
        down_owned,
    )


def solution(mesh):
    n, ranks = mesh.shape["seq"], mesh.shape["fsdp"]
    named = Mesh(mesh.devices, ("z", "f"))
    every = ("z", "f")
    rows, vector, matrix = P("f", "z", None), P(every), P(every, None)
    in_specs = (
        rows,
        vector,
        matrix,
        matrix,
        matrix,
        matrix,
        vector,
        matrix,
        matrix,
        matrix,
        rows,
        P("f", None),
        P("f", None),
    )
    out_specs = (rows, rows, vector) + (matrix,) * 4 + (vector,) + (matrix,) * 3

    def step(*operands):
        return on_device(n, ranks, *operands)

    return jax.shard_map(
        step, mesh=named, in_specs=in_specs, out_specs=out_specs, check_vma=False
    )
```

```python
import math

import jax
import jax.numpy as jnp
from jax import lax
from jax.experimental import pallas as pl
from jax.experimental.pallas import tpu as pltpu
from jax.sharding import Mesh
from jax.sharding import PartitionSpec as P

QUERY_HEADS = 16
KEY_VALUE_HEADS = 8
HEAD_SIZE = 96
FF = 4096
STRETCH = 128

EPSILON = 1e-05
THETA = 100000.0

BF = jnp.bfloat16
F32 = jnp.float32


def layout(doc_lengths, slot_map, slots):
    count = slot_map.shape[0]
    stretches = jnp.arange(count, dtype=jnp.int32)
    logical = jnp.sum(
        jnp.where(slot_map[None, :] == slots[:, None], stretches[None, :], 0), axis=1
    )
    places = (
        logical[:, None] * STRETCH + jnp.arange(STRETCH, dtype=jnp.int32)[None, :]
    ).reshape(-1)
    endings = jnp.cumsum(doc_lengths)
    passed = endings[None, :] <= places[:, None]
    document = jnp.sum(passed.astype(jnp.int32), axis=1)
    starts = jnp.sum(jnp.where(passed, doc_lengths[None, :], 0), axis=1)
    return document, places - starts


def rotary_tables(positions):
    half = HEAD_SIZE // 2
    freqs = THETA ** (-2.0 * jnp.arange(half, dtype=F32) / HEAD_SIZE)
    angles = positions.astype(F32)[:, None] * freqs[None, :]
    return jnp.cos(angles).T, jnp.sin(angles).T


def rotate(rows, cosine, sine):
    half = rows.shape[0] // 2
    first, second = rows[:half], rows[half:]
    return jnp.concatenate(
        [first * cosine - second * sine, second * cosine + first * sine], axis=0
    )


def contract(left, right, at_left, at_right):
    return lax.dot_general(
        left, right, (((at_left,), (at_right,)), ((), ())), preferred_element_type=F32
    )


RATIO = QUERY_HEADS // KEY_VALUE_HEADS
SCALE = 1.0 / math.sqrt(HEAD_SIZE)
VMEM_BYTES = 40 * 1024 * 1024
MOST_VMEM_BYTES = 60 * 1024 * 1024


def lasting(microseconds):
    return pl.CostEstimate(
        flops=int(microseconds * 1e9), bytes_accessed=int(microseconds * 3e6), transcendentals=0
    )


def forward_kernel(q_ref, k_ref, v_ref, bias_ref, out_ref, lse_ref):
    keys, values = k_ref[...], v_ref[...]
    for head in range(RATIO):
        rows = slice(head * HEAD_SIZE, (head + 1) * HEAD_SIZE)
        scores = contract(keys, q_ref[rows, :], 0, 0) * SCALE + bias_ref[...]
        peak = jnp.max(scores, axis=0, keepdims=True)
        weights = jnp.exp(scores - peak)
        totals = jnp.sum(weights, axis=0, keepdims=True)
        mixed = contract(values, weights.astype(BF), 1, 0)
        out_ref[rows, :] = (mixed / totals).astype(BF)
        lse_ref[0, head : head + 1, :] = peak + jnp.log(totals)


def backward_kernel(
    place_ref,
    q_ref,
    k_ref,
    v_ref,
    grad_ref,
    lse_ref,
    cos_ref,
    sin_ref,
    bias_ref,
    token_ref,
    dq_ref,
    dkv_ref,
    block_ref,
):
    count = q_ref.shape[1]
    keys, values = k_ref[...], v_ref[...]
    cosine, sine = cos_ref[:, :count], sin_ref[:, :count]
    grad_keys = jnp.zeros(keys.shape, F32)
    grad_values = jnp.zeros(keys.shape, F32)
    for head in range(RATIO):
        rows = slice(head * HEAD_SIZE, (head + 1) * HEAD_SIZE)
        queries, grads = q_ref[rows, :], grad_ref[rows, :]
        scores = contract(keys, queries, 0, 0) * SCALE + bias_ref[...]
        probs = jnp.exp(scores - lse_ref[0, head : head + 1, :])
        grad_probs = contract(values, grads, 0, 0)
        centre = jnp.sum(probs * grad_probs, axis=0, keepdims=True)
        grad_scores = (probs * (grad_probs - centre)).astype(BF)
        grad_queries = contract(keys, grad_scores, 1, 0) * SCALE
        dq_ref[rows, :] = rotate(grad_queries, cosine, -sine).astype(BF)
        grad_keys += contract(queries, grad_scores, 1, 1)
        grad_values += contract(grads, probs.astype(BF), 1, 1)
    grad_keys = rotate(grad_keys * SCALE, cos_ref[...], -sin_ref[...]).astype(BF)
    grad_values = grad_values.astype(BF)
    dkv_ref[0] = grad_keys
    dkv_ref[1] = grad_values
    blocks = block_ref.shape[0]
    for block in range(blocks):
        at = slice(block * count, (block + 1) * count)
        place = lax.rem(place_ref[0] - block + blocks, blocks)
        block_ref[place, 0] = grad_keys[:, at]
        block_ref[place, 1] = grad_values[:, at]


def attention_forward(queries, keys, values, bias):
    count, span = queries.shape[1], keys.shape[1]
    pair = RATIO * HEAD_SIZE
    mine = lambda rows, cols: pl.BlockSpec((rows, cols), lambda g: (g, 0))
    return pl.pallas_call(
        forward_kernel,
        grid=(KEY_VALUE_HEADS,),
        in_specs=[
            mine(pair, count),
            mine(HEAD_SIZE, span),
            mine(HEAD_SIZE, span),
            pl.BlockSpec(bias.shape, lambda g: (0, 0)),
        ],
        out_specs=[
            mine(pair, count),
            pl.BlockSpec((1, RATIO, count), lambda g: (g, 0, 0)),
        ],
        out_shape=[
            jax.ShapeDtypeStruct(queries.shape, BF),
            jax.ShapeDtypeStruct((KEY_VALUE_HEADS, RATIO, count), F32),
        ],
        compiler_params=pltpu.CompilerParams(vmem_limit_bytes=MOST_VMEM_BYTES),
        cost_estimate=lasting(0.1),
        name="attention_forward",
    )(queries, keys, values, bias)


def attention_backward(place, heads, queries, keys, values, grads, totals, cosine, sine, bias, token, blocks):
    count, span = queries.shape[1], keys.shape[1]
    pair = RATIO * HEAD_SIZE
    first, amount = heads.start, len(heads)
    whole = lambda a: pl.BlockSpec(a.shape, lambda g: (0,) * a.ndim)
    mine = lambda rows, cols: pl.BlockSpec((rows, cols), lambda g: (g + first, 0))
    rows = amount * HEAD_SIZE
    return pl.pallas_call(
        backward_kernel,
        grid=(amount,),
        in_specs=[
            pl.BlockSpec(memory_space=pltpu.SMEM),
            mine(pair, count),
            mine(HEAD_SIZE, span),
            mine(HEAD_SIZE, span),
            mine(pair, count),
            pl.BlockSpec((1, RATIO, count), lambda g: (g + first, 0, 0)),
            whole(cosine),
            whole(sine),
            whole(bias),
            whole(token),
        ],
        out_specs=[
            pl.BlockSpec((pair, count), lambda g: (g, 0)),
            pl.BlockSpec((2, HEAD_SIZE, span), lambda g: (0, g, 0)),
            pl.BlockSpec((blocks, 2, HEAD_SIZE, count), lambda g: (0, 0, g, 0)),
        ],
        out_shape=[
            jax.ShapeDtypeStruct((amount * pair, count), BF),
            jax.ShapeDtypeStruct((2, rows, span), BF),
            jax.ShapeDtypeStruct((blocks, 2, rows, count), BF),
        ],
        compiler_params=pltpu.CompilerParams(vmem_limit_bytes=VMEM_BYTES),
        cost_estimate=lasting(0.1),
        name="attention_backward",
    )(place, queries, keys, values, grads, totals, cosine, sine, bias, token)


def product(left, right):
    return jnp.dot(left, right, preferred_element_type=F32)


def over_rows(left, right):
    return lax.dot_general(left, right, (((0,), (0,)), ((), ())), preferred_element_type=F32)


def times_transposed(left, right):
    return lax.dot_general(left, right, (((1,), (1,)), ((), ())), preferred_element_type=F32)


def blank(shape, dtype):
    return pl.pallas_call(
        lambda out_ref: None,
        out_shape=jax.ShapeDtypeStruct(shape, dtype),
        out_specs=pl.BlockSpec(memory_space=pl.ANY),
        name="blank",
    )()


def terms_kernel(steps, by_rows, owners_ref, left_ref, *refs):
    rights, (away_ref, mine_ref, total_ref) = refs[:-3], refs[-3:]
    step = pl.program_id(0)
    slots, n, rows, cols = away_ref.shape
    for right_ref, (first, last) in zip(rights, steps):

        @pl.when((step >= first) & (step < last))
        def _(right_ref=right_ref):
            if by_rows:
                right = right_ref[...]
                product = contract(left_ref[:, : right.shape[1]], right, 1, 1)
            else:
                product = contract(left_ref[...], right_ref[...], 1, 0)
            total_ref[...] = product.astype(BF)

    for slot in range(slots):
        for z in range(n):
            base = z * 2 * slots * rows
            for out_ref, at in ((mine_ref, slot), (away_ref, slots + slot)):
                start = pl.multiple_of(base + owners_ref[at] * rows, 16)
                out_ref[slot, z] = total_ref[pl.ds(start, rows), :]


def owned_terms(owners, n, left, rights, by_rows):
    tile = 256
    depth = left.shape[0] // (8 * n)
    steps, first = [], 0
    for right in rights:
        last = first + right.shape[0 if by_rows else 1] // tile
        steps.append((first, last))
        first = last
    specs = []
    for right, (start, stop) in zip(rights, steps):
        if by_rows:
            specs.append(
                pl.BlockSpec(
                    (tile, right.shape[1]),
                    lambda j, o, start=start, stop=stop: (jnp.clip(j, start, stop - 1) - start, 0),
                )
            )
        else:
            specs.append(pl.BlockSpec((right.shape[0], tile), lambda j, o: (0, j)))
    out = jax.ShapeDtypeStruct((4, n, depth, first * tile), BF)
    out_spec = pl.BlockSpec((4, n, depth, tile), lambda j, o: (0, 0, 0, j))
    return pl.pallas_call(
        lambda *refs: terms_kernel(steps, by_rows, *refs),
        grid_spec=pltpu.PrefetchScalarGridSpec(
            num_scalar_prefetch=1,
            grid=(first,),
            in_specs=[pl.BlockSpec(left.shape, lambda j, o: (0, 0))] + specs,
            out_specs=[out_spec, out_spec],
            scratch_shapes=[pltpu.VMEM((left.shape[0], tile), BF)],
        ),
        out_shape=[out, out],
        compiler_params=pltpu.CompilerParams(vmem_limit_bytes=VMEM_BYTES),
        cost_estimate=lasting(0.1),
        name="owned_terms",
    )(owners, left, *rights)


def project_kernel(n, count, starts_ref, *refs):
    parts, blocks, (cos_ref, sin_ref) = refs[:count], refs[count : count + n], refs[count + n : count + n + 2]
    refs = refs[count + n + 2 :]
    q_ref, k_ref, v_ref, normed_ref, weight_out, weight_ref, token_ref, part_sem, token_sem, out_sem = refs
    rows, (count, width) = parts[0].shape[1], blocks[0].shape
    token_copies = [
        pltpu.make_async_copy(block, token_ref.at[pl.ds(k * count, count)], token_sem.at[k])
        for k, block in enumerate(blocks)
    ]
    part_copies = []
    for part in parts:
        for j in range(part.shape[0]):
            k = len(part_copies)
            at = pl.multiple_of(starts_ref[k], 16)
            part_copies.append(
                pltpu.make_async_copy(part.at[j], weight_ref.at[pl.ds(at, rows)], part_sem.at[k])
            )
    for copy in token_copies + part_copies:
        copy.start()
    for k, copy in enumerate(token_copies):
        copy.wait()
        x = token_ref[k * count : (k + 1) * count, :].astype(F32)
        inverse = lax.rsqrt(jnp.mean(x * x, axis=-1, keepdims=True) + EPSILON)
        normed_ref[:, k * count : (k + 1) * count] = (x * inverse).astype(BF).T
    for copy in part_copies:
        copy.wait()
    out_copy = pltpu.make_async_copy(weight_ref, weight_out, out_sem)
    out_copy.start()
    pair_cols = k_ref.shape[0]
    tile = 4 * HEAD_SIZE
    for out_ref, base, rotated in ((q_ref, 0, True), (k_ref, width, True), (v_ref, width + pair_cols, False)):
        tokens = out_ref.shape[1]

        def step(j, carry, out_ref=out_ref, base=base, rotated=rotated, tokens=tokens):
            at = pl.multiple_of(j * tile, tile)
            columns = weight_ref[:, pl.ds(pl.multiple_of(base + at, 128), tile)]
            product = contract(columns, normed_ref[:, :tokens], 0, 0)
            for head in range(4):
                part = product[head * HEAD_SIZE : (head + 1) * HEAD_SIZE]
                if rotated:
                    part = rotate(part, cos_ref[:, :tokens], sin_ref[:, :tokens])
                start = pl.multiple_of(at + head * HEAD_SIZE, 16)
                out_ref[pl.ds(start, HEAD_SIZE), :] = part.astype(BF)
            return carry

        lax.fori_loop(0, out_ref.shape[0] // tile, step, 0)
    out_copy.wait()


def project(starts, parts, blocks, cosine, sine):
    rows, cols = parts[0].shape[1:]
    n, (count, width) = len(blocks), blocks[0].shape
    span, pair_cols = n * count, KEY_VALUE_HEADS * HEAD_SIZE
    every = pl.BlockSpec(memory_space=pl.ANY)
    vmem = pl.BlockSpec(memory_space=pltpu.VMEM)
    shape = (starts.shape[0] * rows, cols)
    return pl.pallas_call(
        lambda *refs: project_kernel(n, len(parts), *refs),
        in_specs=[pl.BlockSpec(memory_space=pltpu.SMEM)] + [every] * (len(parts) + n) + [vmem, vmem],
        out_specs=[vmem, vmem, vmem, vmem, every],
        out_shape=[
            jax.ShapeDtypeStruct((width, count), BF),
            jax.ShapeDtypeStruct((pair_cols, span), BF),
            jax.ShapeDtypeStruct((pair_cols, span), BF),
            jax.ShapeDtypeStruct((width, span), BF),
            jax.ShapeDtypeStruct(shape, BF),
        ],
        scratch_shapes=[
            pltpu.VMEM(shape, BF),
            pltpu.VMEM((span, width), BF),
            pltpu.SemaphoreType.DMA(starts.shape),
            pltpu.SemaphoreType.DMA((n,)),
            pltpu.SemaphoreType.DMA,
        ],
        compiler_params=pltpu.CompilerParams(vmem_limit_bytes=MOST_VMEM_BYTES),
        cost_estimate=lasting(0.1),
        name="project",
    )(starts, *parts, *blocks, cosine, sine)


def feed_kernel(count, *refs):
    parts, grads, blocks_ref = refs[:count], refs[count : 2 * count], refs[2 * count]
    refs = refs[2 * count + 1 :]
    scaled_ref, hidden_ref, both_ref, sum_ref, down_ref = refs[:5]
    total_ref, part_ref, grad_ref, weight_ref, part_sem, grad_sem, block_sem = refs[5:]
    step = pl.program_id(0)
    units = hidden_ref.shape[1]
    (n, rows, _), width = blocks_ref.shape, down_ref.shape[1]
    unit = units // n
    pieces = rows // unit
    piece = width // pieces

    def copies(k):
        return (
            pltpu.make_async_copy(parts[k], part_ref.at[k], part_sem.at[k]),
            pltpu.make_async_copy(grads[k], grad_ref.at[k], grad_sem.at[k]),
        )

    @pl.when(step == 0)
    def _():
        block_copies = [
            pltpu.make_async_copy(
                blocks_ref.at[k, :, : 2 * units],
                weight_ref.at[pl.ds(k * rows, rows)],
                block_sem.at[k * (1 + pieces)],
            )
            for k in range(n)
        ]
        block_copies += [
            pltpu.make_async_copy(
                blocks_ref.at[k, pl.ds(j * unit, unit), 2 * units :],
                down_ref.at[pl.ds(k * unit, unit), j * piece : (j + 1) * piece],
                block_sem.at[k * (1 + pieces) + 1 + j],
            )
            for k in range(n)
            for j in range(pieces)
        ]
        for copy in block_copies:
            copy.start()
        for k in range(count):
            for copy in copies(k):
                copy.start()
        for copy in block_copies:
            copy.wait()
        total_ref[...] = jnp.zeros_like(total_ref)

    for k in range(count):

        @pl.when(step == k)
        def _(k=k):
            for copy in copies(k):
                copy.wait()

    part, grad = part_ref[step], grad_ref[step]
    gate = product(part, weight_ref[:, :units])
    upper = product(part, weight_ref[:, units:])
    sigmoid = jax.nn.sigmoid(gate)
    silu = gate * sigmoid
    hidden = (silu * upper).astype(BF)
    hidden_ref[...] = hidden
    grad_hidden = contract(grad, down_ref[...], 1, 1)
    grad_gate = (grad_hidden * upper * sigmoid * (1.0 + gate * (1.0 - sigmoid))).astype(BF)
    grad_up = (grad_hidden * silu).astype(BF)
    both_ref[:, :units] = grad_gate
    both_ref[:, units:] = grad_up
    scaled = contract(grad_gate, weight_ref[:, :units], 1, 1)
    scaled += contract(grad_up, weight_ref[:, units:], 1, 1)
    scaled_ref[...] = scaled.astype(BF)
    total_ref[...] += contract(hidden, grad, 0, 0)

    @pl.when(step == count - 1)
    def _():
        sum_ref[...] = total_ref[...].astype(BF)


def feed_forward(parts, grads, blocks, units):
    count, n = len(parts), blocks.shape[0]
    rows, width = parts[0].shape
    every = pl.BlockSpec(memory_space=pl.ANY)
    part = lambda cols: pl.BlockSpec((rows, cols), lambda k: (k, 0))
    whole = pl.BlockSpec((units, width), lambda k: (0, 0))
    return pl.pallas_call(
        lambda *refs: feed_kernel(count, *refs),
        grid=(count,),
        in_specs=[every] * (2 * count + 1),
        out_specs=[part(width), part(units), part(2 * units), whole, whole],
        out_shape=[
            jax.ShapeDtypeStruct((count * rows, width), BF),
            jax.ShapeDtypeStruct((count * rows, units), BF),
            jax.ShapeDtypeStruct((count * rows, 2 * units), BF),
            jax.ShapeDtypeStruct((units, width), BF),
            jax.ShapeDtypeStruct((units, width), BF),
        ],
        scratch_shapes=[
            pltpu.VMEM((units, width), F32),
            pltpu.VMEM((count, rows, width), BF),
            pltpu.VMEM((count, rows, width), BF),
            pltpu.VMEM((n * blocks.shape[1], 2 * units), BF),
            pltpu.SemaphoreType.DMA((count,)),
            pltpu.SemaphoreType.DMA((count,)),
            pltpu.SemaphoreType.DMA((n * (1 + blocks.shape[1] * n // units),)),
        ],
        compiler_params=pltpu.CompilerParams(vmem_limit_bytes=MOST_VMEM_BYTES),
        cost_estimate=lasting(30),
        name="feed_forward",
    )(*parts, *grads, blocks)


def add_kernel(a_ref, b_ref, out_ref):
    out_ref[...] = (a_ref[0].astype(F32) + b_ref[0].astype(F32)).astype(BF)


def add_half(a, b, which):
    cols = a.shape[-1]
    both = [x.reshape(2, -1, cols) for x in (a, b)]
    rows = both[0].shape[1]
    tile = rows // 2 if rows % 32 == 0 else rows
    out = pl.pallas_call(
        add_kernel,
        grid=(rows // tile,),
        in_specs=[pl.BlockSpec((1, tile, cols), lambda j: (which, j, 0))] * 2,
        out_specs=pl.BlockSpec((tile, cols), lambda j: (j, 0)),
        out_shape=jax.ShapeDtypeStruct((rows, cols), BF),
        compiler_params=pltpu.CompilerParams(vmem_limit_bytes=VMEM_BYTES),
        cost_estimate=lasting(0.1),
        name="add_half",
    )(*both)
    return out.reshape((a.shape[0] // 2,) + a.shape[1:])


def feed_terms_kernel(count, *refs):
    parts, (far_ref, near_ref, *boths, out_ref, token_ref) = refs[:count], refs[count:]
    token_ref[...] = jnp.zeros_like(token_ref)
    rows, cols = parts[0].shape[0], boths[0].shape[1]
    unit, width = far_ref.shape
    pieces = out_ref.shape[0] // unit
    piece = width // pieces
    each = boths[0].shape[0] // rows
    total = jnp.zeros((out_ref.shape[0], cols), F32)
    for k, part in enumerate(parts):
        at = k % each * rows
        total += contract(part[...], boths[k // each][at : at + rows, :], 0, 0)
    out_ref[:, :cols] = total.astype(BF)
    down = (far_ref[...].astype(F32) + near_ref[...].astype(F32)).astype(BF)
    for j in range(pieces):
        out_ref[j * unit : (j + 1) * unit, cols:] = down[:, j * piece : (j + 1) * piece]


def feed_terms(parts, downs, boths, n):
    rows, width = parts[0].shape
    tile, cols = width // n, boths[0].shape[1]
    unit = downs[0].shape[0] // n
    more = width * unit // tile
    return pl.pallas_call(
        lambda *refs: feed_terms_kernel(len(parts), *refs),
        grid=(n,),
        in_specs=[pl.BlockSpec((rows, tile), lambda j: (0, j))] * len(parts)
        + [pl.BlockSpec((unit, width), lambda j: (j, 0))] * 2
        + [pl.BlockSpec(both.shape, lambda j: (0, 0)) for both in boths],
        out_specs=[
            pl.BlockSpec((tile, cols + more), lambda j: (j, 0)),
            pl.BlockSpec((8, 128), lambda j: (0, 0)),
        ],
        out_shape=[
            jax.ShapeDtypeStruct((width, cols + more), BF),
            jax.ShapeDtypeStruct((8, 128), F32),
        ],
        compiler_params=pltpu.CompilerParams(vmem_limit_bytes=VMEM_BYTES),
        cost_estimate=lasting(15),
        name="feed_terms",
    )(*parts, *downs, *boths)


def feed_finish_kernel(
    arrived_ref, gate_ref, up_ref, gain_ref, gate_out, up_out, gain_out
):
    ranks, rows, cols = arrived_ref.shape
    units = cols // 2
    n = gate_ref.shape[1] // (ranks * 128)
    unit = units // n
    gain = gain_ref[...]
    total = jnp.zeros((rows, unit), F32)
    for r in range(ranks):
        for z in range(n):
            at = slice((z * ranks + r) * unit, (z * ranks + r + 1) * unit)
            for half, weight_ref, out_ref in ((0, gate_ref, gate_out), (units, up_ref, up_out)):
                start = half + z * unit
                grad = arrived_ref[r, :, start : start + unit].astype(F32)
                out_ref[:, at] = grad * gain
                total += grad * weight_ref[:, at].astype(F32)
    gain_out[...] = jnp.sum(total, axis=1, keepdims=True)


def feed_finish(arrived, gate, up, gain):
    return pl.pallas_call(
        feed_finish_kernel,
        out_shape=[
            jax.ShapeDtypeStruct(gate.shape, F32),
            jax.ShapeDtypeStruct(up.shape, F32),
            jax.ShapeDtypeStruct(gain.shape, F32),
        ],
        compiler_params=pltpu.CompilerParams(vmem_limit_bytes=VMEM_BYTES),
        cost_estimate=lasting(0.1),
        name="feed_finish",
    )(arrived, gate, up, gain)


def attention_finish_kernel(n, *refs):
    projected, outs, weights = refs[:n], refs[n : 2 * n], refs[2 * n : 2 * n + 3]
    gain_ref, *grad_refs, out_ref, gain_out = refs[2 * n + 3 :]
    gain = gain_ref[...]
    out_ref[...] = sum(ref[...].astype(F32) for ref in outs)
    first = 0
    total = jnp.zeros(gain.shape, F32)
    for weight_ref, grad_ref in zip(weights, grad_refs):
        at = slice(first, first + weight_ref.shape[1])
        first = at.stop
        grad = sum(ref[:, at].astype(F32) for ref in projected)
        grad_ref[...] = grad * gain
        total += jnp.sum(grad * weight_ref[...].astype(F32), axis=1, keepdims=True)
    gain_out[...] = total


def attention_finish(projected, outs, weights, gain):
    shapes = [weight.shape for weight in weights] + [outs[0].shape, gain.shape]
    return pl.pallas_call(
        lambda *refs: attention_finish_kernel(len(outs), *refs),
        out_shape=[jax.ShapeDtypeStruct(shape, F32) for shape in shapes],
        compiler_params=pltpu.CompilerParams(vmem_limit_bytes=VMEM_BYTES),
        cost_estimate=lasting(0.1),
        name="attention_finish",
    )(*projected, *outs, *weights, gain)


def middle_kernel(near_ref, far_ref, resid_ref, grad_ref, weight_ref, total_ref, round_ref, mixed_ref):
    @pl.when(pl.program_id(0) == 0)
    def _():
        resid = resid_ref[...]
        scaled = near_ref[...].astype(F32) + far_ref[...].astype(F32)
        inverse = lax.rsqrt(jnp.mean(resid * resid, axis=-1, keepdims=True) + EPSILON)
        normed = resid * inverse
        mean = jnp.mean(scaled * normed, axis=-1, keepdims=True)
        total = grad_ref[...].astype(F32) + inverse * (scaled - normed * mean)
        total_ref[...] = total
        round_ref[...] = total.astype(BF)

    mixed_ref[...] = contract(weight_ref[...], round_ref[...], 1, 1).astype(BF)


def middle_gradient(near, far, resid, grad, weight):
    count, width = resid.shape
    tile = 256
    last = weight.shape[1] // width - 1
    whole = pl.BlockSpec((count, width), lambda j: (0, 0))
    return pl.pallas_call(
        middle_kernel,
        grid=(width // tile,),
        in_specs=[whole] * 4 + [pl.BlockSpec((tile, width), lambda j: (j, last))],
        out_specs=[whole, whole, pl.BlockSpec((tile, count), lambda j: (j, 0))],
        out_shape=[
            jax.ShapeDtypeStruct((count, width), F32),
            jax.ShapeDtypeStruct((count, width), BF),
            jax.ShapeDtypeStruct((width, count), BF),
        ],
        compiler_params=pltpu.CompilerParams(vmem_limit_bytes=VMEM_BYTES),
        cost_estimate=lasting(0.1),
        name="middle_gradient",
    )(near, far, resid, grad, weight)


def input_kernel(query_ref, pair_ref, weight_ref, own_ref, resid_ref, out_ref, left_ref, total_ref):
    step = pl.program_id(0)
    queries, tile = query_ref.shape[0], weight_ref.shape[0]

    @pl.when(step == 0)
    def _():
        left_ref[:, :queries] = query_ref[...].T
        left_ref[:, queries:] = pair_ref[...].T

    at = pl.multiple_of(step * tile, tile)
    total_ref[:, pl.ds(at, tile)] = contract(
        left_ref[...], weight_ref[:, : left_ref.shape[1]], 1, 1
    )

    @pl.when(step == pl.num_programs(0) - 1)
    def _():
        x, scaled = own_ref[...].astype(F32), total_ref[...]
        inverse = lax.rsqrt(jnp.mean(x * x, axis=-1, keepdims=True) + EPSILON)
        normed = x * inverse
        mean = jnp.mean(scaled * normed, axis=-1, keepdims=True)
        out_ref[...] = (resid_ref[...] + inverse * (scaled - normed * mean)).astype(BF)


def input_gradient(queries, pairs, weight, own, resid):
    count, width = own.shape
    tile = 256
    whole = lambda a: pl.BlockSpec(a.shape, lambda j: (0, 0))
    features = queries.shape[0] + pairs.shape[0]
    return pl.pallas_call(
        input_kernel,
        grid=(width // tile,),
        in_specs=[
            whole(queries),
            whole(pairs),
            pl.BlockSpec((tile, weight.shape[1]), lambda j: (j, 0)),
            whole(own),
            whole(resid),
        ],
        out_specs=pl.BlockSpec((count, width), lambda j: (0, 0)),
        out_shape=jax.ShapeDtypeStruct((count, width), BF),
        scratch_shapes=[pltpu.VMEM((count, features), BF), pltpu.VMEM((count, width), F32)],
        compiler_params=pltpu.CompilerParams(vmem_limit_bytes=VMEM_BYTES),
        cost_estimate=lasting(0.1),
        name="input_gradient",
    )(queries, pairs, weight, own, resid)


def on_device(n, ranks, *operands):
    (
        tokens,
        gain_attn,
        w_query,
        key_weight,
        value_weight,
        w_out,
        gain_mlp,
        w_gate,
        w_up,
        w_down,
        out_grad,
        lengths,
        stretch_map,
    ) = operands
    at_z, rank = lax.axis_index("z"), lax.axis_index("f")
    grid = ranks == 8 and w_down.shape[0] % 128 == 0
    turn = rank % 2
    first, second = 4 >> turn, 2 << turn
    scope = jax.named_scope

    def stage(*arrays):
        return lax.optimization_barrier(arrays)

    def shift(a, by):
        return lax.ppermute(a, "z", [(i, (i + by) % n) for i in range(n)])

    def swap_first(a):
        return lax.ppermute(a, "f", [(i, i ^ (4 >> i % 2)) for i in range(ranks)])

    def swap_second(a):
        return lax.ppermute(a, "f", [(i, i ^ (2 << i % 2)) for i in range(ranks)])

    def swap_core(a):
        return lax.ppermute(a, "f", [(i, i ^ 1) for i in range(ranks)])

    def pick(a, index, axis):
        return lax.dynamic_index_in_dim(a, index, axis, keepdims=False)

    def put(a, piece, *index):
        index = index + (0,) * (a.ndim - len(index))
        return lax.dynamic_update_slice(a, piece, index)

    def direct(a):
        return [a] + [shift(a, by) for by in range(1, n)]

    def stack_z(blocks):
        out = blank((n,) + blocks[0].shape, BF)
        for k, block in enumerate(blocks):
            out = put(out, block[None], (at_z - k) % n)
        return out

    def send_z(terms):
        sent = [shift(pick(terms, (at_z - by) % n, 0), -by) for by in range(1, n)]
        return [pick(terms, at_z, 0)] + sent

    def total(terms):
        return sum(term.astype(F32) for term in terms)

    def add(a, b):
        return (a.astype(F32) + b.astype(F32)).astype(BF)

    def spread_second(pair):
        return swap_second(pair) if grid else pair

    def spread_all(pair, other):
        if grid:
            return [pair, other, swap_core(pair), swap_core(other)]
        rows = lax.all_gather(pair, "f", tiled=True)
        return jnp.split(rows, rows.shape[0] // (2 * pair.shape[0]))

    def send_core(terms):
        return swap_core(terms) if grid else terms

    def add_halves(terms, arrived):
        return add_half(terms, arrived, 0), add_half(terms, arrived, 1)

    if grid:
        owners = [rank, rank ^ first, rank ^ second, rank ^ 6]
        owners += [rank ^ 1, rank ^ 1 ^ second, rank ^ 1 ^ first, rank ^ 7]
        owners = jnp.stack(owners).astype(jnp.int32)

    def weight_terms(left, rights, by_rows):
        if grid:
            return owned_terms(owners, n, left, rights, by_rows)
        columns = [
            contract(left[:, : r.shape[1]], r, 1, 1) if by_rows else product(left, r)
            for r in rights
        ]
        terms = jnp.concatenate(columns, axis=1).astype(BF)
        return terms, terms

    def sum_f(mine):
        terms = mine.reshape(n, ranks, -1, mine.shape[1]).transpose(1, 0, 2, 3)
        return lax.psum_scatter(terms, "f", scatter_dimension=0, tiled=False)

    token_count, width = tokens.shape[1:]
    shard_rows = w_query.shape[0]
    unit = w_down.shape[0]
    hidden_units = n * unit
    pair_cols = KEY_VALUE_HEADS * HEAD_SIZE
    gain_one = gain_attn.astype(F32)[:, None]
    gain_two = gain_mlp.astype(F32)[:, None]

    def along(weight, grad):
        return jnp.sum(weight.astype(F32) * grad, axis=1)

    slots_each = stretch_map.shape[1] // n
    slots = (
        ((at_z - jnp.arange(n, dtype=jnp.int32)) % n)[:, None] * slots_each
        + jnp.arange(slots_each, dtype=jnp.int32)[None, :]
    ).reshape(-1)
    doc_all, place_all = layout(lengths[0], stretch_map[0], slots)
    allowed = (doc_all[:, None] == doc_all[None, :token_count]) & (
        place_all[:, None] <= place_all[None, :token_count]
    )
    bias = jnp.where(allowed, 0.0, -1e30).astype(F32)
    cosine, sine = rotary_tables(place_all)

    def scaled(weight, gain):
        return (weight.astype(F32) * gain).astype(BF)

    shard = jnp.concatenate([w_query, key_weight, value_weight], axis=1)
    shard = jnp.concatenate([scaled(shard, gain_one), w_out], axis=1)
    own = tokens[0]
    blocks = [own]
    gate_up = scaled(jnp.concatenate([w_gate, w_up], axis=1), gain_two)
    gate_up = gate_up.reshape(shard_rows, 2, n, ranks, unit).transpose(3, 0, 1, 2, 4)
    gate_up = gate_up.reshape(ranks, shard_rows, 2 * hidden_units)
    with scope("gate_up_f"):
        gate_up = lax.all_to_all(gate_up, "f", 0, 0, tiled=True)
    gate_up_rows = ranks * shard_rows
    pieces = gate_up_rows // unit
    grad_own = grad_first = out_grad[0]

    def beside_down(gate_up):
        gate_up = gate_up.reshape(gate_up_rows, 2 * hidden_units)
        down = w_down.reshape(unit, pieces, width // pieces).transpose(1, 0, 2)
        return jnp.concatenate([gate_up, down.reshape(gate_up_rows, width // pieces)], axis=1)

    if grid:
        with scope("attention_weights_z"):
            behind = [shift(shard, 1)]
            while len(behind) < n - 1:
                behind.append(shift(behind[-1], 1))
        with scope("attention_weights_own"):
            near = [shard, swap_first(shard), swap_second(shard)]
            near.append(swap_second(near[1]))
        with scope("tokens_z"):
            blocks.append(shift(own, 1))
        with scope("out_grad_first"):
            grad_first = swap_first(grad_own)
        *behind, near[2], near[3], gate_up, blocks[1], grad_first = stage(
            *behind, near[2], near[3], gate_up, blocks[1], grad_first
        )
        gate_up_down = beside_down(gate_up)
        with scope("attention_weights_core"):
            near_core = [swap_core(part) for part in near]
        rest = [jnp.stack(behind)]
        with scope("attention_weights_first"):
            rest.append(swap_first(rest[0]))
        with scope("attention_weights_second"):
            rest.append(swap_second(rest[0]))
        with scope("tokens_z"):
            blocks.append(shift(blocks[1], 1))
        rest[1], rest[2], blocks[2], cosine, sine, bias, gate_up_down, *near_core = stage(
            rest[1], rest[2], blocks[2], cosine, sine, bias, gate_up_down, *near_core
        )
        with scope("attention_weights_core"):
            rest_core = [swap_core(part) for part in rest]
        with scope("attention_weights_second"):
            rest.append(swap_second(rest[1]))
        with scope("tokens_z"):
            while len(blocks) < n:
                blocks.append(shift(blocks[-1], 1))
        gate_up_down, blocks[-1] = stage(gate_up_down, blocks[-1])
        rest[3], blocks[-1], *rest_core = stage(rest[3], blocks[-1], *rest_core)
        with scope("attention_weights_core"):
            rest_core.append(swap_core(rest[3]))
    else:
        gate_up_down = beside_down(gate_up)
        while len(blocks) < n:
            blocks.append(shift(blocks[-1], 1))
    with scope("gate_up_down_z"):
        gate_up_down = lax.all_gather(gate_up_down, "z")
    cuts = [width, width + pair_cols, width + 2 * pair_cols]

    inputs = own.astype(F32)
    if grid:
        parts, starts = [], []
        for near_parts, rest_parts, moves in (
            (near, rest, (0, first, second, 6)),
            (near_core, rest_core, (1, 1 ^ second, 1 ^ first, 7)),
        ):
            for near_part, rest_part, move in zip(near_parts, rest_parts, moves):
                parts += [near_part[None], rest_part]
                starts += [(at_z - k) % n * ranks + (rank ^ move) for k in range(n)]
        starts = jnp.stack(starts).astype(jnp.int32) * shard_rows
        queries, keys, values, normed_group, gathered = project(
            starts, parts, blocks, cosine, sine
        )
        q_weight, key_matrix, value_matrix, out_weight = jnp.split(gathered, cuts, axis=1)
    else:
        gathered = lax.all_gather(shard, ("z", "f"), tiled=True)
        q_weight, key_matrix, value_matrix, out_weight = jnp.split(gathered, cuts, axis=1)
        normed_group = jnp.concatenate(blocks, axis=0).astype(F32)
        inverse = lax.rsqrt(jnp.mean(normed_group * normed_group, axis=-1, keepdims=True) + EPSILON)
        normed_group = (normed_group * inverse).astype(BF).T

        def rotated(weight, tokens):
            rows = contract(weight, normed_group[:, :tokens], 0, 0)
            rows = rows.reshape(-1, HEAD_SIZE, tokens)
            turned = [rotate(r, cosine[:, :tokens], sine[:, :tokens]) for r in rows]
            return jnp.concatenate(turned, axis=0).astype(BF)

        queries, keys = rotated(q_weight, token_count), rotated(key_matrix, n * token_count)
        values = contract(value_matrix, normed_group, 0, 0).astype(BF)
    span = n * token_count

    queries, grad_first = stage(queries, grad_first)
    with scope("out_grad_second"):
        grad_pair = jnp.concatenate([grad_own, grad_first], axis=0) if grid else grad_own
        grad_other = spread_second(grad_pair)

    attention_output, log_totals = attention_forward(queries, keys, values, bias)
    resid = inputs + contract(attention_output, out_weight, 0, 0)
    second_inverse = lax.rsqrt(jnp.mean(resid * resid, axis=-1, keepdims=True) + EPSILON)
    second_normed = resid * second_inverse
    normed_two = second_normed.astype(BF)
    normed_two, grad_other = stage(normed_two, grad_other)

    with scope("normed_first"):
        normed_first = swap_first(normed_two) if grid else normed_two
    with scope("out_grad_all"):
        grad_parts = spread_all(grad_pair, grad_other)
    with scope("normed_second"):
        (normed_first,) = stage(normed_first)
        normed_pair = normed_first
        if grid:
            normed_pair = jnp.concatenate([normed_two, normed_first], axis=0)
        normed_other = spread_second(normed_pair)
        normed_other, gate_up_down = stage(normed_other, gate_up_down)
        normed_parts = spread_all(normed_pair, normed_other)
    half = len(normed_parts) // 2

    scaled_far, hidden_far, both_far, down_far, down_weight = feed_forward(
        normed_parts[half:], grad_parts[half:], gate_up_down, hidden_units
    )
    with scope("scaled_core"):
        scaled_far = send_core(scaled_far)
    scaled_near, hidden_near, both_near, down_near, _ = feed_forward(
        normed_parts[:half], grad_parts[:half], gate_up_down, hidden_units
    )
    with scope("scaled_second"):
        if grid:
            scaled_near, far = add_halves(scaled_near, scaled_far)
            far, both_near = stage(far, both_near)
            far = swap_second(far)
        else:
            scaled_two = jnp.concatenate([scaled_near, scaled_far], axis=0)
            scaled_two = lax.psum_scatter(scaled_two, "f", scatter_dimension=0, tiled=True)
            scaled_two = far = scaled_two.astype(F32)
    with scope("feed_sum_z"):
        if grid:
            terms, token = feed_terms(normed_parts, [down_far, down_near], [both_near, both_far], n)
        else:
            terms = over_rows(
                jnp.concatenate(normed_parts, axis=0),
                jnp.concatenate([both_near, both_far], axis=0),
            ).astype(BF)
            down_terms = add(down_far, down_near).reshape(n, unit, pieces, width // pieces)
            down_terms = down_terms.transpose(0, 2, 1, 3).reshape(width, width // pieces)
            terms = jnp.concatenate([terms, down_terms], axis=1)
            token = jnp.zeros((8, 128), F32)
        feed_owned = lax.psum_scatter(terms, "z", scatter_dimension=0, tiled=True)
    far, token = stage(far, token)
    if grid:
        with scope("scaled_first"):
            scaled_near, far = add_halves(scaled_near, far)
            far = swap_first(far)
    if grid:
        (far,) = stage(far)
    else:
        far, scaled_near = scaled_two.astype(BF), jnp.zeros_like(scaled_two, BF)
    grad_resid, grad_attn_out, grad_mixed = middle_gradient(
        scaled_near, far, resid, out_grad[0], gathered
    )

    with scope("out_core"):
        out_away, out_mine = weight_terms(attention_output, [grad_attn_out], False)
        out_away = send_core(out_away)
    grad_mixed, out_away = stage(grad_mixed, out_away)
    with scope("out_second"):
        if grid:
            out_near, out_far = add_halves(out_mine, out_away)
            out_far = swap_second(out_far)
        else:
            out_near = out_far = sum_f(out_mine)
    grad_queries, grad_kv, by_block = attention_backward(
        at_z.astype(jnp.int32)[None],
        range(KEY_VALUE_HEADS),
        queries,
        keys,
        values,
        grad_mixed,
        log_totals,
        cosine,
        sine,
        bias,
        token,
        n,
    )
    grad_queries, out_far = stage(grad_queries, out_far)

    with scope("kv_grad_z"):
        kv_total = lax.psum_scatter(by_block, "z", scatter_dimension=0, tiled=False)
    with scope("projected_core"):
        away, mine = weight_terms(
            normed_group, [grad_queries, grad_kv.reshape(2 * pair_cols, span)], True
        )
    if grid:
        with scope("out_first"):
            out_near, out_far = add_halves(out_near, out_far)
            out_far = swap_first(out_far)
        away, out_far = stage(away, out_far)
        with scope("projected_core"):
            away = send_core(away)
        away, hidden_far, hidden_near = stage(away, hidden_far, hidden_near)
        with scope("projected_second"):
            near, far = add_halves(mine, away)
            far = swap_second(far)
        out_near = add(out_near[0], out_far[0])
    with scope("result_core"):
        result_far = send_core(product(hidden_far, down_weight).astype(BF))
        result_near = product(hidden_near, down_weight).astype(BF)
    def exchange(owned):
        with scope("gate_up_sum_f"):
            owned = owned[:, : 2 * hidden_units].reshape(ranks, shard_rows, -1)
            return lax.all_to_all(owned, "f", 0, 0, tiled=True)

    if grid:
        result_near, result_far = add_halves(result_near, result_far)
        far, result_far = stage(far, result_far)
        with scope("projected_first"):
            near, far = add_halves(near, far)
            far = swap_first(far)
        with scope("out_z"):
            out_owned = send_z(out_near)
        gate_up_owned = exchange(feed_owned)
        with scope("result_second"):
            result_far = swap_second(result_far)
        far, kv_total, gate_up_owned, result_far, *out_owned = stage(
            far, kv_total, gate_up_owned, result_far, *out_owned
        )
        with scope("result_first"):
            result_near, result_far = add_halves(result_near, result_far)
            result = result_near.astype(F32) + swap_first(result_far).astype(F32)
        near = add(near[0], far[0])
    else:
        near = sum_f(mine)
        gate_up_owned = exchange(feed_owned)
        result = jnp.concatenate([result_near, result_far], axis=0)
        result = lax.psum_scatter(result, "f", scatter_dimension=0, tiled=True)
        with scope("out_z"):
            out_owned = send_z(out_near)
    with scope("projected_z"):
        projected = send_z(near)
    result = (resid + result.astype(F32)).astype(BF)

    down_owned = feed_owned[:, 2 * hidden_units :].reshape(pieces, unit, width // pieces)
    down_owned = down_owned.transpose(1, 0, 2).reshape(unit, width).astype(F32)
    input_grad = input_gradient(
        grad_queries, kv_total.reshape(2 * pair_cols, token_count), gathered, own, grad_resid
    )
    if grid:
        gate_owned, up_owned, gain_two_owned = feed_finish(gate_up_owned, w_gate, w_up, gain_two)
        input_grad, gain_two_owned, down_owned, result, *projected = stage(
            input_grad, gain_two_owned, down_owned, result, *projected
        )
        query_owned, key_owned, value_owned, out_owned, gain_one_owned = attention_finish(
            projected, out_owned, [w_query, key_weight, value_weight], gain_one
        )
    else:
        gate_up_owned = (
            gate_up_owned.astype(F32)
            .reshape(ranks, shard_rows, 2, n, unit)
            .transpose(2, 1, 3, 0, 4)
            .reshape(2, shard_rows, n * ranks * unit)
        )
        gate_owned, up_owned = gate_up_owned[0], gate_up_owned[1]
        gain_two_owned = along(w_gate, gate_owned) + along(w_up, up_owned)
        gate_owned, up_owned = gate_owned * gain_two, up_owned * gain_two
        out_owned, grads = total(out_owned), jnp.split(total(projected), cuts[:2], axis=1)
        weights = (w_query, key_weight, value_weight)
        gain_one_owned = sum(along(weight, grad) for weight, grad in zip(weights, grads))
        query_owned, key_owned, value_owned = (grad * gain_one for grad in grads)
    return (
        result[None],
        input_grad[None],
        gain_one_owned.reshape(-1),
        query_owned,
        key_owned,
        value_owned,
        out_owned,
        gain_two_owned.reshape(-1),
        gate_owned,
        up_owned,
        down_owned,
    )


def solution(mesh):
    n, ranks = mesh.shape["seq"], mesh.shape["fsdp"]
    named = Mesh(mesh.devices, ("z", "f"))
    every = ("z", "f")
    rows, vector, matrix = P("f", "z", None), P(every), P(every, None)
    in_specs = (
        rows,
        vector,
        matrix,
        matrix,
        matrix,
        matrix,
        vector,
        matrix,
        matrix,
        matrix,
        rows,
        P("f", None),
        P("f", None),
    )
    out_specs = (rows, rows, vector) + (matrix,) * 4 + (vector,) + (matrix,) * 3

    def step(*operands):
        return on_device(n, ranks, *operands)

    return jax.shard_map(
        step, mesh=named, in_specs=in_specs, out_specs=out_specs, check_vma=False
    )
```

```python
import math

import jax
import jax.numpy as jnp
from jax import lax
from jax.experimental import pallas as pl
from jax.experimental.pallas import tpu as pltpu
from jax.sharding import Mesh
from jax.sharding import PartitionSpec as P

QUERY_HEADS = 16
KEY_VALUE_HEADS = 8
HEAD_SIZE = 96
FF = 4096
STRETCH = 128

EPSILON = 1e-05
THETA = 100000.0

BF = jnp.bfloat16
F32 = jnp.float32


def layout(doc_lengths, slot_map, slots):
    count = slot_map.shape[0]
    stretches = jnp.arange(count, dtype=jnp.int32)
    logical = jnp.sum(
        jnp.where(slot_map[None, :] == slots[:, None], stretches[None, :], 0), axis=1
    )
    places = (
        logical[:, None] * STRETCH + jnp.arange(STRETCH, dtype=jnp.int32)[None, :]
    ).reshape(-1)
    endings = jnp.cumsum(doc_lengths)
    passed = endings[None, :] <= places[:, None]
    document = jnp.sum(passed.astype(jnp.int32), axis=1)
    starts = jnp.sum(jnp.where(passed, doc_lengths[None, :], 0), axis=1)
    return document, places - starts


def rotary_tables(positions):
    half = HEAD_SIZE // 2
    freqs = THETA ** (-2.0 * jnp.arange(half, dtype=F32) / HEAD_SIZE)
    angles = positions.astype(F32)[:, None] * freqs[None, :]
    return jnp.cos(angles).T, jnp.sin(angles).T


def rotate(rows, cosine, sine):
    half = rows.shape[0] // 2
    first, second = rows[:half], rows[half:]
    return jnp.concatenate(
        [first * cosine - second * sine, second * cosine + first * sine], axis=0
    )


def contract(left, right, at_left, at_right):
    return lax.dot_general(
        left, right, (((at_left,), (at_right,)), ((), ())), preferred_element_type=F32
    )


RATIO = QUERY_HEADS // KEY_VALUE_HEADS
SCALE = 1.0 / math.sqrt(HEAD_SIZE)
VMEM_BYTES = 40 * 1024 * 1024
MOST_VMEM_BYTES = 60 * 1024 * 1024


def lasting(microseconds):
    return pl.CostEstimate(
        flops=int(microseconds * 1e9), bytes_accessed=int(microseconds * 3e6), transcendentals=0
    )


def forward_kernel(q_ref, k_ref, v_ref, bias_ref, out_ref, lse_ref):
    keys, values = k_ref[...], v_ref[...]
    for head in range(RATIO):
        rows = slice(head * HEAD_SIZE, (head + 1) * HEAD_SIZE)
        scores = contract(keys, q_ref[rows, :], 0, 0) * SCALE + bias_ref[...]
        peak = jnp.max(scores, axis=0, keepdims=True)
        weights = jnp.exp(scores - peak)
        totals = jnp.sum(weights, axis=0, keepdims=True)
        mixed = contract(values, weights.astype(BF), 1, 0)
        out_ref[rows, :] = (mixed / totals).astype(BF)
        lse_ref[0, head : head + 1, :] = peak + jnp.log(totals)


def backward_kernel(
    place_ref,
    q_ref,
    k_ref,
    v_ref,
    grad_ref,
    lse_ref,
    cos_ref,
    sin_ref,
    bias_ref,
    token_ref,
    dq_ref,
    dkv_ref,
    block_ref,
):
    count = q_ref.shape[1]
    keys, values = k_ref[...], v_ref[...]
    cosine, sine = cos_ref[:, :count], sin_ref[:, :count]
    grad_keys = jnp.zeros(keys.shape, F32)
    grad_values = jnp.zeros(keys.shape, F32)
    for head in range(RATIO):
        rows = slice(head * HEAD_SIZE, (head + 1) * HEAD_SIZE)
        queries, grads = q_ref[rows, :], grad_ref[rows, :]
        scores = contract(keys, queries, 0, 0) * SCALE + bias_ref[...]
        probs = jnp.exp(scores - lse_ref[0, head : head + 1, :])
        grad_probs = contract(values, grads, 0, 0)
        centre = jnp.sum(probs * grad_probs, axis=0, keepdims=True)
        grad_scores = (probs * (grad_probs - centre)).astype(BF)
        grad_queries = contract(keys, grad_scores, 1, 0) * SCALE
        dq_ref[rows, :] = rotate(grad_queries, cosine, -sine).astype(BF)
        grad_keys += contract(queries, grad_scores, 1, 1)
        grad_values += contract(grads, probs.astype(BF), 1, 1)
    grad_keys = rotate(grad_keys * SCALE, cos_ref[...], -sin_ref[...]).astype(BF)
    grad_values = grad_values.astype(BF)
    dkv_ref[0] = grad_keys
    dkv_ref[1] = grad_values
    blocks = block_ref.shape[0]
    for block in range(blocks):
        at = slice(block * count, (block + 1) * count)
        place = lax.rem(place_ref[0] - block + blocks, blocks)
        block_ref[place, 0] = grad_keys[:, at]
        block_ref[place, 1] = grad_values[:, at]


def attention_forward(queries, keys, values, bias):
    count, span = queries.shape[1], keys.shape[1]
    pair = RATIO * HEAD_SIZE
    mine = lambda rows, cols: pl.BlockSpec((rows, cols), lambda g: (g, 0))
    return pl.pallas_call(
        forward_kernel,
        grid=(KEY_VALUE_HEADS,),
        in_specs=[
            mine(pair, count),
            mine(HEAD_SIZE, span),
            mine(HEAD_SIZE, span),
            pl.BlockSpec(bias.shape, lambda g: (0, 0)),
        ],
        out_specs=[
            mine(pair, count),
            pl.BlockSpec((1, RATIO, count), lambda g: (g, 0, 0)),
        ],
        out_shape=[
            jax.ShapeDtypeStruct(queries.shape, BF),
            jax.ShapeDtypeStruct((KEY_VALUE_HEADS, RATIO, count), F32),
        ],
        compiler_params=pltpu.CompilerParams(vmem_limit_bytes=MOST_VMEM_BYTES),
        cost_estimate=lasting(0.1),
        name="attention_forward",
    )(queries, keys, values, bias)


def attention_backward(place, heads, queries, keys, values, grads, totals, cosine, sine, bias, token, blocks):
    count, span = queries.shape[1], keys.shape[1]
    pair = RATIO * HEAD_SIZE
    first, amount = heads.start, len(heads)
    whole = lambda a: pl.BlockSpec(a.shape, lambda g: (0,) * a.ndim)
    mine = lambda rows, cols: pl.BlockSpec((rows, cols), lambda g: (g + first, 0))
    rows = amount * HEAD_SIZE
    return pl.pallas_call(
        backward_kernel,
        grid=(amount,),
        in_specs=[
            pl.BlockSpec(memory_space=pltpu.SMEM),
            mine(pair, count),
            mine(HEAD_SIZE, span),
            mine(HEAD_SIZE, span),
            mine(pair, count),
            pl.BlockSpec((1, RATIO, count), lambda g: (g + first, 0, 0)),
            whole(cosine),
            whole(sine),
            whole(bias),
            whole(token),
        ],
        out_specs=[
            pl.BlockSpec((pair, count), lambda g: (g, 0)),
            pl.BlockSpec((2, HEAD_SIZE, span), lambda g: (0, g, 0)),
            pl.BlockSpec((blocks, 2, HEAD_SIZE, count), lambda g: (0, 0, g, 0)),
        ],
        out_shape=[
            jax.ShapeDtypeStruct((amount * pair, count), BF),
            jax.ShapeDtypeStruct((2, rows, span), BF),
            jax.ShapeDtypeStruct((blocks, 2, rows, count), BF),
        ],
        compiler_params=pltpu.CompilerParams(vmem_limit_bytes=VMEM_BYTES),
        cost_estimate=lasting(0.1),
        name="attention_backward",
    )(place, queries, keys, values, grads, totals, cosine, sine, bias, token)


def product(left, right):
    return jnp.dot(left, right, preferred_element_type=F32)


def over_rows(left, right):
    return lax.dot_general(left, right, (((0,), (0,)), ((), ())), preferred_element_type=F32)


def times_transposed(left, right):
    return lax.dot_general(left, right, (((1,), (1,)), ((), ())), preferred_element_type=F32)


def blank(shape, dtype):
    return pl.pallas_call(
        lambda out_ref: None,
        out_shape=jax.ShapeDtypeStruct(shape, dtype),
        out_specs=pl.BlockSpec(memory_space=pl.ANY),
        name="blank",
    )()


def terms_kernel(steps, by_rows, owners_ref, left_ref, *refs):
    rights, (away_ref, mine_ref, total_ref) = refs[:-3], refs[-3:]
    step = pl.program_id(0)
    slots, n, rows, cols = away_ref.shape
    for right_ref, (first, last) in zip(rights, steps):

        @pl.when((step >= first) & (step < last))
        def _(right_ref=right_ref):
            if by_rows:
                right = right_ref[...]
                product = contract(left_ref[:, : right.shape[1]], right, 1, 1)
            else:
                product = contract(left_ref[...], right_ref[...], 1, 0)
            total_ref[...] = product.astype(BF)

    for slot in range(slots):
        for z in range(n):
            base = z * 2 * slots * rows
            for out_ref, at in ((mine_ref, slot), (away_ref, slots + slot)):
                start = pl.multiple_of(base + owners_ref[at] * rows, 16)
                out_ref[slot, z] = total_ref[pl.ds(start, rows), :]


def owned_terms(owners, n, left, rights, by_rows):
    tile = 256
    depth = left.shape[0] // (8 * n)
    steps, first = [], 0
    for right in rights:
        last = first + right.shape[0 if by_rows else 1] // tile
        steps.append((first, last))
        first = last
    specs = []
    for right, (start, stop) in zip(rights, steps):
        if by_rows:
            specs.append(
                pl.BlockSpec(
                    (tile, right.shape[1]),
                    lambda j, o, start=start, stop=stop: (jnp.clip(j, start, stop - 1) - start, 0),
                )
            )
        else:
            specs.append(pl.BlockSpec((right.shape[0], tile), lambda j, o: (0, j)))
    out = jax.ShapeDtypeStruct((4, n, depth, first * tile), BF)
    out_spec = pl.BlockSpec((4, n, depth, tile), lambda j, o: (0, 0, 0, j))
    return pl.pallas_call(
        lambda *refs: terms_kernel(steps, by_rows, *refs),
        grid_spec=pltpu.PrefetchScalarGridSpec(
            num_scalar_prefetch=1,
            grid=(first,),
            in_specs=[pl.BlockSpec(left.shape, lambda j, o: (0, 0))] + specs,
            out_specs=[out_spec, out_spec],
            scratch_shapes=[pltpu.VMEM((left.shape[0], tile), BF)],
        ),
        out_shape=[out, out],
        compiler_params=pltpu.CompilerParams(vmem_limit_bytes=VMEM_BYTES),
        cost_estimate=lasting(0.1),
        name="owned_terms",
    )(owners, left, *rights)


def project_kernel(n, count, starts_ref, *refs):
    parts, blocks, (cos_ref, sin_ref) = refs[:count], refs[count : count + n], refs[count + n : count + n + 2]
    refs = refs[count + n + 2 :]
    q_ref, k_ref, v_ref, normed_ref, weight_out, weight_ref, token_ref, part_sem, token_sem, out_sem = refs
    rows, (count, width) = parts[0].shape[1], blocks[0].shape
    token_copies = [
        pltpu.make_async_copy(block, token_ref.at[pl.ds(k * count, count)], token_sem.at[k])
        for k, block in enumerate(blocks)
    ]
    pair_cols = k_ref.shape[0]
    middle, cols = width + 2 * pair_cols, weight_ref.shape[1]
    early, late = [], []
    for part in parts:
        for j in range(part.shape[0]):
            k = len(early)
            at = pl.multiple_of(starts_ref[k], 16)
            for copies, columns, sem in (
                (early, slice(0, middle), part_sem.at[0, k]),
                (late, slice(middle, cols), part_sem.at[1, k]),
            ):
                copies.append(
                    pltpu.make_async_copy(
                        part.at[j, :, columns], weight_ref.at[pl.ds(at, rows), columns], sem
                    )
                )
    for copy in token_copies + early + late:
        copy.start()
    for k, copy in enumerate(token_copies):
        copy.wait()
        x = token_ref[k * count : (k + 1) * count, :].astype(F32)
        inverse = lax.rsqrt(jnp.mean(x * x, axis=-1, keepdims=True) + EPSILON)
        normed_ref[:, k * count : (k + 1) * count] = (x * inverse).astype(BF).T
    for copy in early:
        copy.wait()
    out_copy = pltpu.make_async_copy(weight_ref, weight_out, out_sem)
    tile = 4 * HEAD_SIZE
    for out_ref, base, rotated in ((q_ref, 0, True), (k_ref, width, True), (v_ref, width + pair_cols, False)):
        tokens = out_ref.shape[1]

        def step(j, carry, out_ref=out_ref, base=base, rotated=rotated, tokens=tokens):
            at = pl.multiple_of(j * tile, tile)
            columns = weight_ref[:, pl.ds(pl.multiple_of(base + at, 128), tile)]
            product = contract(columns, normed_ref[:, :tokens], 0, 0)
            for head in range(4):
                part = product[head * HEAD_SIZE : (head + 1) * HEAD_SIZE]
                if rotated:
                    part = rotate(part, cos_ref[:, :tokens], sin_ref[:, :tokens])
                start = pl.multiple_of(at + head * HEAD_SIZE, 16)
                out_ref[pl.ds(start, HEAD_SIZE), :] = part.astype(BF)
            return carry

        lax.fori_loop(0, out_ref.shape[0] // tile, step, 0)
        if out_ref is q_ref:
            for copy in late:
                copy.wait()
            out_copy.start()
    out_copy.wait()


def project(starts, parts, blocks, cosine, sine):
    rows, cols = parts[0].shape[1:]
    n, (count, width) = len(blocks), blocks[0].shape
    span, pair_cols = n * count, KEY_VALUE_HEADS * HEAD_SIZE
    every = pl.BlockSpec(memory_space=pl.ANY)
    vmem = pl.BlockSpec(memory_space=pltpu.VMEM)
    shape = (starts.shape[0] * rows, cols)
    return pl.pallas_call(
        lambda *refs: project_kernel(n, len(parts), *refs),
        in_specs=[pl.BlockSpec(memory_space=pltpu.SMEM)] + [every] * (len(parts) + n) + [vmem, vmem],
        out_specs=[vmem, vmem, vmem, vmem, every],
        out_shape=[
            jax.ShapeDtypeStruct((width, count), BF),
            jax.ShapeDtypeStruct((pair_cols, span), BF),
            jax.ShapeDtypeStruct((pair_cols, span), BF),
            jax.ShapeDtypeStruct((width, span), BF),
            jax.ShapeDtypeStruct(shape, BF),
        ],
        scratch_shapes=[
            pltpu.VMEM(shape, BF),
            pltpu.VMEM((span, width), BF),
            pltpu.SemaphoreType.DMA((2,) + starts.shape),
            pltpu.SemaphoreType.DMA((n,)),
            pltpu.SemaphoreType.DMA,
        ],
        compiler_params=pltpu.CompilerParams(vmem_limit_bytes=MOST_VMEM_BYTES),
        cost_estimate=lasting(0.1),
        name="project",
    )(starts, *parts, *blocks, cosine, sine)


def feed_kernel(count, *refs):
    parts, grads, blocks_ref = refs[:count], refs[count : 2 * count], refs[2 * count]
    refs = refs[2 * count + 1 :]
    scaled_ref, hidden_ref, both_ref, sum_ref, down_ref = refs[:5]
    total_ref, part_ref, grad_ref, weight_ref, part_sem, grad_sem, block_sem = refs[5:]
    step = pl.program_id(0)
    units = hidden_ref.shape[1]
    (n, rows, _), width = blocks_ref.shape, down_ref.shape[1]
    unit = units // n
    pieces = rows // unit
    piece = width // pieces

    def copies(k):
        return (
            pltpu.make_async_copy(parts[k], part_ref.at[k], part_sem.at[k]),
            pltpu.make_async_copy(grads[k], grad_ref.at[k], grad_sem.at[k]),
        )

    @pl.when(step == 0)
    def _():
        block_copies = [
            pltpu.make_async_copy(
                blocks_ref.at[k, :, : 2 * units],
                weight_ref.at[pl.ds(k * rows, rows)],
                block_sem.at[k * (1 + pieces)],
            )
            for k in range(n)
        ]
        block_copies += [
            pltpu.make_async_copy(
                blocks_ref.at[k, pl.ds(j * unit, unit), 2 * units :],
                down_ref.at[pl.ds(k * unit, unit), j * piece : (j + 1) * piece],
                block_sem.at[k * (1 + pieces) + 1 + j],
            )
            for k in range(n)
            for j in range(pieces)
        ]
        for copy in block_copies:
            copy.start()
        for k in range(count):
            for copy in copies(k):
                copy.start()
        for copy in block_copies:
            copy.wait()
        total_ref[...] = jnp.zeros_like(total_ref)

    for k in range(count):

        @pl.when(step == k)
        def _(k=k):
            for copy in copies(k):
                copy.wait()

    part, grad = part_ref[step], grad_ref[step]
    gate = product(part, weight_ref[:, :units])
    upper = product(part, weight_ref[:, units:])
    sigmoid = jax.nn.sigmoid(gate)
    silu = gate * sigmoid
    hidden = (silu * upper).astype(BF)
    hidden_ref[...] = hidden
    grad_hidden = contract(grad, down_ref[...], 1, 1)
    grad_gate = (grad_hidden * upper * sigmoid * (1.0 + gate * (1.0 - sigmoid))).astype(BF)
    grad_up = (grad_hidden * silu).astype(BF)
    both_ref[:, :units] = grad_gate
    both_ref[:, units:] = grad_up
    scaled = contract(grad_gate, weight_ref[:, :units], 1, 1)
    scaled += contract(grad_up, weight_ref[:, units:], 1, 1)
    scaled_ref[...] = scaled.astype(BF)
    total_ref[...] += contract(hidden, grad, 0, 0)

    @pl.when(step == count - 1)
    def _():
        sum_ref[...] = total_ref[...].astype(BF)


def feed_forward(parts, grads, blocks, units):
    count, n = len(parts), blocks.shape[0]
    rows, width = parts[0].shape
    every = pl.BlockSpec(memory_space=pl.ANY)
    part = lambda cols: pl.BlockSpec((rows, cols), lambda k: (k, 0))
    whole = pl.BlockSpec((units, width), lambda k: (0, 0))
    return pl.pallas_call(
        lambda *refs: feed_kernel(count, *refs),
        grid=(count,),
        in_specs=[every] * (2 * count + 1),
        out_specs=[part(width), part(units), part(2 * units), whole, whole],
        out_shape=[
            jax.ShapeDtypeStruct((count * rows, width), BF),
            jax.ShapeDtypeStruct((count * rows, units), BF),
            jax.ShapeDtypeStruct((count * rows, 2 * units), BF),
            jax.ShapeDtypeStruct((units, width), BF),
            jax.ShapeDtypeStruct((units, width), BF),
        ],
        scratch_shapes=[
            pltpu.VMEM((units, width), F32),
            pltpu.VMEM((count, rows, width), BF),
            pltpu.VMEM((count, rows, width), BF),
            pltpu.VMEM((n * blocks.shape[1], 2 * units), BF),
            pltpu.SemaphoreType.DMA((count,)),
            pltpu.SemaphoreType.DMA((count,)),
            pltpu.SemaphoreType.DMA((n * (1 + blocks.shape[1] * n // units),)),
        ],
        compiler_params=pltpu.CompilerParams(vmem_limit_bytes=MOST_VMEM_BYTES),
        cost_estimate=lasting(30),
        name="feed_forward",
    )(*parts, *grads, blocks)


def add_kernel(a_ref, b_ref, out_ref):
    out_ref[...] = (a_ref[0].astype(F32) + b_ref[0].astype(F32)).astype(BF)


def add_half(a, b, which):
    cols = a.shape[-1]
    both = [x.reshape(2, -1, cols) for x in (a, b)]
    rows = both[0].shape[1]
    tile = rows // 2 if rows % 32 == 0 else rows
    out = pl.pallas_call(
        add_kernel,
        grid=(rows // tile,),
        in_specs=[pl.BlockSpec((1, tile, cols), lambda j: (which, j, 0))] * 2,
        out_specs=pl.BlockSpec((tile, cols), lambda j: (j, 0)),
        out_shape=jax.ShapeDtypeStruct((rows, cols), BF),
        compiler_params=pltpu.CompilerParams(vmem_limit_bytes=VMEM_BYTES),
        cost_estimate=lasting(0.1),
        name="add_half",
    )(*both)
    return out.reshape((a.shape[0] // 2,) + a.shape[1:])


def feed_terms_kernel(count, *refs):
    parts, (far_ref, near_ref, *boths, out_ref, token_ref) = refs[:count], refs[count:]
    token_ref[...] = jnp.zeros_like(token_ref)
    rows, cols = parts[0].shape[0], boths[0].shape[1]
    unit, width = far_ref.shape
    pieces = out_ref.shape[0] // unit
    piece = width // pieces
    each = boths[0].shape[0] // rows
    total = jnp.zeros((out_ref.shape[0], cols), F32)
    for k, part in enumerate(parts):
        at = k % each * rows
        total += contract(part[...], boths[k // each][at : at + rows, :], 0, 0)
    out_ref[:, :cols] = total.astype(BF)
    down = (far_ref[...].astype(F32) + near_ref[...].astype(F32)).astype(BF)
    for j in range(pieces):
        out_ref[j * unit : (j + 1) * unit, cols:] = down[:, j * piece : (j + 1) * piece]


def feed_terms(parts, downs, boths, n):
    rows, width = parts[0].shape
    tile, cols = width // n, boths[0].shape[1]
    unit = downs[0].shape[0] // n
    more = width * unit // tile
    return pl.pallas_call(
        lambda *refs: feed_terms_kernel(len(parts), *refs),
        grid=(n,),
        in_specs=[pl.BlockSpec((rows, tile), lambda j: (0, j))] * len(parts)
        + [pl.BlockSpec((unit, width), lambda j: (j, 0))] * 2
        + [pl.BlockSpec(both.shape, lambda j: (0, 0)) for both in boths],
        out_specs=[
            pl.BlockSpec((tile, cols + more), lambda j: (j, 0)),
            pl.BlockSpec((8, 128), lambda j: (0, 0)),
        ],
        out_shape=[
            jax.ShapeDtypeStruct((width, cols + more), BF),
            jax.ShapeDtypeStruct((8, 128), F32),
        ],
        compiler_params=pltpu.CompilerParams(vmem_limit_bytes=VMEM_BYTES),
        cost_estimate=lasting(15),
        name="feed_terms",
    )(*parts, *downs, *boths)


def feed_finish_kernel(
    arrived_ref, gate_ref, up_ref, gain_ref, gate_out, up_out, gain_out
):
    ranks, rows, cols = arrived_ref.shape
    units = cols // 2
    n = gate_ref.shape[1] // (ranks * 128)
    unit = units // n
    gain = gain_ref[...]
    total = jnp.zeros((rows, unit), F32)
    for r in range(ranks):
        for z in range(n):
            at = slice((z * ranks + r) * unit, (z * ranks + r + 1) * unit)
            for half, weight_ref, out_ref in ((0, gate_ref, gate_out), (units, up_ref, up_out)):
                start = half + z * unit
                grad = arrived_ref[r, :, start : start + unit].astype(F32)
                out_ref[:, at] = grad * gain
                total += grad * weight_ref[:, at].astype(F32)
    gain_out[...] = jnp.sum(total, axis=1, keepdims=True)


def feed_finish(arrived, gate, up, gain):
    return pl.pallas_call(
        feed_finish_kernel,
        out_shape=[
            jax.ShapeDtypeStruct(gate.shape, F32),
            jax.ShapeDtypeStruct(up.shape, F32),
            jax.ShapeDtypeStruct(gain.shape, F32),
        ],
        compiler_params=pltpu.CompilerParams(vmem_limit_bytes=VMEM_BYTES),
        cost_estimate=lasting(0.1),
        name="feed_finish",
    )(arrived, gate, up, gain)


def attention_finish_kernel(n, *refs):
    projected, outs, weights = refs[:n], refs[n : 2 * n], refs[2 * n : 2 * n + 3]
    gain_ref, *grad_refs, out_ref, gain_out = refs[2 * n + 3 :]
    gain = gain_ref[...]
    out_ref[...] = sum(ref[...].astype(F32) for ref in outs)
    first = 0
    total = jnp.zeros(gain.shape, F32)
    for weight_ref, grad_ref in zip(weights, grad_refs):
        at = slice(first, first + weight_ref.shape[1])
        first = at.stop
        grad = sum(ref[:, at].astype(F32) for ref in projected)
        grad_ref[...] = grad * gain
        total += jnp.sum(grad * weight_ref[...].astype(F32), axis=1, keepdims=True)
    gain_out[...] = total


def attention_finish(projected, outs, weights, gain):
    shapes = [weight.shape for weight in weights] + [outs[0].shape, gain.shape]
    return pl.pallas_call(
        lambda *refs: attention_finish_kernel(len(outs), *refs),
        out_shape=[jax.ShapeDtypeStruct(shape, F32) for shape in shapes],
        compiler_params=pltpu.CompilerParams(vmem_limit_bytes=VMEM_BYTES),
        cost_estimate=lasting(0.1),
        name="attention_finish",
    )(*projected, *outs, *weights, gain)


def middle_kernel(near_ref, far_ref, resid_ref, grad_ref, weight_ref, total_ref, round_ref, mixed_ref):
    @pl.when(pl.program_id(0) == 0)
    def _():
        resid = resid_ref[...]
        scaled = near_ref[...].astype(F32) + far_ref[...].astype(F32)
        inverse = lax.rsqrt(jnp.mean(resid * resid, axis=-1, keepdims=True) + EPSILON)
        normed = resid * inverse
        mean = jnp.mean(scaled * normed, axis=-1, keepdims=True)
        total = grad_ref[...].astype(F32) + inverse * (scaled - normed * mean)
        total_ref[...] = total
        round_ref[...] = total.astype(BF)

    mixed_ref[...] = contract(weight_ref[...], round_ref[...], 1, 1).astype(BF)


def middle_gradient(near, far, resid, grad, weight):
    count, width = resid.shape
    tile = 256
    last = weight.shape[1] // width - 1
    whole = pl.BlockSpec((count, width), lambda j: (0, 0))
    return pl.pallas_call(
        middle_kernel,
        grid=(width // tile,),
        in_specs=[whole] * 4 + [pl.BlockSpec((tile, width), lambda j: (j, last))],
        out_specs=[whole, whole, pl.BlockSpec((tile, count), lambda j: (j, 0))],
        out_shape=[
            jax.ShapeDtypeStruct((count, width), F32),
            jax.ShapeDtypeStruct((count, width), BF),
            jax.ShapeDtypeStruct((width, count), BF),
        ],
        compiler_params=pltpu.CompilerParams(vmem_limit_bytes=VMEM_BYTES),
        cost_estimate=lasting(0.1),
        name="middle_gradient",
    )(near, far, resid, grad, weight)


def input_kernel(query_ref, pair_ref, weight_ref, own_ref, resid_ref, out_ref, left_ref, total_ref):
    step = pl.program_id(0)
    queries, tile = query_ref.shape[0], weight_ref.shape[0]

    @pl.when(step == 0)
    def _():
        left_ref[:, :queries] = query_ref[...].T
        left_ref[:, queries:] = pair_ref[...].T

    at = pl.multiple_of(step * tile, tile)
    total_ref[:, pl.ds(at, tile)] = contract(
        left_ref[...], weight_ref[:, : left_ref.shape[1]], 1, 1
    )

    @pl.when(step == pl.num_programs(0) - 1)
    def _():
        x, scaled = own_ref[...].astype(F32), total_ref[...]
        inverse = lax.rsqrt(jnp.mean(x * x, axis=-1, keepdims=True) + EPSILON)
        normed = x * inverse
        mean = jnp.mean(scaled * normed, axis=-1, keepdims=True)
        out_ref[...] = (resid_ref[...] + inverse * (scaled - normed * mean)).astype(BF)


def input_gradient(queries, pairs, weight, own, resid):
    count, width = own.shape
    tile = 256
    whole = lambda a: pl.BlockSpec(a.shape, lambda j: (0, 0))
    features = queries.shape[0] + pairs.shape[0]
    return pl.pallas_call(
        input_kernel,
        grid=(width // tile,),
        in_specs=[
            whole(queries),
            whole(pairs),
            pl.BlockSpec((tile, weight.shape[1]), lambda j: (j, 0)),
            whole(own),
            whole(resid),
        ],
        out_specs=pl.BlockSpec((count, width), lambda j: (0, 0)),
        out_shape=jax.ShapeDtypeStruct((count, width), BF),
        scratch_shapes=[pltpu.VMEM((count, features), BF), pltpu.VMEM((count, width), F32)],
        compiler_params=pltpu.CompilerParams(vmem_limit_bytes=VMEM_BYTES),
        cost_estimate=lasting(0.1),
        name="input_gradient",
    )(queries, pairs, weight, own, resid)


def on_device(n, ranks, *operands):
    (
        tokens,
        gain_attn,
        w_query,
        key_weight,
        value_weight,
        w_out,
        gain_mlp,
        w_gate,
        w_up,
        w_down,
        out_grad,
        lengths,
        stretch_map,
    ) = operands
    at_z, rank = lax.axis_index("z"), lax.axis_index("f")
    grid = ranks == 8 and w_down.shape[0] % 128 == 0
    turn = rank % 2
    first, second = 4 >> turn, 2 << turn
    scope = jax.named_scope

    def stage(*arrays):
        return lax.optimization_barrier(arrays)

    def shift(a, by):
        return lax.ppermute(a, "z", [(i, (i + by) % n) for i in range(n)])

    def swap_first(a):
        return lax.ppermute(a, "f", [(i, i ^ (4 >> i % 2)) for i in range(ranks)])

    def swap_second(a):
        return lax.ppermute(a, "f", [(i, i ^ (2 << i % 2)) for i in range(ranks)])

    def swap_core(a):
        return lax.ppermute(a, "f", [(i, i ^ 1) for i in range(ranks)])

    def pick(a, index, axis):
        return lax.dynamic_index_in_dim(a, index, axis, keepdims=False)

    def put(a, piece, *index):
        index = index + (0,) * (a.ndim - len(index))
        return lax.dynamic_update_slice(a, piece, index)

    def direct(a):
        return [a] + [shift(a, by) for by in range(1, n)]

    def stack_z(blocks):
        out = blank((n,) + blocks[0].shape, BF)
        for k, block in enumerate(blocks):
            out = put(out, block[None], (at_z - k) % n)
        return out

    def send_z(terms):
        sent = [shift(pick(terms, (at_z - by) % n, 0), -by) for by in range(1, n)]
        return [pick(terms, at_z, 0)] + sent

    def total(terms):
        return sum(term.astype(F32) for term in terms)

    def add(a, b):
        return (a.astype(F32) + b.astype(F32)).astype(BF)

    def spread_second(pair):
        return swap_second(pair) if grid else pair

    def spread_all(pair, other):
        if grid:
            return [pair, other, swap_core(pair), swap_core(other)]
        rows = lax.all_gather(pair, "f", tiled=True)
        return jnp.split(rows, rows.shape[0] // (2 * pair.shape[0]))

    def send_core(terms):
        return swap_core(terms) if grid else terms

    def add_halves(terms, arrived):
        return add_half(terms, arrived, 0), add_half(terms, arrived, 1)

    if grid:
        owners = [rank, rank ^ first, rank ^ second, rank ^ 6]
        owners += [rank ^ 1, rank ^ 1 ^ second, rank ^ 1 ^ first, rank ^ 7]
        owners = jnp.stack(owners).astype(jnp.int32)

    def weight_terms(left, rights, by_rows):
        if grid:
            return owned_terms(owners, n, left, rights, by_rows)
        columns = [
            contract(left[:, : r.shape[1]], r, 1, 1) if by_rows else product(left, r)
            for r in rights
        ]
        terms = jnp.concatenate(columns, axis=1).astype(BF)
        return terms, terms

    def sum_f(mine):
        terms = mine.reshape(n, ranks, -1, mine.shape[1]).transpose(1, 0, 2, 3)
        return lax.psum_scatter(terms, "f", scatter_dimension=0, tiled=False)

    token_count, width = tokens.shape[1:]
    shard_rows = w_query.shape[0]
    unit = w_down.shape[0]
    hidden_units = n * unit
    pair_cols = KEY_VALUE_HEADS * HEAD_SIZE
    gain_one = gain_attn.astype(F32)[:, None]
    gain_two = gain_mlp.astype(F32)[:, None]

    def along(weight, grad):
        return jnp.sum(weight.astype(F32) * grad, axis=1)

    slots_each = stretch_map.shape[1] // n
    slots = (
        ((at_z - jnp.arange(n, dtype=jnp.int32)) % n)[:, None] * slots_each
        + jnp.arange(slots_each, dtype=jnp.int32)[None, :]
    ).reshape(-1)
    doc_all, place_all = layout(lengths[0], stretch_map[0], slots)
    allowed = (doc_all[:, None] == doc_all[None, :token_count]) & (
        place_all[:, None] <= place_all[None, :token_count]
    )
    bias = jnp.where(allowed, 0.0, -1e30).astype(F32)
    cosine, sine = rotary_tables(place_all)

    def scaled(weight, gain):
        return (weight.astype(F32) * gain).astype(BF)

    shard = jnp.concatenate([w_query, key_weight, value_weight], axis=1)
    shard = jnp.concatenate([scaled(shard, gain_one), w_out], axis=1)
    own = tokens[0]
    blocks = [own]
    gate_up = scaled(jnp.concatenate([w_gate, w_up], axis=1), gain_two)
    gate_up = gate_up.reshape(shard_rows, 2, n, ranks, unit).transpose(3, 0, 1, 2, 4)
    gate_up = gate_up.reshape(ranks, shard_rows, 2 * hidden_units)
    with scope("gate_up_f"):
        gate_up = lax.all_to_all(gate_up, "f", 0, 0, tiled=True)
    gate_up_rows = ranks * shard_rows
    pieces = gate_up_rows // unit
    grad_own = grad_first = out_grad[0]

    def beside_down(gate_up):
        gate_up = gate_up.reshape(gate_up_rows, 2 * hidden_units)
        down = w_down.reshape(unit, pieces, width // pieces).transpose(1, 0, 2)
        return jnp.concatenate([gate_up, down.reshape(gate_up_rows, width // pieces)], axis=1)

    if grid:
        with scope("attention_weights_z"):
            behind = [shift(shard, 1)]
            while len(behind) < n - 1:
                behind.append(shift(behind[-1], 1))
        with scope("attention_weights_own"):
            near = [shard, swap_first(shard), swap_second(shard)]
            near.append(swap_second(near[1]))
            mid = [behind[0], swap_first(behind[0]), swap_second(behind[0])]
            mid.append(swap_second(mid[1]))
        with scope("tokens_z"):
            blocks.append(shift(own, 1))
        with scope("out_grad_first"):
            grad_first = swap_first(grad_own)
        *behind, near[2], near[3], mid[2], mid[3], gate_up, blocks[1], grad_first = stage(
            *behind, near[2], near[3], mid[2], mid[3], gate_up, blocks[1], grad_first
        )
        gate_up_down = beside_down(gate_up)
        with scope("attention_weights_core"):
            cores = [swap_core(part) for part in near + mid]
        rest = [jnp.stack(behind[1:])]
        with scope("attention_weights_first"):
            rest.append(swap_first(rest[0]))
        with scope("attention_weights_second"):
            rest.append(swap_second(rest[0]))
        with scope("tokens_z"):
            blocks.append(shift(blocks[1], 1))
        rest[1], rest[2], blocks[2], cosine, sine, bias, gate_up_down, *cores = stage(
            rest[1], rest[2], blocks[2], cosine, sine, bias, gate_up_down, *cores
        )
        near_core, mid_core = cores[:4], cores[4:]
        with scope("attention_weights_core"):
            rest_core = [swap_core(part) for part in rest]
        with scope("attention_weights_second"):
            rest.append(swap_second(rest[1]))
        with scope("tokens_z"):
            while len(blocks) < n:
                blocks.append(shift(blocks[-1], 1))
        rest[3], blocks[-1], gate_up_down, *rest_core = stage(
            rest[3], blocks[-1], gate_up_down, *rest_core
        )
        with scope("attention_weights_core"):
            rest_core.append(swap_core(rest[3]))
    else:
        gate_up_down = beside_down(gate_up)
        while len(blocks) < n:
            blocks.append(shift(blocks[-1], 1))
    with scope("gate_up_down_z"):
        gate_up_down = lax.all_gather(gate_up_down, "z")
    cuts = [width, width + pair_cols, width + 2 * pair_cols]

    inputs = own.astype(F32)
    if grid:
        parts, starts = [], []
        for *held, moves in (
            (near, mid, rest, (0, first, second, 6)),
            (near_core, mid_core, rest_core, (1, 1 ^ second, 1 ^ first, 7)),
        ):
            for near_part, mid_part, rest_part, move in zip(*held, moves):
                parts += [near_part[None], mid_part[None], rest_part]
                starts += [(at_z - k) % n * ranks + (rank ^ move) for k in range(n)]
        starts = jnp.stack(starts).astype(jnp.int32) * shard_rows
        queries, keys, values, normed_group, gathered = project(
            starts, parts, blocks, cosine, sine
        )
        q_weight, key_matrix, value_matrix, out_weight = jnp.split(gathered, cuts, axis=1)
    else:
        gathered = lax.all_gather(shard, ("z", "f"), tiled=True)
        q_weight, key_matrix, value_matrix, out_weight = jnp.split(gathered, cuts, axis=1)
        normed_group = jnp.concatenate(blocks, axis=0).astype(F32)
        inverse = lax.rsqrt(jnp.mean(normed_group * normed_group, axis=-1, keepdims=True) + EPSILON)
        normed_group = (normed_group * inverse).astype(BF).T

        def rotated(weight, tokens):
            rows = contract(weight, normed_group[:, :tokens], 0, 0)
            rows = rows.reshape(-1, HEAD_SIZE, tokens)
            turned = [rotate(r, cosine[:, :tokens], sine[:, :tokens]) for r in rows]
            return jnp.concatenate(turned, axis=0).astype(BF)

        queries, keys = rotated(q_weight, token_count), rotated(key_matrix, n * token_count)
        values = contract(value_matrix, normed_group, 0, 0).astype(BF)
    span = n * token_count

    queries, grad_first = stage(queries, grad_first)
    with scope("out_grad_second"):
        grad_pair = jnp.concatenate([grad_own, grad_first], axis=0) if grid else grad_own
        grad_other = spread_second(grad_pair)

    attention_output, log_totals = attention_forward(queries, keys, values, bias)
    resid = inputs + contract(attention_output, out_weight, 0, 0)
    second_inverse = lax.rsqrt(jnp.mean(resid * resid, axis=-1, keepdims=True) + EPSILON)
    second_normed = resid * second_inverse
    normed_two = second_normed.astype(BF)
    normed_two, grad_other = stage(normed_two, grad_other)

    with scope("normed_first"):
        normed_first = swap_first(normed_two) if grid else normed_two
    with scope("out_grad_all"):
        grad_parts = spread_all(grad_pair, grad_other)
    with scope("normed_second"):
        (normed_first,) = stage(normed_first)
        normed_pair = normed_first
        if grid:
            normed_pair = jnp.concatenate([normed_two, normed_first], axis=0)
        normed_other = spread_second(normed_pair)
        normed_parts = spread_all(normed_pair, normed_other)
        normed_parts[1], gate_up_down = stage(normed_parts[1], gate_up_down)
    half = len(normed_parts) // 2

    scaled_far, hidden_far, both_far, down_far, down_weight = feed_forward(
        normed_parts[half:], grad_parts[half:], gate_up_down, hidden_units
    )
    with scope("scaled_core"):
        scaled_far = send_core(scaled_far)
    scaled_near, hidden_near, both_near, down_near, _ = feed_forward(
        normed_parts[:half], grad_parts[:half], gate_up_down, hidden_units
    )
    with scope("scaled_second"):
        if grid:
            scaled_near, far = add_halves(scaled_near, scaled_far)
            far, both_near = stage(far, both_near)
            far = swap_second(far)
        else:
            scaled_two = jnp.concatenate([scaled_near, scaled_far], axis=0)
            scaled_two = lax.psum_scatter(scaled_two, "f", scatter_dimension=0, tiled=True)
            scaled_two = far = scaled_two.astype(F32)
    with scope("feed_sum_z"):
        if grid:
            terms, token = feed_terms(normed_parts, [down_far, down_near], [both_near, both_far], n)
        else:
            terms = over_rows(
                jnp.concatenate(normed_parts, axis=0),
                jnp.concatenate([both_near, both_far], axis=0),
            ).astype(BF)
            down_terms = add(down_far, down_near).reshape(n, unit, pieces, width // pieces)
            down_terms = down_terms.transpose(0, 2, 1, 3).reshape(width, width // pieces)
            terms = jnp.concatenate([terms, down_terms], axis=1)
            token = jnp.zeros((8, 128), F32)
        feed_owned = lax.psum_scatter(terms, "z", scatter_dimension=0, tiled=True)
    far, token = stage(far, token)
    if grid:
        with scope("scaled_first"):
            scaled_near, far = add_halves(scaled_near, far)
            far = swap_first(far)
    if grid:
        (far,) = stage(far)
    else:
        far, scaled_near = scaled_two.astype(BF), jnp.zeros_like(scaled_two, BF)
    grad_resid, grad_attn_out, grad_mixed = middle_gradient(
        scaled_near, far, resid, out_grad[0], gathered
    )

    with scope("out_core"):
        out_away, out_mine = weight_terms(attention_output, [grad_attn_out], False)
        out_away = send_core(out_away)
    grad_mixed, out_away = stage(grad_mixed, out_away)
    with scope("out_second"):
        if grid:
            out_near, out_far = add_halves(out_mine, out_away)
            out_far = swap_second(out_far)
        else:
            out_near = out_far = sum_f(out_mine)
    grad_queries, grad_kv, by_block = attention_backward(
        at_z.astype(jnp.int32)[None],
        range(KEY_VALUE_HEADS),
        queries,
        keys,
        values,
        grad_mixed,
        log_totals,
        cosine,
        sine,
        bias,
        token,
        n,
    )
    grad_queries, out_far = stage(grad_queries, out_far)

    with scope("kv_grad_z"):
        kv_total = lax.psum_scatter(by_block, "z", scatter_dimension=0, tiled=False)
    with scope("projected_core"):
        away, mine = weight_terms(
            normed_group, [grad_queries, grad_kv.reshape(2 * pair_cols, span)], True
        )
    if grid:
        with scope("out_first"):
            out_near, out_far = add_halves(out_near, out_far)
            out_far = swap_first(out_far)
        away, out_far = stage(away, out_far)
        with scope("projected_core"):
            away = send_core(away)
        away, hidden_far, hidden_near = stage(away, hidden_far, hidden_near)
        with scope("projected_second"):
            near, far = add_halves(mine, away)
            far = swap_second(far)
        out_near = add(out_near[0], out_far[0])
    with scope("result_core"):
        result_far = send_core(product(hidden_far, down_weight).astype(BF))
        result_near = product(hidden_near, down_weight).astype(BF)
    def exchange(owned):
        with scope("gate_up_sum_f"):
            owned = owned[:, : 2 * hidden_units].reshape(ranks, shard_rows, -1)
            return lax.all_to_all(owned, "f", 0, 0, tiled=True)

    if grid:
        result_near, result_far = add_halves(result_near, result_far)
        far, result_far = stage(far, result_far)
        with scope("projected_first"):
            near, far = add_halves(near, far)
            far = swap_first(far)
        with scope("out_z"):
            out_owned = send_z(out_near)
        gate_up_owned = exchange(feed_owned)
        with scope("result_second"):
            result_far = swap_second(result_far)
        far, kv_total, gate_up_owned, result_far, *out_owned = stage(
            far, kv_total, gate_up_owned, result_far, *out_owned
        )
        with scope("result_first"):
            result_near, result_far = add_halves(result_near, result_far)
            result = result_near.astype(F32) + swap_first(result_far).astype(F32)
        near = add(near[0], far[0])
    else:
        near = sum_f(mine)
        gate_up_owned = exchange(feed_owned)
        result = jnp.concatenate([result_near, result_far], axis=0)
        result = lax.psum_scatter(result, "f", scatter_dimension=0, tiled=True)
        with scope("out_z"):
            out_owned = send_z(out_near)
    with scope("projected_z"):
        projected = send_z(near)
    result = (resid + result.astype(F32)).astype(BF)

    down_owned = feed_owned[:, 2 * hidden_units :].reshape(pieces, unit, width // pieces)
    down_owned = down_owned.transpose(1, 0, 2).reshape(unit, width).astype(F32)
    input_grad = input_gradient(
        grad_queries, kv_total.reshape(2 * pair_cols, token_count), gathered, own, grad_resid
    )
    if grid:
        gate_owned, up_owned, gain_two_owned = feed_finish(gate_up_owned, w_gate, w_up, gain_two)
        input_grad, gain_two_owned, down_owned, result, *projected = stage(
            input_grad, gain_two_owned, down_owned, result, *projected
        )
        query_owned, key_owned, value_owned, out_owned, gain_one_owned = attention_finish(
            projected, out_owned, [w_query, key_weight, value_weight], gain_one
        )
    else:
        gate_up_owned = (
            gate_up_owned.astype(F32)
            .reshape(ranks, shard_rows, 2, n, unit)
            .transpose(2, 1, 3, 0, 4)
            .reshape(2, shard_rows, n * ranks * unit)
        )
        gate_owned, up_owned = gate_up_owned[0], gate_up_owned[1]
        gain_two_owned = along(w_gate, gate_owned) + along(w_up, up_owned)
        gate_owned, up_owned = gate_owned * gain_two, up_owned * gain_two
        out_owned, grads = total(out_owned), jnp.split(total(projected), cuts[:2], axis=1)
        weights = (w_query, key_weight, value_weight)
        gain_one_owned = sum(along(weight, grad) for weight, grad in zip(weights, grads))
        query_owned, key_owned, value_owned = (grad * gain_one for grad in grads)
    return (
        result[None],
        input_grad[None],
        gain_one_owned.reshape(-1),
        query_owned,
        key_owned,
        value_owned,
        out_owned,
        gain_two_owned.reshape(-1),
        gate_owned,
        up_owned,
        down_owned,
    )


def solution(mesh):
    n, ranks = mesh.shape["seq"], mesh.shape["fsdp"]
    named = Mesh(mesh.devices, ("z", "f"))
    every = ("z", "f")
    rows, vector, matrix = P("f", "z", None), P(every), P(every, None)
    in_specs = (
        rows,
        vector,
        matrix,
        matrix,
        matrix,
        matrix,
        vector,
        matrix,
        matrix,
        matrix,
        rows,
        P("f", None),
        P("f", None),
    )
    out_specs = (rows, rows, vector) + (matrix,) * 4 + (vector,) + (matrix,) * 3

    def step(*operands):
        return on_device(n, ranks, *operands)

    return jax.shard_map(
        step, mesh=named, in_specs=in_specs, out_specs=out_specs, check_vma=False
    )
```

```python
import math

import jax
import jax.numpy as jnp
from jax import lax
from jax.experimental import pallas as pl
from jax.experimental.pallas import tpu as pltpu
from jax.sharding import Mesh
from jax.sharding import PartitionSpec as P

QUERY_HEADS = 16
KEY_VALUE_HEADS = 8
HEAD_SIZE = 96
FF = 4096
STRETCH = 128

EPSILON = 1e-05
THETA = 100000.0

BF = jnp.bfloat16
F32 = jnp.float32


def layout(doc_lengths, slot_map, slots):
    count = slot_map.shape[0]
    stretches = jnp.arange(count, dtype=jnp.int32)
    logical = jnp.sum(
        jnp.where(slot_map[None, :] == slots[:, None], stretches[None, :], 0), axis=1
    )
    places = (
        logical[:, None] * STRETCH + jnp.arange(STRETCH, dtype=jnp.int32)[None, :]
    ).reshape(-1)
    endings = jnp.cumsum(doc_lengths)
    passed = endings[None, :] <= places[:, None]
    document = jnp.sum(passed.astype(jnp.int32), axis=1)
    starts = jnp.sum(jnp.where(passed, doc_lengths[None, :], 0), axis=1)
    return document, places - starts


def rotary_tables(positions):
    half = HEAD_SIZE // 2
    freqs = THETA ** (-2.0 * jnp.arange(half, dtype=F32) / HEAD_SIZE)
    angles = positions.astype(F32)[:, None] * freqs[None, :]
    return jnp.cos(angles).T, jnp.sin(angles).T


def rotate(rows, cosine, sine):
    half = rows.shape[0] // 2
    first, second = rows[:half], rows[half:]
    return jnp.concatenate(
        [first * cosine - second * sine, second * cosine + first * sine], axis=0
    )


def contract(left, right, at_left, at_right):
    return lax.dot_general(
        left, right, (((at_left,), (at_right,)), ((), ())), preferred_element_type=F32
    )


RATIO = QUERY_HEADS // KEY_VALUE_HEADS
SCALE = 1.0 / math.sqrt(HEAD_SIZE)
VMEM_BYTES = 40 * 1024 * 1024
MOST_VMEM_BYTES = 60 * 1024 * 1024


def lasting(microseconds):
    return pl.CostEstimate(
        flops=int(microseconds * 1e9), bytes_accessed=int(microseconds * 3e6), transcendentals=0
    )


def forward_kernel(q_ref, k_ref, v_ref, bias_ref, out_ref, lse_ref):
    keys, values = k_ref[...], v_ref[...]
    for head in range(RATIO):
        rows = slice(head * HEAD_SIZE, (head + 1) * HEAD_SIZE)
        scores = contract(keys, q_ref[rows, :], 0, 0) * SCALE + bias_ref[...]
        peak = jnp.max(scores, axis=0, keepdims=True)
        weights = jnp.exp(scores - peak)
        totals = jnp.sum(weights, axis=0, keepdims=True)
        mixed = contract(values, weights.astype(BF), 1, 0)
        out_ref[rows, :] = (mixed / totals).astype(BF)
        lse_ref[0, head : head + 1, :] = peak + jnp.log(totals)


def backward_kernel(
    place_ref,
    q_ref,
    k_ref,
    v_ref,
    grad_ref,
    lse_ref,
    cos_ref,
    sin_ref,
    bias_ref,
    token_ref,
    dq_ref,
    dkv_ref,
    block_ref,
):
    count = q_ref.shape[1]
    keys, values = k_ref[...], v_ref[...]
    cosine, sine = cos_ref[:, :count], sin_ref[:, :count]
    grad_keys = jnp.zeros(keys.shape, F32)
    grad_values = jnp.zeros(keys.shape, F32)
    for head in range(RATIO):
        rows = slice(head * HEAD_SIZE, (head + 1) * HEAD_SIZE)
        queries, grads = q_ref[rows, :], grad_ref[rows, :]
        scores = contract(keys, queries, 0, 0) * SCALE + bias_ref[...]
        probs = jnp.exp(scores - lse_ref[0, head : head + 1, :])
        grad_probs = contract(values, grads, 0, 0)
        centre = jnp.sum(probs * grad_probs, axis=0, keepdims=True)
        grad_scores = (probs * (grad_probs - centre)).astype(BF)
        grad_queries = contract(keys, grad_scores, 1, 0) * SCALE
        dq_ref[rows, :] = rotate(grad_queries, cosine, -sine).astype(BF)
        grad_keys += contract(queries, grad_scores, 1, 1)
        grad_values += contract(grads, probs.astype(BF), 1, 1)
    grad_keys = rotate(grad_keys * SCALE, cos_ref[...], -sin_ref[...]).astype(BF)
    grad_values = grad_values.astype(BF)
    dkv_ref[0] = grad_keys
    dkv_ref[1] = grad_values
    blocks = block_ref.shape[0]
    for block in range(blocks):
        at = slice(block * count, (block + 1) * count)
        place = lax.rem(place_ref[0] - block + blocks, blocks)
        block_ref[place, 0] = grad_keys[:, at]
        block_ref[place, 1] = grad_values[:, at]


def attention_forward(queries, keys, values, bias):
    count, span = queries.shape[1], keys.shape[1]
    pair = RATIO * HEAD_SIZE
    mine = lambda rows, cols: pl.BlockSpec((rows, cols), lambda g: (g, 0))
    return pl.pallas_call(
        forward_kernel,
        grid=(KEY_VALUE_HEADS,),
        in_specs=[
            mine(pair, count),
            mine(HEAD_SIZE, span),
            mine(HEAD_SIZE, span),
            pl.BlockSpec(bias.shape, lambda g: (0, 0)),
        ],
        out_specs=[
            mine(pair, count),
            pl.BlockSpec((1, RATIO, count), lambda g: (g, 0, 0)),
        ],
        out_shape=[
            jax.ShapeDtypeStruct(queries.shape, BF),
            jax.ShapeDtypeStruct((KEY_VALUE_HEADS, RATIO, count), F32),
        ],
        compiler_params=pltpu.CompilerParams(vmem_limit_bytes=MOST_VMEM_BYTES),
        cost_estimate=lasting(0.1),
        name="attention_forward",
    )(queries, keys, values, bias)


def attention_backward(place, heads, queries, keys, values, grads, totals, cosine, sine, bias, token, blocks):
    count, span = queries.shape[1], keys.shape[1]
    pair = RATIO * HEAD_SIZE
    first, amount = heads.start, len(heads)
    whole = lambda a: pl.BlockSpec(a.shape, lambda g: (0,) * a.ndim)
    mine = lambda rows, cols: pl.BlockSpec((rows, cols), lambda g: (g + first, 0))
    rows = amount * HEAD_SIZE
    return pl.pallas_call(
        backward_kernel,
        grid=(amount,),
        in_specs=[
            pl.BlockSpec(memory_space=pltpu.SMEM),
            mine(pair, count),
            mine(HEAD_SIZE, span),
            mine(HEAD_SIZE, span),
            mine(pair, count),
            pl.BlockSpec((1, RATIO, count), lambda g: (g + first, 0, 0)),
            whole(cosine),
            whole(sine),
            whole(bias),
            whole(token),
        ],
        out_specs=[
            pl.BlockSpec((pair, count), lambda g: (g, 0)),
            pl.BlockSpec((2, HEAD_SIZE, span), lambda g: (0, g, 0)),
            pl.BlockSpec((blocks, 2, HEAD_SIZE, count), lambda g: (0, 0, g, 0)),
        ],
        out_shape=[
            jax.ShapeDtypeStruct((amount * pair, count), BF),
            jax.ShapeDtypeStruct((2, rows, span), BF),
            jax.ShapeDtypeStruct((blocks, 2, rows, count), BF),
        ],
        compiler_params=pltpu.CompilerParams(vmem_limit_bytes=VMEM_BYTES),
        cost_estimate=lasting(0.1),
        name="attention_backward",
    )(place, queries, keys, values, grads, totals, cosine, sine, bias, token)


def product(left, right):
    return jnp.dot(left, right, preferred_element_type=F32)


def over_rows(left, right):
    return lax.dot_general(left, right, (((0,), (0,)), ((), ())), preferred_element_type=F32)


def times_transposed(left, right):
    return lax.dot_general(left, right, (((1,), (1,)), ((), ())), preferred_element_type=F32)


def blank(shape, dtype):
    return pl.pallas_call(
        lambda out_ref: None,
        out_shape=jax.ShapeDtypeStruct(shape, dtype),
        out_specs=pl.BlockSpec(memory_space=pl.ANY),
        name="blank",
    )()


def terms_kernel(steps, by_rows, owners_ref, left_ref, *refs):
    rights, (away_ref, mine_ref, total_ref) = refs[:-3], refs[-3:]
    step = pl.program_id(0)
    slots, n, rows, cols = away_ref.shape
    for right_ref, (first, last) in zip(rights, steps):

        @pl.when((step >= first) & (step < last))
        def _(right_ref=right_ref):
            if by_rows:
                right = right_ref[...]
                product = contract(left_ref[:, : right.shape[1]], right, 1, 1)
            else:
                product = contract(left_ref[...], right_ref[...], 1, 0)
            total_ref[...] = product.astype(BF)

    for slot in range(slots):
        for z in range(n):
            base = z * 2 * slots * rows
            for out_ref, at in ((mine_ref, slot), (away_ref, slots + slot)):
                start = pl.multiple_of(base + owners_ref[at] * rows, 16)
                out_ref[slot, z] = total_ref[pl.ds(start, rows), :]


def owned_terms(owners, n, left, rights, by_rows):
    tile = 256
    depth = left.shape[0] // (8 * n)
    steps, first = [], 0
    for right in rights:
        last = first + right.shape[0 if by_rows else 1] // tile
        steps.append((first, last))
        first = last
    specs = []
    for right, (start, stop) in zip(rights, steps):
        if by_rows:
            specs.append(
                pl.BlockSpec(
                    (tile, right.shape[1]),
                    lambda j, o, start=start, stop=stop: (jnp.clip(j, start, stop - 1) - start, 0),
                )
            )
        else:
            specs.append(pl.BlockSpec((right.shape[0], tile), lambda j, o: (0, j)))
    out = jax.ShapeDtypeStruct((4, n, depth, first * tile), BF)
    out_spec = pl.BlockSpec((4, n, depth, tile), lambda j, o: (0, 0, 0, j))
    return pl.pallas_call(
        lambda *refs: terms_kernel(steps, by_rows, *refs),
        grid_spec=pltpu.PrefetchScalarGridSpec(
            num_scalar_prefetch=1,
            grid=(first,),
            in_specs=[pl.BlockSpec(left.shape, lambda j, o: (0, 0))] + specs,
            out_specs=[out_spec, out_spec],
            scratch_shapes=[pltpu.VMEM((left.shape[0], tile), BF)],
        ),
        out_shape=[out, out],
        compiler_params=pltpu.CompilerParams(vmem_limit_bytes=VMEM_BYTES),
        cost_estimate=lasting(0.1),
        name="owned_terms",
    )(owners, left, *rights)


def project_kernel(n, count, starts_ref, *refs):
    parts, blocks, (cos_ref, sin_ref) = refs[:count], refs[count : count + n], refs[count + n : count + n + 2]
    refs = refs[count + n + 2 :]
    q_ref, k_ref, v_ref, normed_ref, weight_out, weight_ref, token_ref, part_sem, token_sem, out_sem = refs
    rows, (count, width) = parts[0].shape[1], blocks[0].shape
    token_copies = [
        pltpu.make_async_copy(block, token_ref.at[pl.ds(k * count, count)], token_sem.at[k])
        for k, block in enumerate(blocks)
    ]
    pair_cols = k_ref.shape[0]
    middle, cols = width + 2 * pair_cols, weight_ref.shape[1]
    early, late = [], []
    for part in parts:
        for j in range(part.shape[0]):
            k = len(early)
            at = pl.multiple_of(starts_ref[k], 16)
            for copies, columns, sem in (
                (early, slice(0, middle), part_sem.at[0, k]),
                (late, slice(middle, cols), part_sem.at[1, k]),
            ):
                copies.append(
                    pltpu.make_async_copy(
                        part.at[j, :, columns], weight_ref.at[pl.ds(at, rows), columns], sem
                    )
                )
    for copy in token_copies + early + late:
        copy.start()
    for k, copy in enumerate(token_copies):
        copy.wait()
        x = token_ref[k * count : (k + 1) * count, :].astype(F32)
        inverse = lax.rsqrt(jnp.mean(x * x, axis=-1, keepdims=True) + EPSILON)
        normed_ref[:, k * count : (k + 1) * count] = (x * inverse).astype(BF).T
    for copy in early:
        copy.wait()
    out_copy = pltpu.make_async_copy(weight_ref, weight_out, out_sem)
    tile = 4 * HEAD_SIZE
    for out_ref, base, rotated in ((q_ref, 0, True), (k_ref, width, True), (v_ref, width + pair_cols, False)):
        tokens = out_ref.shape[1]

        def step(j, carry, out_ref=out_ref, base=base, rotated=rotated, tokens=tokens):
            at = pl.multiple_of(j * tile, tile)
            columns = weight_ref[:, pl.ds(pl.multiple_of(base + at, 128), tile)]
            product = contract(columns, normed_ref[:, :tokens], 0, 0)
            for head in range(4):
                part = product[head * HEAD_SIZE : (head + 1) * HEAD_SIZE]
                if rotated:
                    part = rotate(part, cos_ref[:, :tokens], sin_ref[:, :tokens])
                start = pl.multiple_of(at + head * HEAD_SIZE, 16)
                out_ref[pl.ds(start, HEAD_SIZE), :] = part.astype(BF)
            return carry

        lax.fori_loop(0, out_ref.shape[0] // tile, step, 0)
        if out_ref is q_ref:
            for copy in late:
                copy.wait()
            out_copy.start()
    out_copy.wait()


def project(starts, parts, blocks, cosine, sine):
    rows, cols = parts[0].shape[1:]
    n, (count, width) = len(blocks), blocks[0].shape
    span, pair_cols = n * count, KEY_VALUE_HEADS * HEAD_SIZE
    every = pl.BlockSpec(memory_space=pl.ANY)
    vmem = pl.BlockSpec(memory_space=pltpu.VMEM)
    shape = (starts.shape[0] * rows, cols)
    return pl.pallas_call(
        lambda *refs: project_kernel(n, len(parts), *refs),
        in_specs=[pl.BlockSpec(memory_space=pltpu.SMEM)] + [every] * (len(parts) + n) + [vmem, vmem],
        out_specs=[vmem, vmem, vmem, vmem, every],
        out_shape=[
            jax.ShapeDtypeStruct((width, count), BF),
            jax.ShapeDtypeStruct((pair_cols, span), BF),
            jax.ShapeDtypeStruct((pair_cols, span), BF),
            jax.ShapeDtypeStruct((width, span), BF),
            jax.ShapeDtypeStruct(shape, BF),
        ],
        scratch_shapes=[
            pltpu.VMEM(shape, BF),
            pltpu.VMEM((span, width), BF),
            pltpu.SemaphoreType.DMA((2,) + starts.shape),
            pltpu.SemaphoreType.DMA((n,)),
            pltpu.SemaphoreType.DMA,
        ],
        compiler_params=pltpu.CompilerParams(vmem_limit_bytes=MOST_VMEM_BYTES),
        cost_estimate=lasting(0.1),
        name="project",
    )(starts, *parts, *blocks, cosine, sine)


def feed_kernel(count, *refs):
    parts, grads, blocks_ref = refs[:count], refs[count : 2 * count], refs[2 * count]
    refs = refs[2 * count + 1 :]
    scaled_ref, hidden_ref, both_ref, sum_ref, down_ref = refs[:5]
    total_ref, part_ref, grad_ref, weight_ref, part_sem, grad_sem, block_sem = refs[5:]
    step = pl.program_id(0)
    units = hidden_ref.shape[1]
    (n, rows, _), width = blocks_ref.shape, down_ref.shape[1]
    unit = units // n
    pieces = rows // unit
    piece = width // pieces

    def copies(k):
        return (
            pltpu.make_async_copy(parts[k], part_ref.at[k], part_sem.at[k]),
            pltpu.make_async_copy(grads[k], grad_ref.at[k], grad_sem.at[k]),
        )

    @pl.when(step == 0)
    def _():
        block_copies = [
            pltpu.make_async_copy(
                blocks_ref.at[k, :, : 2 * units],
                weight_ref.at[pl.ds(k * rows, rows)],
                block_sem.at[k * (1 + pieces)],
            )
            for k in range(n)
        ]
        block_copies += [
            pltpu.make_async_copy(
                blocks_ref.at[k, pl.ds(j * unit, unit), 2 * units :],
                down_ref.at[pl.ds(k * unit, unit), j * piece : (j + 1) * piece],
                block_sem.at[k * (1 + pieces) + 1 + j],
            )
            for k in range(n)
            for j in range(pieces)
        ]
        for copy in block_copies:
            copy.start()
        for k in range(count):
            for copy in copies(k):
                copy.start()
        for copy in block_copies:
            copy.wait()
        total_ref[...] = jnp.zeros_like(total_ref)

    for k in range(count):

        @pl.when(step == k)
        def _(k=k):
            for copy in copies(k):
                copy.wait()

    part, grad = part_ref[step], grad_ref[step]
    gate = product(part, weight_ref[:, :units])
    upper = product(part, weight_ref[:, units:])
    sigmoid = jax.nn.sigmoid(gate)
    silu = gate * sigmoid
    hidden = (silu * upper).astype(BF)
    hidden_ref[...] = hidden
    grad_hidden = contract(grad, down_ref[...], 1, 1)
    grad_gate = (grad_hidden * upper * sigmoid * (1.0 + gate * (1.0 - sigmoid))).astype(BF)
    grad_up = (grad_hidden * silu).astype(BF)
    both_ref[:, :units] = grad_gate
    both_ref[:, units:] = grad_up
    scaled = contract(grad_gate, weight_ref[:, :units], 1, 1)
    scaled += contract(grad_up, weight_ref[:, units:], 1, 1)
    scaled_ref[...] = scaled.astype(BF)
    total_ref[...] += contract(hidden, grad, 0, 0)

    @pl.when(step == count - 1)
    def _():
        sum_ref[...] = total_ref[...].astype(BF)


def feed_forward(parts, grads, blocks, units):
    count, n = len(parts), blocks.shape[0]
    rows, width = parts[0].shape
    every = pl.BlockSpec(memory_space=pl.ANY)
    part = lambda cols: pl.BlockSpec((rows, cols), lambda k: (k, 0))
    whole = pl.BlockSpec((units, width), lambda k: (0, 0))
    return pl.pallas_call(
        lambda *refs: feed_kernel(count, *refs),
        grid=(count,),
        in_specs=[every] * (2 * count + 1),
        out_specs=[part(width), part(units), part(2 * units), whole, whole],
        out_shape=[
            jax.ShapeDtypeStruct((count * rows, width), BF),
            jax.ShapeDtypeStruct((count * rows, units), BF),
            jax.ShapeDtypeStruct((count * rows, 2 * units), BF),
            jax.ShapeDtypeStruct((units, width), BF),
            jax.ShapeDtypeStruct((units, width), BF),
        ],
        scratch_shapes=[
            pltpu.VMEM((units, width), F32),
            pltpu.VMEM((count, rows, width), BF),
            pltpu.VMEM((count, rows, width), BF),
            pltpu.VMEM((n * blocks.shape[1], 2 * units), BF),
            pltpu.SemaphoreType.DMA((count,)),
            pltpu.SemaphoreType.DMA((count,)),
            pltpu.SemaphoreType.DMA((n * (1 + blocks.shape[1] * n // units),)),
        ],
        compiler_params=pltpu.CompilerParams(vmem_limit_bytes=MOST_VMEM_BYTES),
        cost_estimate=lasting(30),
        name="feed_forward",
    )(*parts, *grads, blocks)


def add_kernel(a_ref, b_ref, out_ref):
    out_ref[...] = (a_ref[0].astype(F32) + b_ref[0].astype(F32)).astype(BF)


def add_half(a, b, which):
    cols = a.shape[-1]
    both = [x.reshape(2, -1, cols) for x in (a, b)]
    rows = both[0].shape[1]
    tile = rows // 2 if rows % 32 == 0 else rows
    out = pl.pallas_call(
        add_kernel,
        grid=(rows // tile,),
        in_specs=[pl.BlockSpec((1, tile, cols), lambda j: (which, j, 0))] * 2,
        out_specs=pl.BlockSpec((tile, cols), lambda j: (j, 0)),
        out_shape=jax.ShapeDtypeStruct((rows, cols), BF),
        compiler_params=pltpu.CompilerParams(vmem_limit_bytes=VMEM_BYTES),
        cost_estimate=lasting(0.1),
        name="add_half",
    )(*both)
    return out.reshape((a.shape[0] // 2,) + a.shape[1:])


def feed_terms_kernel(count, *refs):
    parts, (far_ref, near_ref, *boths, out_ref, token_ref) = refs[:count], refs[count:]
    token_ref[...] = jnp.zeros_like(token_ref)
    rows, cols = parts[0].shape[0], boths[0].shape[1]
    unit, width = far_ref.shape
    pieces = out_ref.shape[0] // unit
    piece = width // pieces
    each = boths[0].shape[0] // rows
    total = jnp.zeros((out_ref.shape[0], cols), F32)
    for k, part in enumerate(parts):
        at = k % each * rows
        total += contract(part[...], boths[k // each][at : at + rows, :], 0, 0)
    out_ref[:, :cols] = total.astype(BF)
    down = (far_ref[...].astype(F32) + near_ref[...].astype(F32)).astype(BF)
    for j in range(pieces):
        out_ref[j * unit : (j + 1) * unit, cols:] = down[:, j * piece : (j + 1) * piece]


def feed_terms(parts, downs, boths, n):
    rows, width = parts[0].shape
    tile, cols = width // n, boths[0].shape[1]
    unit = downs[0].shape[0] // n
    more = width * unit // tile
    return pl.pallas_call(
        lambda *refs: feed_terms_kernel(len(parts), *refs),
        grid=(n,),
        in_specs=[pl.BlockSpec((rows, tile), lambda j: (0, j))] * len(parts)
        + [pl.BlockSpec((unit, width), lambda j: (j, 0))] * 2
        + [pl.BlockSpec(both.shape, lambda j: (0, 0)) for both in boths],
        out_specs=[
            pl.BlockSpec((tile, cols + more), lambda j: (j, 0)),
            pl.BlockSpec((8, 128), lambda j: (0, 0)),
        ],
        out_shape=[
            jax.ShapeDtypeStruct((width, cols + more), BF),
            jax.ShapeDtypeStruct((8, 128), F32),
        ],
        compiler_params=pltpu.CompilerParams(vmem_limit_bytes=VMEM_BYTES),
        cost_estimate=lasting(15),
        name="feed_terms",
    )(*parts, *downs, *boths)


def feed_finish_kernel(
    arrived_ref, gate_ref, up_ref, gain_ref, gate_out, up_out, gain_out
):
    ranks, rows, cols = arrived_ref.shape
    units = cols // 2
    n = gate_ref.shape[1] // (ranks * 128)
    unit = units // n
    gain = gain_ref[...]
    total = jnp.zeros((rows, unit), F32)
    for r in range(ranks):
        for z in range(n):
            at = slice((z * ranks + r) * unit, (z * ranks + r + 1) * unit)
            for half, weight_ref, out_ref in ((0, gate_ref, gate_out), (units, up_ref, up_out)):
                start = half + z * unit
                grad = arrived_ref[r, :, start : start + unit].astype(F32)
                out_ref[:, at] = grad * gain
                total += grad * weight_ref[:, at].astype(F32)
    gain_out[...] = jnp.sum(total, axis=1, keepdims=True)


def feed_finish(arrived, gate, up, gain):
    return pl.pallas_call(
        feed_finish_kernel,
        out_shape=[
            jax.ShapeDtypeStruct(gate.shape, F32),
            jax.ShapeDtypeStruct(up.shape, F32),
            jax.ShapeDtypeStruct(gain.shape, F32),
        ],
        compiler_params=pltpu.CompilerParams(vmem_limit_bytes=VMEM_BYTES),
        cost_estimate=lasting(0.1),
        name="feed_finish",
    )(arrived, gate, up, gain)


def attention_finish_kernel(n, *refs):
    projected, outs, weights = refs[:n], refs[n : 2 * n], refs[2 * n : 2 * n + 3]
    gain_ref, *grad_refs, out_ref, gain_out = refs[2 * n + 3 :]
    gain = gain_ref[...]
    out_ref[...] = sum(ref[...].astype(F32) for ref in outs)
    first = 0
    total = jnp.zeros(gain.shape, F32)
    for weight_ref, grad_ref in zip(weights, grad_refs):
        at = slice(first, first + weight_ref.shape[1])
        first = at.stop
        grad = sum(ref[:, at].astype(F32) for ref in projected)
        grad_ref[...] = grad * gain
        total += jnp.sum(grad * weight_ref[...].astype(F32), axis=1, keepdims=True)
    gain_out[...] = total


def attention_finish(projected, outs, weights, gain):
    shapes = [weight.shape for weight in weights] + [outs[0].shape, gain.shape]
    return pl.pallas_call(
        lambda *refs: attention_finish_kernel(len(outs), *refs),
        out_shape=[jax.ShapeDtypeStruct(shape, F32) for shape in shapes],
        compiler_params=pltpu.CompilerParams(vmem_limit_bytes=VMEM_BYTES),
        cost_estimate=lasting(0.1),
        name="attention_finish",
    )(*projected, *outs, *weights, gain)


def out_kernel(mixed_ref, weight_ref, own_ref, resid_ref, normed_ref, left_ref):
    step, tile = pl.program_id(0), weight_ref.shape[1]

    @pl.when(step == 0)
    def _():
        left_ref[...] = mixed_ref[...].T

    at = pl.ds(pl.multiple_of(step * tile, tile), tile)
    resid_ref[:, at] = own_ref[:, at].astype(F32) + product(left_ref[...], weight_ref[...])

    @pl.when(step == pl.num_programs(0) - 1)
    def _():
        resid = resid_ref[...]
        inverse = lax.rsqrt(jnp.mean(resid * resid, axis=-1, keepdims=True) + EPSILON)
        normed_ref[...] = (resid * inverse).astype(BF)


def out_product(mixed, weight, own):
    count, width = own.shape
    tile = 256
    first = (weight.shape[1] - width) // tile
    whole = lambda a: pl.BlockSpec(a.shape, lambda j: (0, 0))
    return pl.pallas_call(
        out_kernel,
        grid=(width // tile,),
        in_specs=[
            whole(mixed),
            pl.BlockSpec((weight.shape[0], tile), lambda j: (0, j + first)),
            whole(own),
        ],
        out_specs=[whole(own), whole(own)],
        out_shape=[
            jax.ShapeDtypeStruct((count, width), F32),
            jax.ShapeDtypeStruct((count, width), BF),
        ],
        scratch_shapes=[pltpu.VMEM((count, mixed.shape[0]), BF)],
        compiler_params=pltpu.CompilerParams(vmem_limit_bytes=VMEM_BYTES),
        cost_estimate=lasting(0.1),
        name="out_product",
    )(mixed, weight, own)


def middle_kernel(near_ref, far_ref, resid_ref, grad_ref, weight_ref, total_ref, round_ref, mixed_ref):
    @pl.when(pl.program_id(0) == 0)
    def _():
        resid = resid_ref[...]
        scaled = near_ref[...].astype(F32) + far_ref[...].astype(F32)
        inverse = lax.rsqrt(jnp.mean(resid * resid, axis=-1, keepdims=True) + EPSILON)
        normed = resid * inverse
        mean = jnp.mean(scaled * normed, axis=-1, keepdims=True)
        total = grad_ref[...].astype(F32) + inverse * (scaled - normed * mean)
        total_ref[...] = total
        round_ref[...] = total.astype(BF)

    mixed_ref[...] = contract(weight_ref[...], round_ref[...], 1, 1).astype(BF)


def middle_gradient(near, far, resid, grad, weight):
    count, width = resid.shape
    tile = 256
    last = weight.shape[1] // width - 1
    whole = pl.BlockSpec((count, width), lambda j: (0, 0))
    return pl.pallas_call(
        middle_kernel,
        grid=(width // tile,),
        in_specs=[whole] * 4 + [pl.BlockSpec((tile, width), lambda j: (j, last))],
        out_specs=[whole, whole, pl.BlockSpec((tile, count), lambda j: (j, 0))],
        out_shape=[
            jax.ShapeDtypeStruct((count, width), F32),
            jax.ShapeDtypeStruct((count, width), BF),
            jax.ShapeDtypeStruct((width, count), BF),
        ],
        compiler_params=pltpu.CompilerParams(vmem_limit_bytes=VMEM_BYTES),
        cost_estimate=lasting(0.1),
        name="middle_gradient",
    )(near, far, resid, grad, weight)


def input_kernel(query_ref, pair_ref, weight_ref, own_ref, resid_ref, out_ref, left_ref, total_ref):
    step = pl.program_id(0)
    queries, tile = query_ref.shape[0], weight_ref.shape[0]

    @pl.when(step == 0)
    def _():
        left_ref[:, :queries] = query_ref[...].T
        left_ref[:, queries:] = pair_ref[...].T

    at = pl.multiple_of(step * tile, tile)
    total_ref[:, pl.ds(at, tile)] = contract(
        left_ref[...], weight_ref[:, : left_ref.shape[1]], 1, 1
    )

    @pl.when(step == pl.num_programs(0) - 1)
    def _():
        x, scaled = own_ref[...].astype(F32), total_ref[...]
        inverse = lax.rsqrt(jnp.mean(x * x, axis=-1, keepdims=True) + EPSILON)
        normed = x * inverse
        mean = jnp.mean(scaled * normed, axis=-1, keepdims=True)
        out_ref[...] = (resid_ref[...] + inverse * (scaled - normed * mean)).astype(BF)


def input_gradient(queries, pairs, weight, own, resid):
    count, width = own.shape
    tile = 256
    whole = lambda a: pl.BlockSpec(a.shape, lambda j: (0, 0))
    features = queries.shape[0] + pairs.shape[0]
    return pl.pallas_call(
        input_kernel,
        grid=(width // tile,),
        in_specs=[
            whole(queries),
            whole(pairs),
            pl.BlockSpec((tile, weight.shape[1]), lambda j: (j, 0)),
            whole(own),
            whole(resid),
        ],
        out_specs=pl.BlockSpec((count, width), lambda j: (0, 0)),
        out_shape=jax.ShapeDtypeStruct((count, width), BF),
        scratch_shapes=[pltpu.VMEM((count, features), BF), pltpu.VMEM((count, width), F32)],
        compiler_params=pltpu.CompilerParams(vmem_limit_bytes=VMEM_BYTES),
        cost_estimate=lasting(0.1),
        name="input_gradient",
    )(queries, pairs, weight, own, resid)


def on_device(n, ranks, *operands):
    (
        tokens,
        gain_attn,
        w_query,
        key_weight,
        value_weight,
        w_out,
        gain_mlp,
        w_gate,
        w_up,
        w_down,
        out_grad,
        lengths,
        stretch_map,
    ) = operands
    at_z, rank = lax.axis_index("z"), lax.axis_index("f")
    grid = ranks == 8 and w_down.shape[0] % 128 == 0
    turn = rank % 2
    first, second = 4 >> turn, 2 << turn
    scope = jax.named_scope

    def stage(*arrays):
        return lax.optimization_barrier(arrays)

    def shift(a, by):
        return lax.ppermute(a, "z", [(i, (i + by) % n) for i in range(n)])

    def swap_first(a):
        return lax.ppermute(a, "f", [(i, i ^ (4 >> i % 2)) for i in range(ranks)])

    def swap_second(a):
        return lax.ppermute(a, "f", [(i, i ^ (2 << i % 2)) for i in range(ranks)])

    def swap_core(a):
        return lax.ppermute(a, "f", [(i, i ^ 1) for i in range(ranks)])

    def pick(a, index, axis):
        return lax.dynamic_index_in_dim(a, index, axis, keepdims=False)

    def put(a, piece, *index):
        index = index + (0,) * (a.ndim - len(index))
        return lax.dynamic_update_slice(a, piece, index)

    def direct(a):
        return [a] + [shift(a, by) for by in range(1, n)]

    def stack_z(blocks):
        out = blank((n,) + blocks[0].shape, BF)
        for k, block in enumerate(blocks):
            out = put(out, block[None], (at_z - k) % n)
        return out

    def send_z(terms):
        sent = [shift(pick(terms, (at_z - by) % n, 0), -by) for by in range(1, n)]
        return [pick(terms, at_z, 0)] + sent

    def total(terms):
        return sum(term.astype(F32) for term in terms)

    def add(a, b):
        return (a.astype(F32) + b.astype(F32)).astype(BF)

    def spread_second(pair):
        return swap_second(pair) if grid else pair

    def spread_all(pair, other):
        if grid:
            return [pair, other, swap_core(pair), swap_core(other)]
        rows = lax.all_gather(pair, "f", tiled=True)
        return jnp.split(rows, rows.shape[0] // (2 * pair.shape[0]))

    def send_core(terms):
        return swap_core(terms) if grid else terms

    def add_halves(terms, arrived):
        return add_half(terms, arrived, 0), add_half(terms, arrived, 1)

    if grid:
        owners = [rank, rank ^ first, rank ^ second, rank ^ 6]
        owners += [rank ^ 1, rank ^ 1 ^ second, rank ^ 1 ^ first, rank ^ 7]
        owners = jnp.stack(owners).astype(jnp.int32)

    def weight_terms(left, rights, by_rows):
        if grid:
            return owned_terms(owners, n, left, rights, by_rows)
        columns = [
            contract(left[:, : r.shape[1]], r, 1, 1) if by_rows else product(left, r)
            for r in rights
        ]
        terms = jnp.concatenate(columns, axis=1).astype(BF)
        return terms, terms

    def sum_f(mine):
        terms = mine.reshape(n, ranks, -1, mine.shape[1]).transpose(1, 0, 2, 3)
        return lax.psum_scatter(terms, "f", scatter_dimension=0, tiled=False)

    token_count, width = tokens.shape[1:]
    shard_rows = w_query.shape[0]
    unit = w_down.shape[0]
    hidden_units = n * unit
    pair_cols = KEY_VALUE_HEADS * HEAD_SIZE
    gain_one = gain_attn.astype(F32)[:, None]
    gain_two = gain_mlp.astype(F32)[:, None]

    def along(weight, grad):
        return jnp.sum(weight.astype(F32) * grad, axis=1)

    slots_each = stretch_map.shape[1] // n
    slots = (
        ((at_z - jnp.arange(n, dtype=jnp.int32)) % n)[:, None] * slots_each
        + jnp.arange(slots_each, dtype=jnp.int32)[None, :]
    ).reshape(-1)
    doc_all, place_all = layout(lengths[0], stretch_map[0], slots)
    allowed = (doc_all[:, None] == doc_all[None, :token_count]) & (
        place_all[:, None] <= place_all[None, :token_count]
    )
    bias = jnp.where(allowed, 0.0, -1e30).astype(F32)
    cosine, sine = rotary_tables(place_all)

    def scaled(weight, gain):
        return (weight.astype(F32) * gain).astype(BF)

    shard = jnp.concatenate([w_query, key_weight, value_weight], axis=1)
    shard = jnp.concatenate([scaled(shard, gain_one), w_out], axis=1)
    own = tokens[0]
    blocks = [own]
    gate_up = scaled(jnp.concatenate([w_gate, w_up], axis=1), gain_two)
    gate_up = gate_up.reshape(shard_rows, 2, n, ranks, unit).transpose(3, 0, 1, 2, 4)
    gate_up = gate_up.reshape(ranks, shard_rows, 2 * hidden_units)
    with scope("gate_up_f"):
        gate_up = lax.all_to_all(gate_up, "f", 0, 0, tiled=True)
    gate_up_rows = ranks * shard_rows
    pieces = gate_up_rows // unit
    grad_own = grad_first = out_grad[0]

    def beside_down(gate_up):
        gate_up = gate_up.reshape(gate_up_rows, 2 * hidden_units)
        down = w_down.reshape(unit, pieces, width // pieces).transpose(1, 0, 2)
        return jnp.concatenate([gate_up, down.reshape(gate_up_rows, width // pieces)], axis=1)

    if grid:
        with scope("attention_weights_z"):
            behind = [shift(shard, 1)]
            while len(behind) < n - 1:
                behind.append(shift(behind[-1], 1))
        with scope("attention_weights_own"):
            near = [shard, swap_first(shard), swap_second(shard)]
            near.append(swap_second(near[1]))
            mid = [behind[0], swap_first(behind[0]), swap_second(behind[0])]
            mid.append(swap_second(mid[1]))
        with scope("tokens_z"):
            blocks.append(shift(own, 1))
        with scope("out_grad_first"):
            grad_first = swap_first(grad_own)
        *behind, near[2], near[3], mid[2], mid[3], gate_up, blocks[1], grad_first = stage(
            *behind, near[2], near[3], mid[2], mid[3], gate_up, blocks[1], grad_first
        )
        gate_up_down = beside_down(gate_up)
        with scope("attention_weights_core"):
            cores = [swap_core(part) for part in near + mid]
        rest = [jnp.stack(behind[1:])]
        with scope("attention_weights_first"):
            rest.append(swap_first(rest[0]))
        with scope("attention_weights_second"):
            rest.append(swap_second(rest[0]))
        with scope("tokens_z"):
            blocks.append(shift(blocks[1], 1))
        rest[1], rest[2], blocks[2], cosine, sine, bias, gate_up_down, *cores = stage(
            rest[1], rest[2], blocks[2], cosine, sine, bias, gate_up_down, *cores
        )
        near_core, mid_core = cores[:4], cores[4:]
        with scope("attention_weights_core"):
            rest_core = [swap_core(part) for part in rest]
        with scope("attention_weights_second"):
            rest.append(swap_second(rest[1]))
        with scope("tokens_z"):
            while len(blocks) < n:
                blocks.append(shift(blocks[-1], 1))
        rest[3], blocks[-1], gate_up_down, *rest_core = stage(
            rest[3], blocks[-1], gate_up_down, *rest_core
        )
        with scope("attention_weights_core"):
            rest_core.append(swap_core(rest[3]))
    else:
        gate_up_down = beside_down(gate_up)
        while len(blocks) < n:
            blocks.append(shift(blocks[-1], 1))
    with scope("gate_up_down_z"):
        gate_up_down = lax.all_gather(gate_up_down, "z")
    cuts = [width, width + pair_cols, width + 2 * pair_cols]

    inputs = own.astype(F32)
    if grid:
        parts, starts = [], []
        for *held, moves in (
            (near, mid, rest, (0, first, second, 6)),
            (near_core, mid_core, rest_core, (1, 1 ^ second, 1 ^ first, 7)),
        ):
            for near_part, mid_part, rest_part, move in zip(*held, moves):
                parts += [near_part[None], mid_part[None], rest_part]
                starts += [(at_z - k) % n * ranks + (rank ^ move) for k in range(n)]
        starts = jnp.stack(starts).astype(jnp.int32) * shard_rows
        queries, keys, values, normed_group, gathered = project(
            starts, parts, blocks, cosine, sine
        )
        q_weight, key_matrix, value_matrix, out_weight = jnp.split(gathered, cuts, axis=1)
    else:
        gathered = lax.all_gather(shard, ("z", "f"), tiled=True)
        q_weight, key_matrix, value_matrix, out_weight = jnp.split(gathered, cuts, axis=1)
        normed_group = jnp.concatenate(blocks, axis=0).astype(F32)
        inverse = lax.rsqrt(jnp.mean(normed_group * normed_group, axis=-1, keepdims=True) + EPSILON)
        normed_group = (normed_group * inverse).astype(BF).T

        def rotated(weight, tokens):
            rows = contract(weight, normed_group[:, :tokens], 0, 0)
            rows = rows.reshape(-1, HEAD_SIZE, tokens)
            turned = [rotate(r, cosine[:, :tokens], sine[:, :tokens]) for r in rows]
            return jnp.concatenate(turned, axis=0).astype(BF)

        queries, keys = rotated(q_weight, token_count), rotated(key_matrix, n * token_count)
        values = contract(value_matrix, normed_group, 0, 0).astype(BF)
    span = n * token_count

    queries, grad_first = stage(queries, grad_first)
    with scope("out_grad_second"):
        grad_pair = jnp.concatenate([grad_own, grad_first], axis=0) if grid else grad_own
        grad_other = spread_second(grad_pair)

    attention_output, log_totals = attention_forward(queries, keys, values, bias)
    resid, normed_two = out_product(attention_output, gathered, own)
    normed_two, grad_other = stage(normed_two, grad_other)

    with scope("normed_first"):
        normed_first = swap_first(normed_two) if grid else normed_two
    with scope("out_grad_all"):
        grad_parts = spread_all(grad_pair, grad_other)
    with scope("normed_second"):
        (normed_first,) = stage(normed_first)
        normed_pair = normed_first
        if grid:
            normed_pair = jnp.concatenate([normed_two, normed_first], axis=0)
        normed_other = spread_second(normed_pair)
        normed_parts = spread_all(normed_pair, normed_other)
        normed_parts[1], gate_up_down = stage(normed_parts[1], gate_up_down)
    half = len(normed_parts) // 2

    scaled_far, hidden_far, both_far, down_far, down_weight = feed_forward(
        normed_parts[half:], grad_parts[half:], gate_up_down, hidden_units
    )
    with scope("scaled_core"):
        scaled_far = send_core(scaled_far)
    scaled_near, hidden_near, both_near, down_near, _ = feed_forward(
        normed_parts[:half], grad_parts[:half], gate_up_down, hidden_units
    )
    with scope("scaled_second"):
        if grid:
            scaled_near, far = add_halves(scaled_near, scaled_far)
            far, both_near = stage(far, both_near)
            far = swap_second(far)
        else:
            scaled_two = jnp.concatenate([scaled_near, scaled_far], axis=0)
            scaled_two = lax.psum_scatter(scaled_two, "f", scatter_dimension=0, tiled=True)
            scaled_two = far = scaled_two.astype(F32)
    with scope("feed_sum_z"):
        if grid:
            terms, token = feed_terms(normed_parts, [down_far, down_near], [both_near, both_far], n)
        else:
            terms = over_rows(
                jnp.concatenate(normed_parts, axis=0),
                jnp.concatenate([both_near, both_far], axis=0),
            ).astype(BF)
            down_terms = add(down_far, down_near).reshape(n, unit, pieces, width // pieces)
            down_terms = down_terms.transpose(0, 2, 1, 3).reshape(width, width // pieces)
            terms = jnp.concatenate([terms, down_terms], axis=1)
            token = jnp.zeros((8, 128), F32)
        feed_owned = lax.psum_scatter(terms, "z", scatter_dimension=0, tiled=True)
    far, token = stage(far, token)
    if grid:
        with scope("scaled_first"):
            scaled_near, far = add_halves(scaled_near, far)
            far = swap_first(far)
    if grid:
        (far,) = stage(far)
    else:
        far, scaled_near = scaled_two.astype(BF), jnp.zeros_like(scaled_two, BF)
    grad_resid, grad_attn_out, grad_mixed = middle_gradient(
        scaled_near, far, resid, out_grad[0], gathered
    )

    with scope("out_core"):
        out_away, out_mine = weight_terms(attention_output, [grad_attn_out], False)
        out_away = send_core(out_away)
    grad_mixed, out_away = stage(grad_mixed, out_away)
    with scope("out_second"):
        if grid:
            out_near, out_far = add_halves(out_mine, out_away)
            out_far = swap_second(out_far)
        else:
            out_near = out_far = sum_f(out_mine)
    grad_queries, grad_kv, by_block = attention_backward(
        at_z.astype(jnp.int32)[None],
        range(KEY_VALUE_HEADS),
        queries,
        keys,
        values,
        grad_mixed,
        log_totals,
        cosine,
        sine,
        bias,
        token,
        n,
    )
    grad_queries, out_far = stage(grad_queries, out_far)

    with scope("kv_grad_z"):
        kv_total = lax.psum_scatter(by_block, "z", scatter_dimension=0, tiled=False)
    with scope("projected_core"):
        away, mine = weight_terms(
            normed_group, [grad_queries, grad_kv.reshape(2 * pair_cols, span)], True
        )
    if grid:
        with scope("out_first"):
            out_near, out_far = add_halves(out_near, out_far)
            out_far = swap_first(out_far)
        away, out_far = stage(away, out_far)
        with scope("projected_core"):
            away = send_core(away)
        away, hidden_far, hidden_near = stage(away, hidden_far, hidden_near)
        with scope("projected_second"):
            near, far = add_halves(mine, away)
            far = swap_second(far)
        out_near = add(out_near[0], out_far[0])
    with scope("result_core"):
        result_far = send_core(product(hidden_far, down_weight).astype(BF))
        result_near = product(hidden_near, down_weight).astype(BF)
    def exchange(owned):
        with scope("gate_up_sum_f"):
            owned = owned[:, : 2 * hidden_units].reshape(ranks, shard_rows, -1)
            return lax.all_to_all(owned, "f", 0, 0, tiled=True)

    if grid:
        result_near, result_far = add_halves(result_near, result_far)
        far, result_far = stage(far, result_far)
        with scope("projected_first"):
            near, far = add_halves(near, far)
            far = swap_first(far)
        with scope("out_z"):
            out_owned = send_z(out_near)
        gate_up_owned = exchange(feed_owned)
        with scope("result_second"):
            result_far = swap_second(result_far)
        far, kv_total, gate_up_owned, result_far, *out_owned = stage(
            far, kv_total, gate_up_owned, result_far, *out_owned
        )
        with scope("result_first"):
            result_near, result_far = add_halves(result_near, result_far)
            result = result_near.astype(F32) + swap_first(result_far).astype(F32)
        near = add(near[0], far[0])
    else:
        near = sum_f(mine)
        gate_up_owned = exchange(feed_owned)
        result = jnp.concatenate([result_near, result_far], axis=0)
        result = lax.psum_scatter(result, "f", scatter_dimension=0, tiled=True)
        with scope("out_z"):
            out_owned = send_z(out_near)
    with scope("projected_z"):
        projected = send_z(near)
    result = (resid + result.astype(F32)).astype(BF)

    down_owned = feed_owned[:, 2 * hidden_units :].reshape(pieces, unit, width // pieces)
    down_owned = down_owned.transpose(1, 0, 2).reshape(unit, width).astype(F32)
    input_grad = input_gradient(
        grad_queries, kv_total.reshape(2 * pair_cols, token_count), gathered, own, grad_resid
    )
    if grid:
        gate_owned, up_owned, gain_two_owned = feed_finish(gate_up_owned, w_gate, w_up, gain_two)
        input_grad, gain_two_owned, down_owned, result, *projected = stage(
            input_grad, gain_two_owned, down_owned, result, *projected
        )
        query_owned, key_owned, value_owned, out_owned, gain_one_owned = attention_finish(
            projected, out_owned, [w_query, key_weight, value_weight], gain_one
        )
    else:
        gate_up_owned = (
            gate_up_owned.astype(F32)
            .reshape(ranks, shard_rows, 2, n, unit)
            .transpose(2, 1, 3, 0, 4)
            .reshape(2, shard_rows, n * ranks * unit)
        )
        gate_owned, up_owned = gate_up_owned[0], gate_up_owned[1]
        gain_two_owned = along(w_gate, gate_owned) + along(w_up, up_owned)
        gate_owned, up_owned = gate_owned * gain_two, up_owned * gain_two
        out_owned, grads = total(out_owned), jnp.split(total(projected), cuts[:2], axis=1)
        weights = (w_query, key_weight, value_weight)
        gain_one_owned = sum(along(weight, grad) for weight, grad in zip(weights, grads))
        query_owned, key_owned, value_owned = (grad * gain_one for grad in grads)
    return (
        result[None],
        input_grad[None],
        gain_one_owned.reshape(-1),
        query_owned,
        key_owned,
        value_owned,
        out_owned,
        gain_two_owned.reshape(-1),
        gate_owned,
        up_owned,
        down_owned,
    )


def solution(mesh):
    n, ranks = mesh.shape["seq"], mesh.shape["fsdp"]
    named = Mesh(mesh.devices, ("z", "f"))
    every = ("z", "f")
    rows, vector, matrix = P("f", "z", None), P(every), P(every, None)
    in_specs = (
        rows,
        vector,
        matrix,
        matrix,
        matrix,
        matrix,
        vector,
        matrix,
        matrix,
        matrix,
        rows,
        P("f", None),
        P("f", None),
    )
    out_specs = (rows, rows, vector) + (matrix,) * 4 + (vector,) + (matrix,) * 3

    def step(*operands):
        return on_device(n, ranks, *operands)

    return jax.shard_map(
        step, mesh=named, in_specs=in_specs, out_specs=out_specs, check_vma=False
    )
```
